128 devices in a mesh: blk: 8 (over y_hi, z), dp: 16 (over x, y_lo, core).
Axes of the slice: x: 4, y: 4 (y_hi: 2, y_lo: 2; y = y_hi * 2 + y_lo), z: 4, core: 2. Of those that a mesh axis runs over, the one named last changes fastest.
Arguments:
- image_embeds: bfloat16 [20480, 1152], P(('blk', 'dp')), may hold values from -6 to 6
- text_embeds: bfloat16 [20480, 1152], P(('blk', 'dp')), may hold values from -6 to 6
- log_scale: float32 [1], replicated, may hold values from 3 to 4.1
- logit_bias: float32 [1], replicated, may hold values from -2 to 0
Outputs:
- image_grad: bfloat16 [20480, 1152], P(('blk', 'dp'))
- text_grad: bfloat16 [20480, 1152], P(('blk', 'dp'))
The draws below stay inside these ranges and needn't reach their ends.
All inputs are finite; a program needn't handle non-finite values.
Results may differ from the reference program's by a relative error of at most 0.011.
Values may be sent and summed in bfloat16 or wider, within the bound.
No kernel may reach another device: no remote copies, remote signals or barrier semaphores. Data moves between devices by JAX's collectives and lax.ppermute only.
A program may use at most 128 MiB of HBM per device.

```python
import jax
import jax.numpy as jnp
from jax import lax

D = 1152
PAIRS = 20480
GROUP = 2560
N_BLK = 8


def shard_levels(stream_key, shape, cuts, low, high):
    gain = 1.0
    for position, shards_of in cuts:
        steps = jax.random.uniform(jax.random.fold_in(jax.random.fold_in(stream_key, 6), position), (shards_of,), jnp.float32, low / len(cuts), high / len(cuts))
        gain = gain * jnp.repeat(jnp.exp(steps), shape[position] // shards_of).reshape((-1,) + (1,) * (len(shape) - 1 - position))
    return gain


def noise(own_key, extent, spread, bound, split=(), kind=jnp.bfloat16):
    loudness = shard_levels(own_key, extent, split, -0.22, 0.18) if split else 1.0
    drawn = jax.random.normal(own_key, extent, jnp.float32) * spread * loudness
    return jnp.minimum(jnp.maximum(drawn, -bound), bound).astype(kind)


def setup_inputs(seed: int = 0) -> dict:
    splits = jax.random.split(jax.random.key(seed), 5)
    image_embeds = noise(splits[0], (PAIRS, D), 1.0, 6.0, ((0, 128),))
    text_embeds = noise(splits[1], (PAIRS, D), 1.0, 6.0, ((0, 128),))
    log_scale = jnp.clip(jax.random.uniform(splits[2], (1,), jnp.float32, 3.0, 4.1), 3.0, 4.1)
    logit_bias = jnp.clip(jax.random.uniform(splits[3], (1,), jnp.float32, -2.0, 0.0), -2.0, 0.0)
    return {"image_embeds": image_embeds, "text_embeds": text_embeds, "log_scale": log_scale, "logit_bias": logit_bias}


norm_eps = 1e-06

def normalize(embeds):
    values = embeds.astype(jnp.float32)
    inverse = lax.rsqrt(lax.optimization_barrier(jnp.sum(values * values, axis=1, keepdims=True)) + norm_eps)
    return (values * inverse, inverse)

def project_back(direction, unit_float, inverse):
    along = lax.optimization_barrier(jnp.sum(unit_float * direction, axis=1, keepdims=True))
    return inverse * (direction - unit_float * along)

def reference(image_embeds, text_embeds, log_scale, logit_bias):
    logit_scale = jnp.exp(log_scale[0])
    bias_value = logit_bias[0]
    image_float, image_inverse = normalize(image_embeds)
    text_float, text_inverse = normalize(text_embeds)
    image_unit = image_float.astype(jnp.bfloat16)
    text_unit = text_float.astype(jnp.bfloat16)
    total_rows = image_embeds.shape[0]
    column_ids = jnp.arange(total_rows, dtype=jnp.int32)
    local_ids = jnp.arange(GROUP, dtype=jnp.int32)

    def one_block(text_total, block_index):
        row_start = (block_index * GROUP).astype(jnp.int32)
        block_rows = lax.dynamic_slice_in_dim(image_unit, row_start, GROUP, 0)
        logits = logit_scale * jnp.dot(block_rows, text_unit.T, preferred_element_type=jnp.float32) + bias_value
        positive = ((row_start + local_ids)[:, None] == column_ids[None, :]).astype(jnp.float32)
        weights = (jax.nn.sigmoid(logits) - positive).astype(jnp.bfloat16)
        image_part = jnp.dot(weights, text_unit, preferred_element_type=jnp.float32)
        text_total = text_total + jnp.dot(weights.T, block_rows, preferred_element_type=jnp.float32)
        return (text_total, image_part)
    start_total = jnp.zeros((total_rows, image_embeds.shape[1]), jnp.float32)
    text_total, image_parts = lax.scan(one_block, start_total, jnp.arange(N_BLK, dtype=jnp.int32))
    image_dir = logit_scale * image_parts.reshape(total_rows, image_embeds.shape[1])
    text_dir = logit_scale * text_total
    image_grad = project_back(image_dir, image_float, image_inverse).astype(jnp.bfloat16)
    text_grad = project_back(text_dir, text_float, text_inverse).astype(jnp.bfloat16)
    return (image_grad, text_grad)
```

```python
import functools

import jax
import jax.numpy as jnp
from jax import lax
from jax.experimental import pallas as pl
from jax.experimental.pallas import tpu as pltpu
from jax.sharding import Mesh, PartitionSpec as P

norm_eps = 1e-06
log2_e = 1.4426950408889634
axes = ("yh", "z", "x", "yl", "core")
extents = (2, 4, 4, 2, 2)
rows = 160
chip_rows = 2 * rows
chunk = 256


def pairs_of(move):
    pairs = []
    for yh in range(2):
        for z in range(4):
            for x in range(4):
                for yl in range(2):
                    for core in range(2):
                        place = (yh, z, x, yl, core)
                        pairs.append((linear(place), linear(move(*place))))
    return pairs


def linear(place):
    index = 0
    for value, extent in zip(place, extents):
        index = index * extent + value
    return index


def ring_move(steps):
    def move(yh, z, x, yl, core):
        if core == 0:
            return (yh, z, (x + steps) % 4, yl, core)
        return (yh, (z + steps) % 4, x, yl, core)

    return pairs_of(move)


def ring(value, steps):
    return lax.ppermute(value, axes, ring_move(steps))


def pair(value):
    def move(yh, z, x, yl, core):
        if core == 0:
            return (yh, z, x, 1 - yl, core)
        return (1 - yh, z, x, yl, core)

    return lax.ppermute(value, axes, pairs_of(move))


def swap(value):
    return lax.ppermute(value, "core", [(0, 1), (1, 0)])


def unit_rows(values):
    inverse = lax.rsqrt(jnp.sum(values * values, axis=1, keepdims=True) + norm_eps)
    return values * inverse, inverse


def pack_kernel(core_ref, image_ref, text_ref, got_ref, unit_ref, raw_ref):
    first_core = core_ref[0] == 0
    image = image_ref[...].astype(jnp.float32)
    text = text_ref[...].astype(jnp.float32)
    got = got_ref[...].astype(jnp.float32)
    low = jnp.where(first_core, image, got)
    high = jnp.where(first_core, got, text)
    for half, values in enumerate((low, high)):
        place = pl.ds(half * rows, rows)
        unit_ref[place, :] = unit_rows(values)[0].astype(jnp.bfloat16)
        raw_ref[place, :] = values.astype(jnp.bfloat16)


def pair_kernel(chips, scale_ref, core_ref, *refs):
    mine_in, other_in = refs[:chips], refs[chips : 2 * chips]
    mine_out, other_out = refs[2 * chips : 3 * chips], refs[3 * chips : 4 * chips]
    mine, other, weights, mine_sum, other_sum, in_sem, out_sem = refs[4 * chips :]
    count = chips * rows
    core = core_ref[0]
    half = pl.program_id(0)
    opposite = jnp.where(core == 0, half, 1 - half)

    def half_rows(which):
        return pl.ds(pl.multiple_of(which * rows, rows), rows)

    def loads(which, group):
        arrays, held, sems = (
            (mine_in, mine, 0) if group == 0 else (other_in, other, 1)
        )
        return [
            pltpu.make_async_copy(
                arrays[chip].at[half_rows(which)],
                held.at[which, pl.ds(chip * rows, rows)],
                in_sem.at[sems, which, chip],
            )
            for chip in range(chips)
        ]

    def stores(which, group):
        arrays, held, sems = (
            (mine_out, mine_sum, 0) if group == 0 else (other_out, other_sum, 1)
        )
        return [
            pltpu.make_async_copy(
                held.at[which, pl.ds(chip * rows, rows)],
                arrays[chip].at[half_rows(which)],
                out_sem.at[sems, which, chip],
            )
            for chip in range(chips)
        ]

    @pl.when(half == 0)
    def _():
        for which, far in ((0, opposite), (1, 1 - opposite)):
            for copy in loads(which, 0):
                copy.start()
            for copy in loads(far, 1):
                copy.start()

    for copy in loads(half, 0):
        copy.wait()
    for copy in loads(opposite, 1):
        copy.wait()

    slope = scale_ref[0]
    shift = scale_ref[1]
    mine_rows = mine[half]
    for begin in range(0, count, chunk):
        place = pl.ds(begin, chunk)
        dots = lax.dot_general(
            mine_rows,
            other[opposite, place, :],
            (((1,), (1,)), ((), ())),
            preferred_element_type=jnp.float32,
        )
        power = jnp.exp2(dots * slope + shift)
        share = pl.reciprocal(1.0 + power, approx=True)
        if begin == 0:
            row = lax.broadcasted_iota(jnp.int32, dots.shape, 0)
            column = lax.broadcasted_iota(jnp.int32, dots.shape, 1)
            matched = (row == column) & (row < rows) & (core == 0)
            share = jnp.where(matched, -power * share, share)
        weights[:, place] = share.astype(jnp.bfloat16)
    for begin in range(0, count, chunk):
        place = pl.ds(begin, chunk)
        other_sum[opposite, place, :] = lax.dot_general(
            weights[:, place],
            mine_rows,
            (((0,), (0,)), ((), ())),
            preferred_element_type=jnp.float32,
        ).astype(jnp.bfloat16)
    for copy in stores(opposite, 1):
        copy.start()
    other_rows = other[opposite]
    for begin in range(0, count, chunk):
        place = pl.ds(begin, chunk)
        mine_sum[half, place, :] = jnp.dot(
            weights[place, :], other_rows, preferred_element_type=jnp.float32
        ).astype(jnp.bfloat16)
    for copy in stores(half, 0):
        copy.start()

    @pl.when(half == 1)
    def _():
        for which in range(2):
            for group in range(2):
                for copy in stores(which, group):
                    copy.wait()


def pair_sums(scale, core, mine, other):
    chips = len(mine)
    width = mine[0].shape[1]
    count = chips * rows
    hbm = pl.BlockSpec(memory_space=pl.ANY)
    smem = pl.BlockSpec(memory_space=pltpu.SMEM)
    sums = pl.pallas_call(
        functools.partial(pair_kernel, chips),
        grid=(2,),
        in_specs=[smem, smem] + [hbm] * (2 * chips),
        out_specs=[hbm] * (2 * chips),
        out_shape=[jax.ShapeDtypeStruct((chip_rows, width), jnp.bfloat16)] * (2 * chips),
        scratch_shapes=[
            pltpu.VMEM((2, count, width), jnp.bfloat16),
            pltpu.VMEM((2, count, width), jnp.bfloat16),
            pltpu.VMEM((count, count), jnp.bfloat16),
            pltpu.VMEM((2, count, width), jnp.bfloat16),
            pltpu.VMEM((2, count, width), jnp.bfloat16),
            pltpu.SemaphoreType.DMA((2, 2, chips)),
            pltpu.SemaphoreType.DMA((2, 2, chips)),
        ],
        compiler_params=pltpu.CompilerParams(vmem_limit_bytes=50 * 2**20),
        cost_estimate=pl.CostEstimate(
            flops=12 * count * count * width,
            bytes_accessed=8 * chips * chip_rows * width,
            transcendentals=4 * count * count,
        ),
    )(scale, core, *mine, *other)
    return sums[:chips], sums[chips:]


def final_kernel(scale_ref, core_ref, raw_ref, *refs):
    parts, (keep_ref, give_ref) = refs[:-2], refs[-2:]
    first_core = core_ref[0] == 0
    grads = []
    for half in range(2):
        place = pl.ds(half * rows, rows)
        unit, inverse = unit_rows(raw_ref[place, :].astype(jnp.float32))
        direction = parts[0][place, :].astype(jnp.float32)
        for part in parts[1:]:
            direction = direction + part[place, :].astype(jnp.float32)
        direction = direction * scale_ref[0]
        along = jnp.sum(unit * direction, axis=1, keepdims=True)
        grads.append(inverse * (direction - unit * along))
    low, high = grads
    keep_ref[...] = jnp.where(first_core, low, high).astype(jnp.bfloat16)
    give_ref[...] = jnp.where(first_core, high, low).astype(jnp.bfloat16)


def small_call(kernel, out_shape, scalars, arrays):
    return pl.pallas_call(
        kernel,
        in_specs=[pl.BlockSpec(memory_space=pltpu.SMEM)] * len(scalars)
        + [pl.BlockSpec(memory_space=pltpu.VMEM)] * len(arrays),
        out_specs=[pl.BlockSpec(memory_space=pltpu.VMEM)] * len(out_shape),
        out_shape=[jax.ShapeDtypeStruct(shape, jnp.bfloat16) for shape in out_shape],
        compiler_params=pltpu.CompilerParams(vmem_limit_bytes=32 * 2**20),
    )(*scalars, *arrays)


def add(*parts):
    total = parts[0].astype(jnp.float32)
    for part in parts[1:]:
        total = total + part.astype(jnp.float32)
    return total.astype(jnp.bfloat16)


def on_device(image_embeds, text_embeds, log_scale, logit_bias):
    width = image_embeds.shape[1]
    core = lax.axis_index("core")
    first_core = core == 0
    cores = core.astype(jnp.int32).reshape(1)
    logit_scale = jnp.exp(log_scale)
    factors = jnp.concatenate([-log2_e * logit_scale, -log2_e * logit_bias])
    got = swap(jnp.where(first_core, text_embeds, image_embeds))
    unit, raw = small_call(
        pack_kernel,
        [(chip_rows, width)] * 2,
        (cores,),
        (image_embeds, text_embeds, got),
    )
    near = [unit, ring(unit, 1), ring(unit, -1), ring(unit, 2)]
    across = pair(unit)
    far = [across, ring(across, 1), ring(across, -1), ring(across, 2)]
    mine = near + far
    other = [swap(value) for value in mine]
    mine_sums, other_sums = pair_sums(factors, cores, mine, other)
    sums = [add(one, swap(two)) for one, two in zip(mine_sums, other_sums)]
    near_sums, far_sums = sums[:4], sums[4:]
    back = (0, -1, 1, 2)
    far_total = add(far_sums[0], *[ring(far_sums[k], back[k]) for k in (1, 2, 3)])
    parts = [near_sums[0]] + [ring(near_sums[k], back[k]) for k in (1, 2, 3)] + [pair(far_total)]
    keep, give = small_call(
        final_kernel, [(rows, width)] * 2, (logit_scale, cores), (raw, *parts)
    )
    given = swap(give)
    image_grad = jnp.where(first_core, keep, given)
    text_grad = jnp.where(first_core, given, keep)
    return (image_grad, text_grad)


def solution(mesh):
    fine = Mesh(mesh.devices.reshape(extents), axes)
    split = P(axes, None)
    return jax.shard_map(
        on_device,
        mesh=fine,
        in_specs=(split, split, P(), P()),
        out_specs=(split, split),
        check_vma=False,
    )
```

```python
import functools

import jax
import jax.numpy as jnp
from jax import lax
from jax.experimental import pallas as pl
from jax.experimental.pallas import tpu as pltpu
from jax.sharding import Mesh, PartitionSpec as P

norm_eps = 1e-06
log2_e = 1.4426950408889634
axes = ("yh", "z", "x", "yl", "core")
extents = (2, 4, 4, 2, 2)
rows = 160
chip_rows = 2 * rows
chunk = 256


def pairs_of(move):
    pairs = []
    for yh in range(2):
        for z in range(4):
            for x in range(4):
                for yl in range(2):
                    for core in range(2):
                        place = (yh, z, x, yl, core)
                        pairs.append((linear(place), linear(move(*place))))
    return pairs


def linear(place):
    index = 0
    for value, extent in zip(place, extents):
        index = index * extent + value
    return index


def ring_move(steps):
    def move(yh, z, x, yl, core):
        if core == 0:
            return (yh, z, (x + steps) % 4, yl, core)
        return (yh, (z + steps) % 4, x, yl, core)

    return pairs_of(move)


def ring(value, steps):
    return lax.ppermute(value, axes, ring_move(steps))


def pair(value):
    def move(yh, z, x, yl, core):
        if core == 0:
            return (yh, z, x, 1 - yl, core)
        return (1 - yh, z, x, 1 - yl, core)

    return lax.ppermute(value, axes, pairs_of(move))


def swap(value):
    return lax.ppermute(value, "core", [(0, 1), (1, 0)])


def unit_rows(values):
    inverse = lax.rsqrt(jnp.sum(values * values, axis=1, keepdims=True) + norm_eps)
    return values * inverse, inverse


def pack_kernel(core_ref, image_ref, text_ref, got_ref, unit_ref, raw_ref):
    first_core = core_ref[0] == 0
    image = image_ref[...].astype(jnp.float32)
    text = text_ref[...].astype(jnp.float32)
    got = got_ref[...].astype(jnp.float32)
    low = jnp.where(first_core, image, got)
    high = jnp.where(first_core, got, text)
    for half, values in enumerate((low, high)):
        place = pl.ds(half * rows, rows)
        unit_ref[place, :] = unit_rows(values)[0].astype(jnp.bfloat16)
        raw_ref[place, :] = values.astype(jnp.bfloat16)


def pair_kernel(chips, scale_ref, core_ref, *refs):
    mine_in, other_in = refs[:chips], refs[chips : 2 * chips]
    mine_out, other_out = refs[2 * chips : 3 * chips], refs[3 * chips : 4 * chips]
    mine, other, weights, mine_sum, other_sum, in_sem, out_sem = refs[4 * chips :]
    count = chips * rows
    core = core_ref[0]
    half = pl.program_id(0)
    opposite = jnp.where(core == 0, half, 1 - half)

    def half_rows(which):
        return pl.ds(pl.multiple_of(which * rows, rows), rows)

    def loads(which, group):
        arrays, held, sems = (
            (mine_in, mine, 0) if group == 0 else (other_in, other, 1)
        )
        return [
            pltpu.make_async_copy(
                arrays[chip].at[half_rows(which)],
                held.at[which, pl.ds(chip * rows, rows)],
                in_sem.at[sems, which, chip],
            )
            for chip in range(chips)
        ]

    def stores(which, group):
        arrays, held, sems = (
            (mine_out, mine_sum, 0) if group == 0 else (other_out, other_sum, 1)
        )
        return [
            pltpu.make_async_copy(
                held.at[which, pl.ds(chip * rows, rows)],
                arrays[chip].at[half_rows(which)],
                out_sem.at[sems, which, chip],
            )
            for chip in range(chips)
        ]

    @pl.when(half == 0)
    def _():
        for which, far in ((0, opposite), (1, 1 - opposite)):
            for copy in loads(which, 0):
                copy.start()
            for copy in loads(far, 1):
                copy.start()

    for copy in loads(half, 0):
        copy.wait()
    for copy in loads(opposite, 1):
        copy.wait()

    slope = scale_ref[0]
    shift = scale_ref[1]
    mine_rows = mine[half]
    for begin in range(0, count, chunk):
        place = pl.ds(begin, chunk)
        dots = lax.dot_general(
            mine_rows,
            other[opposite, place, :],
            (((1,), (1,)), ((), ())),
            preferred_element_type=jnp.float32,
        )
        power = jnp.exp2(dots * slope + shift)
        share = pl.reciprocal(1.0 + power, approx=True)
        if begin == 0:
            row = lax.broadcasted_iota(jnp.int32, dots.shape, 0)
            column = lax.broadcasted_iota(jnp.int32, dots.shape, 1)
            matched = (row == column) & (row < rows) & (core == 0)
            share = jnp.where(matched, -power * share, share)
        weights[:, place] = share.astype(jnp.bfloat16)
    for begin in range(0, count, chunk):
        place = pl.ds(begin, chunk)
        other_sum[opposite, place, :] = lax.dot_general(
            weights[:, place],
            mine_rows,
            (((0,), (0,)), ((), ())),
            preferred_element_type=jnp.float32,
        ).astype(jnp.bfloat16)
    for copy in stores(opposite, 1):
        copy.start()
    other_rows = other[opposite]
    for begin in range(0, count, chunk):
        place = pl.ds(begin, chunk)
        mine_sum[half, place, :] = jnp.dot(
            weights[place, :], other_rows, preferred_element_type=jnp.float32
        ).astype(jnp.bfloat16)
    for copy in stores(half, 0):
        copy.start()

    @pl.when(half == 1)
    def _():
        for which in range(2):
            for group in range(2):
                for copy in stores(which, group):
                    copy.wait()


def pair_sums(scale, core, mine, other):
    chips = len(mine)
    width = mine[0].shape[1]
    count = chips * rows
    hbm = pl.BlockSpec(memory_space=pl.ANY)
    smem = pl.BlockSpec(memory_space=pltpu.SMEM)
    sums = pl.pallas_call(
        functools.partial(pair_kernel, chips),
        grid=(2,),
        in_specs=[smem, smem] + [hbm] * (2 * chips),
        out_specs=[hbm] * (2 * chips),
        out_shape=[jax.ShapeDtypeStruct((chip_rows, width), jnp.bfloat16)] * (2 * chips),
        scratch_shapes=[
            pltpu.VMEM((2, count, width), jnp.bfloat16),
            pltpu.VMEM((2, count, width), jnp.bfloat16),
            pltpu.VMEM((count, count), jnp.bfloat16),
            pltpu.VMEM((2, count, width), jnp.bfloat16),
            pltpu.VMEM((2, count, width), jnp.bfloat16),
            pltpu.SemaphoreType.DMA((2, 2, chips)),
            pltpu.SemaphoreType.DMA((2, 2, chips)),
        ],
        compiler_params=pltpu.CompilerParams(vmem_limit_bytes=50 * 2**20),
        cost_estimate=pl.CostEstimate(
            flops=12 * count * count * width,
            bytes_accessed=8 * chips * chip_rows * width,
            transcendentals=4 * count * count,
        ),
    )(scale, core, *mine, *other)
    return sums[:chips], sums[chips:]


def final_kernel(scale_ref, core_ref, raw_ref, *refs):
    parts, (keep_ref, give_ref) = refs[:-2], refs[-2:]
    first_core = core_ref[0] == 0
    grads = []
    for half in range(2):
        place = pl.ds(half * rows, rows)
        unit, inverse = unit_rows(raw_ref[place, :].astype(jnp.float32))
        direction = parts[0][place, :].astype(jnp.float32)
        for part in parts[1:]:
            direction = direction + part[place, :].astype(jnp.float32)
        direction = direction * scale_ref[0]
        along = jnp.sum(unit * direction, axis=1, keepdims=True)
        grads.append(inverse * (direction - unit * along))
    low, high = grads
    keep_ref[...] = jnp.where(first_core, low, high).astype(jnp.bfloat16)
    give_ref[...] = jnp.where(first_core, high, low).astype(jnp.bfloat16)


def small_call(kernel, out_shape, scalars, arrays):
    return pl.pallas_call(
        kernel,
        in_specs=[pl.BlockSpec(memory_space=pltpu.SMEM)] * len(scalars)
        + [pl.BlockSpec(memory_space=pltpu.VMEM)] * len(arrays),
        out_specs=[pl.BlockSpec(memory_space=pltpu.VMEM)] * len(out_shape),
        out_shape=[jax.ShapeDtypeStruct(shape, jnp.bfloat16) for shape in out_shape],
        compiler_params=pltpu.CompilerParams(vmem_limit_bytes=32 * 2**20),
    )(*scalars, *arrays)


def add(*parts):
    total = parts[0].astype(jnp.float32)
    for part in parts[1:]:
        total = total + part.astype(jnp.float32)
    return total.astype(jnp.bfloat16)


def on_device(image_embeds, text_embeds, log_scale, logit_bias):
    width = image_embeds.shape[1]
    core = lax.axis_index("core")
    first_core = core == 0
    cores = core.astype(jnp.int32).reshape(1)
    logit_scale = jnp.exp(log_scale)
    factors = jnp.concatenate([-log2_e * logit_scale, -log2_e * logit_bias])
    got = swap(jnp.where(first_core, text_embeds, image_embeds))
    unit, raw = small_call(
        pack_kernel,
        [(chip_rows, width)] * 2,
        (cores,),
        (image_embeds, text_embeds, got),
    )
    near = [unit, ring(unit, 1), ring(unit, -1), ring(unit, 2)]
    across = pair(unit)
    far = [across, ring(across, 1), ring(across, -1), pair(near[3])]
    mine = near + far
    other = [swap(value) for value in mine]
    mine_sums, other_sums = pair_sums(factors, cores, mine, other)
    sums = [add(one, swap(two)) for one, two in zip(mine_sums, other_sums)]
    near_sums, far_sums = sums[:4], sums[4:]
    far_total = add(far_sums[0], ring(far_sums[1], -1), ring(far_sums[2], 1))
    distant = add(near_sums[3], pair(far_sums[3]))
    parts = [
        near_sums[0],
        ring(near_sums[1], -1),
        ring(near_sums[2], 1),
        ring(distant, 2),
        pair(far_total),
    ]
    keep, give = small_call(
        final_kernel, [(rows, width)] * 2, (logit_scale, cores), (raw, *parts)
    )
    given = swap(give)
    image_grad = jnp.where(first_core, keep, given)
    text_grad = jnp.where(first_core, given, keep)
    return (image_grad, text_grad)


def solution(mesh):
    fine = Mesh(mesh.devices.reshape(extents), axes)
    split = P(axes, None)
    return jax.shard_map(
        on_device,
        mesh=fine,
        in_specs=(split, split, P(), P()),
        out_specs=(split, split),
        check_vma=False,
    )
```

```python
import functools

import jax
import jax.numpy as jnp
from jax import lax
from jax.experimental import pallas as pl
from jax.experimental.pallas import tpu as pltpu
from jax.sharding import Mesh, PartitionSpec as P

norm_eps = 1e-06
log2_e = 1.4426950408889634
axes = ("yh", "z", "x", "yl", "core")
extents = (2, 4, 4, 2, 2)
rows = 160
chip_rows = 2 * rows
chunk = 256


def pairs_of(move):
    pairs = []
    for yh in range(2):
        for z in range(4):
            for x in range(4):
                for yl in range(2):
                    for core in range(2):
                        place = (yh, z, x, yl, core)
                        pairs.append((linear(place), linear(move(*place))))
    return pairs


def linear(place):
    index = 0
    for value, extent in zip(place, extents):
        index = index * extent + value
    return index


def ring_move(steps):
    def move(yh, z, x, yl, core):
        if core == 0:
            return (yh, z, (x + steps) % 4, yl, core)
        return (yh, (z + steps) % 4, x, yl, core)

    return pairs_of(move)


def ring(value, steps):
    return lax.ppermute(value, axes, ring_move(steps))


def pair(value):
    def move(yh, z, x, yl, core):
        if core == 0:
            return (yh, z, x, 1 - yl, core)
        return (1 - yh, z, x, 1 - yl, core)

    return lax.ppermute(value, axes, pairs_of(move))


def swap(value):
    return lax.ppermute(value, "core", [(0, 1), (1, 0)])


def unit_rows(values):
    inverse = lax.rsqrt(jnp.sum(values * values, axis=1, keepdims=True) + norm_eps)
    return values * inverse, inverse


def pack_kernel(core_ref, image_ref, text_ref, got_ref, unit_ref, raw_ref):
    first_core = core_ref[0] == 0
    image = image_ref[...].astype(jnp.float32)
    text = text_ref[...].astype(jnp.float32)
    got = got_ref[...].astype(jnp.float32)
    low = jnp.where(first_core, image, got)
    high = jnp.where(first_core, got, text)
    for half, values in enumerate((low, high)):
        place = pl.ds(half * rows, rows)
        unit_ref[place, :] = unit_rows(values)[0].astype(jnp.bfloat16)
        raw_ref[place, :] = values.astype(jnp.bfloat16)


def stacked(places, begin):
    return jnp.concatenate(
        [ref[pl.ds(first + begin, rows), :] for ref, first in places], axis=0
    )


def places_of(refs):
    return [
        (ref, first) for ref in refs for first in range(0, ref.shape[0], chip_rows)
    ]


def opposite_rows(core, half):
    return pl.multiple_of(jnp.where(core == 0, half, 1 - half) * rows, rows)


def weights_kernel(pieces, scale_ref, core_ref, *refs):
    mine, other = places_of(refs[: pieces[0]]), places_of(refs[pieces[0] : sum(pieces)])
    weights_ref, far_ref = refs[sum(pieces) :]
    count = len(mine) * rows
    core = core_ref[0]
    slope, shift = scale_ref[0], scale_ref[1]
    for half in range(2):
        opposite = opposite_rows(core, half)
        mine_rows = stacked(mine, half * rows)
        other_rows = stacked(other, opposite)
        for begin in range(0, count, chunk):
            dots = lax.dot_general(
                mine_rows,
                other_rows[begin : begin + chunk],
                (((1,), (1,)), ((), ())),
                preferred_element_type=jnp.float32,
            )
            power = jnp.exp2(dots * slope + shift)
            share = pl.reciprocal(1.0 + power, approx=True)
            if begin == 0:
                row = lax.broadcasted_iota(jnp.int32, dots.shape, 0)
                column = lax.broadcasted_iota(jnp.int32, dots.shape, 1)
                matched = (row == column) & (row < rows) & (core == 0)
                share = jnp.where(matched, -power * share, share)
            weights_ref[half, :, pl.ds(begin, chunk)] = share.astype(jnp.bfloat16)
        other_sums(weights_ref, half, opposite, mine_rows, 4, far_ref)


def other_sums(weights_ref, half, opposite, mine_rows, first, sums_ref):
    for chip in range(0, 4, 2):
        total = lax.dot_general(
            weights_ref[half, :, pl.ds((first + chip) * rows, 2 * rows)],
            mine_rows,
            (((0,), (0,)), ((), ())),
            preferred_element_type=jnp.float32,
        ).astype(jnp.bfloat16)
        for step in range(2):
            place = pl.ds((chip + step) * chip_rows + opposite, rows)
            sums_ref[place, :] = total[step * rows : (step + 1) * rows]


def near_kernel(core_ref, weights_ref, *refs):
    mine, sums_ref = places_of(refs[:-1]), refs[-1]
    for half in range(2):
        mine_rows = stacked(mine, half * rows)
        opposite = opposite_rows(core_ref[0], half)
        other_sums(weights_ref, half, opposite, mine_rows, 0, sums_ref)


def sums_kernel(pieces, first, core_ref, weights_ref, *refs):
    other, sums = places_of(refs[:pieces]), refs[-4:]
    core = core_ref[0]
    for half in range(2):
        other_rows = stacked(other, opposite_rows(core, half))
        for chip in range(0, len(sums), 2):
            total = jnp.dot(
                weights_ref[half, pl.ds((first + chip) * rows, 2 * rows), :],
                other_rows,
                preferred_element_type=jnp.float32,
            ).astype(jnp.bfloat16)
            sums[chip][pl.ds(half * rows, rows), :] = total[:rows]
            sums[chip + 1][pl.ds(half * rows, rows), :] = total[rows:]


def final_kernel(scale_ref, core_ref, raw_ref, *refs):
    parts, (keep_ref, give_ref) = refs[:-2], refs[-2:]
    first_core = core_ref[0] == 0
    grads = []
    for half in range(2):
        place = pl.ds(half * rows, rows)
        unit, inverse = unit_rows(raw_ref[place, :].astype(jnp.float32))
        direction = parts[0][place, :].astype(jnp.float32)
        for part in parts[1:]:
            direction = direction + part[place, :].astype(jnp.float32)
        direction = direction * scale_ref[0]
        along = jnp.sum(unit * direction, axis=1, keepdims=True)
        grads.append(inverse * (direction - unit * along))
    low, high = grads
    keep_ref[...] = jnp.where(first_core, low, high).astype(jnp.bfloat16)
    give_ref[...] = jnp.where(first_core, high, low).astype(jnp.bfloat16)


def call(kernel, out_shape, scalars, arrays, flops=0, after=()):
    used = len(scalars) + len(arrays)

    def body(*refs):
        kernel(*refs[:used], *refs[used + len(after) :])

    return pl.pallas_call(
        body,
        in_specs=[pl.BlockSpec(memory_space=pltpu.SMEM)] * len(scalars)
        + [pl.BlockSpec(memory_space=pltpu.VMEM)] * len(arrays)
        + [pl.BlockSpec(memory_space=pl.ANY)] * len(after),
        out_specs=[pl.BlockSpec(memory_space=pltpu.VMEM)] * len(out_shape),
        out_shape=[jax.ShapeDtypeStruct(shape, jnp.bfloat16) for shape in out_shape],
        compiler_params=pltpu.CompilerParams(vmem_limit_bytes=26 * 2**20),
        cost_estimate=pl.CostEstimate(
            flops=flops, bytes_accessed=2**20, transcendentals=0
        ),
    )(*scalars, *arrays, *after)


def add_kernel(groups, *refs):
    count = len(groups)
    inputs, sums = refs[: -count], refs[-count:]
    for sum_ref, group in zip(sums, groups):
        total = None
        for index, first in group:
            part = inputs[index][pl.ds(first, chip_rows), :].astype(jnp.float32)
            total = part if total is None else total + part
        sum_ref[...] = total.astype(jnp.bfloat16)


def add(groups, after):
    arrays = []
    places = []
    for group in groups:
        place = []
        for part in group:
            array, first = part if isinstance(part, tuple) else (part, 0)
            if not any(array is known for known in arrays):
                arrays.append(array)
            index = [array is known for known in arrays].index(True)
            place.append((index, first))
        places.append(place)
    return call(
        functools.partial(add_kernel, places),
        [(chip_rows, arrays[0].shape[1])] * len(groups),
        (),
        arrays,
        after=after,
    )


def on_device(image_embeds, text_embeds, log_scale, logit_bias):
    width = image_embeds.shape[1]
    core = lax.axis_index("core")
    first_core = core == 0
    cores = core.astype(jnp.int32).reshape(1)
    logit_scale = jnp.exp(log_scale)
    factors = jnp.concatenate([-log2_e * logit_scale, -log2_e * logit_bias])
    got = swap(jnp.where(first_core, text_embeds, image_embeds))
    unit, raw = call(
        pack_kernel,
        [(chip_rows, width)] * 2,
        (cores,),
        (image_embeds, text_embeds, got),
    )
    near = [unit, ring(unit, 1), ring(unit, -1), ring(unit, 2)]
    across = pair(unit)
    far = [across, ring(across, 1), ring(across, -1), pair(near[3])]
    mine = near + far
    other = [
        swap(jnp.concatenate([near[0]], axis=0)),
        swap(jnp.concatenate([near[1], near[2]], axis=0)),
        swap(near[3]),
        swap(far[0]),
        swap(jnp.concatenate([far[1], far[2]], axis=0)),
        swap(far[3]),
    ]
    count = len(mine) * rows
    block = (chip_rows, width)
    quarter = count * count * width
    weights, far_other = call(
        functools.partial(weights_kernel, (len(mine), len(other))),
        [(2, count, count), (4 * chip_rows, width)],
        (factors, cores),
        (*mine, *other),
        6 * quarter,
    )
    far_shared = swap(far_other)
    far_own = call(
        functools.partial(sums_kernel, len(other), 4),
        [block] * 4,
        (cores,),
        (weights, *other),
        2 * quarter,
    )
    far_sums = add(
        [(one, (far_shared, k * chip_rows)) for k, one in enumerate(far_own)], ()
    )
    arrived = [ring(far_sums[1], -1), ring(far_sums[2], 1), pair(far_sums[3])]
    (near_other,) = call(
        near_kernel,
        [(4 * chip_rows, width)],
        (cores,),
        (weights, *mine),
        2 * quarter,
        (far_sums[0],),
    )
    near_shared = swap(near_other)
    near_own = call(
        functools.partial(sums_kernel, len(other), 0),
        [block] * 4,
        (cores,),
        (weights, *other),
        2 * quarter,
        (near_other,),
    )
    near = [(one, (near_shared, k * chip_rows)) for k, one in enumerate(near_own)]
    sums = add(
        [
            (far_sums[0], arrived[0], arrived[1]),
            (*near[3], arrived[2]),
            near[1],
            near[2],
            near[0],
        ],
        (),
    )
    parts = [
        sums[4],
        pair(sums[0]),
        ring(sums[1], 2),
        ring(sums[2], -1),
        ring(sums[3], 1),
    ]
    keep, give = call(
        final_kernel, [(rows, width)] * 2, (logit_scale, cores), (raw, *parts)
    )
    given = swap(give)
    image_grad = jnp.where(first_core, keep, given)
    text_grad = jnp.where(first_core, given, keep)
    return (image_grad, text_grad)


def solution(mesh):
    fine = Mesh(mesh.devices.reshape(extents), axes)
    split = P(axes, None)
    return jax.shard_map(
        on_device,
        mesh=fine,
        in_specs=(split, split, P(), P()),
        out_specs=(split, split),
        check_vma=False,
    )
```

```python
import functools

import jax
import jax.numpy as jnp
from jax import lax
from jax.experimental import pallas as pl
from jax.experimental.pallas import tpu as pltpu
from jax.sharding import Mesh, PartitionSpec as P

norm_eps = 1e-06
log2_e = 1.4426950408889634
axes = ("yh", "z", "x", "yl", "core")
extents = (2, 4, 4, 2, 2)
rows = 160
chip_rows = 2 * rows
chunk = 256


def pairs_of(move):
    pairs = []
    for yh in range(2):
        for z in range(4):
            for x in range(4):
                for yl in range(2):
                    for core in range(2):
                        place = (yh, z, x, yl, core)
                        pairs.append((linear(place), linear(move(*place))))
    return pairs


def linear(place):
    index = 0
    for value, extent in zip(place, extents):
        index = index * extent + value
    return index


def ring_move(steps):
    def move(yh, z, x, yl, core):
        if core == 0:
            return (yh, z, (x + steps) % 4, yl, core)
        return (yh, (z + steps) % 4, x, yl, core)

    return pairs_of(move)


def ring(value, steps):
    return lax.ppermute(value, axes, ring_move(steps))


def pair(value):
    def move(yh, z, x, yl, core):
        if core == 0:
            return (yh, z, x, 1 - yl, core)
        return (1 - yh, z, x, 1 - yl, core)

    return lax.ppermute(value, axes, pairs_of(move))


def swap(value):
    return lax.ppermute(value, "core", [(0, 1), (1, 0)])


def unit_rows(values):
    inverse = lax.rsqrt(jnp.sum(values * values, axis=1, keepdims=True) + norm_eps)
    return values * inverse, inverse


def pack_kernel(core_ref, keep_ref, got_ref, unit_ref, raw_ref):
    first_core = core_ref[0] == 0
    keep = keep_ref[...].astype(jnp.float32)
    got = got_ref[...].astype(jnp.float32)
    low = jnp.where(first_core, keep, got)
    high = jnp.where(first_core, got, keep)
    for half, values in enumerate((low, high)):
        place = pl.ds(half * rows, rows)
        unit_ref[place, :] = unit_rows(values)[0].astype(jnp.bfloat16)
        raw_ref[place, :] = values.astype(jnp.bfloat16)


def stacked(places, begin):
    return jnp.concatenate(
        [ref[pl.ds(first + begin, rows), :] for ref, first in places], axis=0
    )


def places_of(refs):
    return [
        (ref, first) for ref in refs for first in range(0, ref.shape[0], chip_rows)
    ]


def opposite_rows(core, half):
    return pl.multiple_of(jnp.where(core == 0, half, 1 - half) * rows, rows)


def weights_kernel(pieces, scale_ref, core_ref, *refs):
    mine, other = places_of(refs[: pieces[0]]), places_of(refs[pieces[0] : sum(pieces)])
    weights_ref, far_ref = refs[sum(pieces) :]
    count = len(mine) * rows
    core = core_ref[0]
    slope, shift = scale_ref[0], scale_ref[1]
    for half in range(2):
        opposite = opposite_rows(core, half)
        mine_rows = stacked(mine, half * rows)
        other_rows = stacked(other, opposite)
        for begin in range(0, count, chunk):
            dots = lax.dot_general(
                mine_rows,
                other_rows[begin : begin + chunk],
                (((1,), (1,)), ((), ())),
                preferred_element_type=jnp.float32,
            )
            power = jnp.exp2(dots * slope + shift)
            share = pl.reciprocal(1.0 + power, approx=True)
            if begin == 0:
                row = lax.broadcasted_iota(jnp.int32, dots.shape, 0)
                column = lax.broadcasted_iota(jnp.int32, dots.shape, 1)
                matched = (row == column) & (row < rows) & (core == 0)
                share = jnp.where(matched, -power * share, share)
            weights_ref[half, :, pl.ds(begin, chunk)] = share.astype(jnp.bfloat16)
        other_sums(weights_ref, half, opposite, mine_rows, 4, far_ref)


def other_sums(weights_ref, half, opposite, mine_rows, first, sums_ref):
    for chip in range(0, 4, 2):
        total = lax.dot_general(
            weights_ref[half, :, pl.ds((first + chip) * rows, 2 * rows)],
            mine_rows,
            (((0,), (0,)), ((), ())),
            preferred_element_type=jnp.float32,
        ).astype(jnp.bfloat16)
        for step in range(2):
            place = pl.ds((chip + step) * chip_rows + opposite, rows)
            sums_ref[place, :] = total[step * rows : (step + 1) * rows]


def near_kernel(core_ref, weights_ref, *refs):
    mine, sums_ref = places_of(refs[:-1]), refs[-1]
    for half in range(2):
        mine_rows = stacked(mine, half * rows)
        opposite = opposite_rows(core_ref[0], half)
        other_sums(weights_ref, half, opposite, mine_rows, 0, sums_ref)


def sums_kernel(pieces, first, core_ref, weights_ref, *refs):
    other, sums = places_of(refs[:pieces]), refs[-4:]
    core = core_ref[0]
    for half in range(2):
        other_rows = stacked(other, opposite_rows(core, half))
        for chip in range(0, len(sums), 2):
            total = jnp.dot(
                weights_ref[half, pl.ds((first + chip) * rows, 2 * rows), :],
                other_rows,
                preferred_element_type=jnp.float32,
            ).astype(jnp.bfloat16)
            sums[chip][pl.ds(half * rows, rows), :] = total[:rows]
            sums[chip + 1][pl.ds(half * rows, rows), :] = total[rows:]


def final_kernel(scale_ref, core_ref, raw_ref, *refs):
    parts, (keep_ref, give_ref) = refs[:-2], refs[-2:]
    first_core = core_ref[0] == 0
    grads = []
    for half in range(2):
        place = pl.ds(half * rows, rows)
        unit, inverse = unit_rows(raw_ref[place, :].astype(jnp.float32))
        direction = parts[0][place, :].astype(jnp.float32)
        for part in parts[1:]:
            direction = direction + part[place, :].astype(jnp.float32)
        direction = direction * scale_ref[0]
        along = jnp.sum(unit * direction, axis=1, keepdims=True)
        grads.append(inverse * (direction - unit * along))
    low, high = grads
    keep_ref[...] = jnp.where(first_core, low, high).astype(jnp.bfloat16)
    give_ref[...] = jnp.where(first_core, high, low).astype(jnp.bfloat16)


def call(kernel, out_shape, scalars, arrays, flops=0, after=()):
    used = len(scalars) + len(arrays)

    def body(*refs):
        kernel(*refs[:used], *refs[used + len(after) :])

    return pl.pallas_call(
        body,
        in_specs=[pl.BlockSpec(memory_space=pltpu.SMEM)] * len(scalars)
        + [pl.BlockSpec(memory_space=pltpu.VMEM)] * len(arrays)
        + [pl.BlockSpec(memory_space=pl.ANY)] * len(after),
        out_specs=[pl.BlockSpec(memory_space=pltpu.VMEM)] * len(out_shape),
        out_shape=[jax.ShapeDtypeStruct(shape, jnp.bfloat16) for shape in out_shape],
        compiler_params=pltpu.CompilerParams(vmem_limit_bytes=26 * 2**20),
        cost_estimate=pl.CostEstimate(
            flops=flops, bytes_accessed=2**20, transcendentals=0
        ),
    )(*scalars, *arrays, *after)


def add_kernel(groups, *refs):
    count = len(groups)
    inputs, sums = refs[: -count], refs[-count:]
    for sum_ref, group in zip(sums, groups):
        total = None
        for index, first in group:
            part = inputs[index][pl.ds(first, chip_rows), :].astype(jnp.float32)
            total = part if total is None else total + part
        sum_ref[...] = total.astype(jnp.bfloat16)


def add(groups, after, flops=0):
    arrays = []
    places = []
    for group in groups:
        place = []
        for part in group:
            array, first = part if isinstance(part, tuple) else (part, 0)
            if not any(array is known for known in arrays):
                arrays.append(array)
            index = [array is known for known in arrays].index(True)
            place.append((index, first))
        places.append(place)
    return call(
        functools.partial(add_kernel, places),
        [(chip_rows, arrays[0].shape[1])] * len(groups),
        (),
        arrays,
        flops,
        after,
    )


def on_device(image_embeds, text_embeds, log_scale, logit_bias):
    width = image_embeds.shape[1]
    core = lax.axis_index("core")
    first_core = core == 0
    cores = core.astype(jnp.int32).reshape(1)
    logit_scale = jnp.exp(log_scale)
    factors = jnp.concatenate([-log2_e * logit_scale, -log2_e * logit_bias])
    give = jnp.where(first_core, text_embeds, image_embeds)
    keep = jnp.where(first_core, image_embeds, text_embeds)
    got = swap(give)
    unit, raw = call(
        pack_kernel,
        [(chip_rows, width)] * 2,
        (cores,),
        (keep, got),
    )
    left, right, across = ring(unit, 1), ring(unit, -1), pair(unit)
    distant = jnp.concatenate([ring(left[:rows], 1), ring(right[rows:], -1)], axis=0)
    near = [unit, left, right, distant]
    far = [across, ring(across, 1), ring(across, -1), pair(distant)]
    mine = near + far
    other = [
        swap(unit),
        swap(jnp.concatenate([left, right], axis=0)),
        swap(distant),
        swap(across),
        swap(jnp.concatenate([far[1], far[2]], axis=0)),
        swap(far[3]),
    ]
    count = len(mine) * rows
    block = (chip_rows, width)
    quarter = count * count * width
    weights, far_other = call(
        functools.partial(weights_kernel, (len(mine), len(other))),
        [(2, count, count), (4 * chip_rows, width)],
        (factors, cores),
        (*mine, *other),
        6 * quarter,
    )
    far_shared = swap(far_other)
    far_own = call(
        functools.partial(sums_kernel, len(other), 4),
        [block] * 4,
        (cores,),
        (weights, *other),
        2 * quarter,
    )
    far_sums = add(
        [(one, (far_shared, k * chip_rows)) for k, one in enumerate(far_own)], ()
    )
    arrived = [ring(far_sums[1], -1), ring(far_sums[2], 1), pair(far_sums[3])]
    (near_other,) = call(
        near_kernel,
        [(4 * chip_rows, width)],
        (cores,),
        (weights, *mine),
        2 * quarter,
        (far_sums[0],),
    )
    near_shared = swap(near_other)
    near_own = call(
        functools.partial(sums_kernel, len(other), 0),
        [block] * 4,
        (cores,),
        (weights, *other),
        2 * quarter,
        (near_other,),
    )
    near_sums = add(
        [(one, (near_shared, k * chip_rows)) for k, one in enumerate(near_own)], ()
    )
    far_total, distant_total = add(
        [(far_sums[0], arrived[0], arrived[1]), (near_sums[3], arrived[2])],
        (near_sums[0],),
    )
    late = [ring(distant_total, 2), pair(far_total)]
    (near_total,) = add(
        [(near_sums[0], ring(near_sums[1], -1), ring(near_sums[2], 1))],
        (),
        16 * quarter,
    )
    parts = [near_total, *late]
    keep, give = call(
        final_kernel, [(rows, width)] * 2, (logit_scale, cores), (raw, *parts)
    )
    given = swap(give)
    image_grad = jnp.where(first_core, keep, given)
    text_grad = jnp.where(first_core, given, keep)
    return (image_grad, text_grad)


def solution(mesh):
    fine = Mesh(mesh.devices.reshape(extents), axes)
    split = P(axes, None)
    return jax.shard_map(
        on_device,
        mesh=fine,
        in_specs=(split, split, P(), P()),
        out_specs=(split, split),
        check_vma=False,
    )
```

```python
import functools

import jax
import jax.numpy as jnp
from jax import lax
from jax.experimental import pallas as pl
from jax.experimental.pallas import tpu as pltpu
from jax.sharding import Mesh, PartitionSpec as P

norm_eps = 1e-06
log2_e = 1.4426950408889634
axes = ("yh", "z", "x", "yl", "core")
extents = (2, 4, 4, 2, 2)
rows = 160
chip_rows = 2 * rows
chunk = 256


def pairs_of(move):
    pairs = []
    for yh in range(2):
        for z in range(4):
            for x in range(4):
                for yl in range(2):
                    for core in range(2):
                        place = (yh, z, x, yl, core)
                        pairs.append((linear(place), linear(move(*place))))
    return pairs


def linear(place):
    index = 0
    for value, extent in zip(place, extents):
        index = index * extent + value
    return index


def ring_move(steps):
    def move(yh, z, x, yl, core):
        if core == 0:
            return (yh, z, (x + steps) % 4, yl, core)
        return (yh, (z + steps) % 4, x, yl, core)

    return pairs_of(move)


def ring(value, steps):
    return lax.ppermute(value, axes, ring_move(steps))


def pair(value):
    def move(yh, z, x, yl, core):
        if core == 0:
            return (yh, z, x, 1 - yl, core)
        return (1 - yh, z, x, 1 - yl, core)

    return lax.ppermute(value, axes, pairs_of(move))


def swap(value):
    return lax.ppermute(value, "core", [(0, 1), (1, 0)])


def unit_rows(values):
    inverse = lax.rsqrt(jnp.sum(values * values, axis=1, keepdims=True) + norm_eps)
    return values * inverse, inverse


def pack_kernel(core_ref, keep_ref, got_ref, unit_ref, raw_ref):
    first_core = core_ref[0] == 0
    keep = keep_ref[...].astype(jnp.float32)
    got = got_ref[...].astype(jnp.float32)
    low = jnp.where(first_core, keep, got)
    high = jnp.where(first_core, got, keep)
    for half, values in enumerate((low, high)):
        place = pl.ds(half * rows, rows)
        unit_ref[place, :] = unit_rows(values)[0].astype(jnp.bfloat16)
        raw_ref[place, :] = values.astype(jnp.bfloat16)


def stacked(places, begin):
    return jnp.concatenate(
        [ref[pl.ds(first + begin, rows), :] for ref, first in places], axis=0
    )


def places_of(refs):
    return [
        (ref, first) for ref in refs for first in range(0, ref.shape[0], chip_rows)
    ]


def opposite_rows(core, half):
    return pl.multiple_of(jnp.where(core == 0, half, 1 - half) * rows, rows)


def spans(count):
    return [(begin, min(chunk, count - begin)) for begin in range(0, count, chunk)]


def weights_of(scale_ref, mine_rows, other_rows, matched=None):
    dots = lax.dot_general(
        mine_rows,
        other_rows,
        (((1,), (1,)), ((), ())),
        preferred_element_type=jnp.float32,
    )
    power = jnp.exp2(dots * scale_ref[0] + scale_ref[1])
    share = pl.reciprocal(1.0 + power, approx=True)
    if matched is not None:
        row = lax.broadcasted_iota(jnp.int32, dots.shape, 0)
        column = lax.broadcasted_iota(jnp.int32, dots.shape, 1)
        share = jnp.where((row == column) & (row < rows) & matched, -power * share, share)
    return share.astype(jnp.bfloat16)


def transposed_dot(weights, values):
    return lax.dot_general(
        weights, values, (((0,), (0,)), ((), ())), preferred_element_type=jnp.float32
    )


def early_kernel(half, pieces, scale_ref, core_ref, *refs):
    mine, other = places_of(refs[: pieces[0]]), places_of(refs[pieces[0] : sum(pieces)])
    mine_sum, other_sum, weights_ref = refs[sum(pieces) :]
    core = core_ref[0]
    mine_rows = stacked(mine, half * rows)
    other_rows = stacked(other, opposite_rows(core, half))
    count = len(mine) * rows
    for begin, size in spans(count):
        weights_ref[:, pl.ds(begin, size)] = weights_of(
            scale_ref,
            mine_rows,
            other_rows[begin : begin + size],
            core == 0 if begin == 0 else None,
        )
    for begin, size in spans(count):
        other_sum[pl.ds(begin, size), :] = transposed_dot(
            weights_ref[:, pl.ds(begin, size)], mine_rows
        )
    mine_sum[...] = jnp.dot(
        weights_ref[...], other_rows, preferred_element_type=jnp.float32
    )


def main_kernel(pieces, scale_ref, core_ref, *refs):
    mine, other = places_of(refs[: pieces[0]]), places_of(refs[pieces[0] : sum(pieces)])
    upper_ref, lower_ref, far_ref = refs[sum(pieces) :]
    core = core_ref[0]
    near = 4 * rows
    for half in range(2):
        opposite = opposite_rows(core, half)
        mine_rows = stacked(mine, half * rows)
        other_rows = stacked(other, opposite)
        for begin, size in spans(near):
            upper_ref[half, :, pl.ds(begin, size)] = weights_of(
                scale_ref,
                mine_rows[:near],
                other_rows[near + begin : near + begin + size],
            )
        for begin, size in spans(2 * near):
            lower_ref[half, :, pl.ds(begin, size)] = weights_of(
                scale_ref, mine_rows[near:], other_rows[begin : begin + size]
            )
        for chip in range(0, 4, 2):
            place = pl.ds(chip * rows, 2 * rows)
            right = pl.ds(near + chip * rows, 2 * rows)
            weights = jnp.concatenate(
                [upper_ref[half, :, place], lower_ref[half, :, right]], axis=0
            )
            total = transposed_dot(weights, mine_rows).astype(jnp.bfloat16)
            for step in range(2):
                far_ref[pl.ds((chip + step) * chip_rows + opposite, rows), :] = total[
                    step * rows : (step + 1) * rows
                ]


def far_kernel(pieces, core_ref, lower_ref, *refs):
    other, sums = places_of(refs[:pieces]), refs[-4:]
    for half in range(2):
        other_rows = stacked(other, opposite_rows(core_ref[0], half))
        for chip in range(0, 4, 2):
            total = jnp.dot(
                lower_ref[half, pl.ds(chip * rows, 2 * rows), :],
                other_rows,
                preferred_element_type=jnp.float32,
            ).astype(jnp.bfloat16)
            for step in range(2):
                sums[chip + step][pl.ds(half * rows, rows), :] = total[
                    step * rows : (step + 1) * rows
                ]


def near_other_kernel(core_ref, lower_ref, *refs):
    mine, parts, sums_ref = places_of(refs[:4]), refs[4:6], refs[-1]
    for half in range(2):
        mine_rows = stacked(mine, half * rows)
        opposite = opposite_rows(core_ref[0], half)
        for chip in range(0, 4, 2):
            place = pl.ds(chip * rows, 2 * rows)
            total = transposed_dot(lower_ref[half, :, place], mine_rows)
            total = (total + parts[half][place, :]).astype(jnp.bfloat16)
            for step in range(2):
                sums_ref[pl.ds((chip + step) * chip_rows + opposite, rows), :] = total[
                    step * rows : (step + 1) * rows
                ]


def near_own_kernel(pieces, core_ref, upper_ref, *refs):
    other, parts, sums = places_of(refs[:pieces]), refs[pieces : pieces + 2], refs[-4:]
    for half in range(2):
        other_rows = stacked(other, opposite_rows(core_ref[0], half))
        for chip in range(0, 4, 2):
            place = pl.ds(chip * rows, 2 * rows)
            total = jnp.dot(
                upper_ref[half, place, :], other_rows, preferred_element_type=jnp.float32
            )
            total = (total + parts[half][place, :]).astype(jnp.bfloat16)
            for step in range(2):
                sums[chip + step][pl.ds(half * rows, rows), :] = total[
                    step * rows : (step + 1) * rows
                ]


def joined_kernel(*refs):
    first = 0
    for ref in refs[:-1]:
        refs[-1][pl.ds(first, ref.shape[0]), :] = ref[...]
        first += ref.shape[0]


def joined(arrays, after=()):
    shape = (sum(array.shape[0] for array in arrays), arrays[0].shape[1])
    return call(joined_kernel, [shape], (), arrays, after=after)[0]


def final_kernel(scale_ref, core_ref, raw_ref, *refs):
    parts, (keep_ref, give_ref) = refs[:-2], refs[-2:]
    first_core = core_ref[0] == 0
    grads = []
    for half in range(2):
        place = pl.ds(half * rows, rows)
        unit, inverse = unit_rows(raw_ref[place, :].astype(jnp.float32))
        direction = parts[0][place, :].astype(jnp.float32)
        for part in parts[1:]:
            direction = direction + part[place, :].astype(jnp.float32)
        direction = direction * scale_ref[0]
        along = jnp.sum(unit * direction, axis=1, keepdims=True)
        grads.append(inverse * (direction - unit * along))
    low, high = grads
    keep_ref[...] = jnp.where(first_core, low, high).astype(jnp.bfloat16)
    give_ref[...] = jnp.where(first_core, high, low).astype(jnp.bfloat16)


def call(kernel, out_shape, scalars, arrays, flops=0, after=(), scratch=(), kind=jnp.bfloat16):
    used = len(scalars) + len(arrays)

    def body(*refs):
        kernel(*refs[:used], *refs[used + len(after) :])

    return pl.pallas_call(
        body,
        in_specs=[pl.BlockSpec(memory_space=pltpu.SMEM)] * len(scalars)
        + [pl.BlockSpec(memory_space=pltpu.VMEM)] * len(arrays)
        + [pl.BlockSpec(memory_space=pl.ANY)] * len(after),
        out_specs=[pl.BlockSpec(memory_space=pltpu.VMEM)] * len(out_shape),
        out_shape=[jax.ShapeDtypeStruct(shape, kind) for shape in out_shape],
        scratch_shapes=list(scratch),
        compiler_params=pltpu.CompilerParams(vmem_limit_bytes=8 * 2**20),
        cost_estimate=pl.CostEstimate(
            flops=flops, bytes_accessed=2**20, transcendentals=0
        ),
    )(*scalars, *arrays, *after)


def add_kernel(groups, *refs):
    count = len(groups)
    inputs, sums = refs[: -count], refs[-count:]
    for sum_ref, group in zip(sums, groups):
        total = None
        for index, first in group:
            part = inputs[index][pl.ds(first, chip_rows), :].astype(jnp.float32)
            total = part if total is None else total + part
        sum_ref[...] = total.astype(sum_ref.dtype)


def add(groups, after=(), flops=0, kind=jnp.bfloat16):
    arrays = []
    places = []
    for group in groups:
        place = []
        for part in group:
            array, first = part if isinstance(part, tuple) else (part, 0)
            if not any(array is known for known in arrays):
                arrays.append(array)
            index = [array is known for known in arrays].index(True)
            place.append((index, first))
        places.append(place)
    return call(
        functools.partial(add_kernel, places),
        [(chip_rows, arrays[0].shape[1])] * len(groups),
        (),
        arrays,
        flops,
        after,
        kind=kind,
    )


def call_main(factors, cores, mine, other, after, quarter):
    near, width = 4 * rows, mine[0].shape[1]
    return call(
        functools.partial(main_kernel, (len(mine), len(other))),
        [(2, near, near), (2, near, 2 * near), (4 * chip_rows, width)],
        (factors, cores),
        (*mine, *other),
        5 * quarter,
        (after,),
    )


def on_device(image_embeds, text_embeds, log_scale, logit_bias):
    width = image_embeds.shape[1]
    core = lax.axis_index("core")
    first_core = core == 0
    cores = core.astype(jnp.int32).reshape(1)
    logit_scale = jnp.exp(log_scale)
    factors = jnp.concatenate([-log2_e * logit_scale, -log2_e * logit_bias])
    give = jnp.where(first_core, text_embeds, image_embeds)
    keep = jnp.where(first_core, image_embeds, text_embeds)
    got = swap(give)
    unit, raw = call(
        pack_kernel,
        [(chip_rows, width)] * 2,
        (cores,),
        (keep, got),
    )
    left, right, across = ring(unit, 1), ring(unit, -1), pair(unit)
    near = [unit, left, right, across]
    near_other = [swap(joined(near))]
    halves = [ring(left[:rows], 1), ring(right[rows:], -1)]
    far_left, far_right = ring(across, 1), ring(across, -1)
    block = (chip_rows, width)
    near_block = (4 * rows, width)
    quarter = 64 * rows * rows * width

    def early(half, after):
        return call(
            functools.partial(early_kernel, half, (len(near), len(near_other))),
            [near_block] * 2,
            (factors, cores),
            (*near, *near_other),
            3 * quarter // 2,
            after,
            [pltpu.VMEM((4 * rows, 4 * rows), jnp.bfloat16)],
            jnp.float32,
        )

    distant = joined(halves)
    far_distant = pair(distant)
    early_low = early(0, (distant,))
    early_high = early(1, early_low[:1])
    own_parts, other_parts = zip(early_low, early_high)
    far = [distant, far_left, far_right, far_distant]
    far_other = [
        swap(distant),
        swap(joined(far[1:3], early_high[:1])),
        swap(far_distant),
    ]
    mine, other = near + far, near_other + far_other
    upper, lower, far_back = call_main(factors, cores, mine, other, early_high[0], quarter)
    far_shared = swap(far_back)
    far_own = call(
        functools.partial(far_kernel, len(other)),
        [block] * 4,
        (cores,),
        (lower, *other),
        2 * quarter,
    )
    far_sums = add(
        [(one, (far_shared, k * chip_rows)) for k, one in enumerate(far_own)]
    )
    arrived = [ring(far_sums[1], -1), ring(far_sums[2], 1), pair(far_sums[3])]
    (near_back,) = call(
        near_other_kernel,
        [(4 * chip_rows, width)],
        (cores,),
        (lower, *far, *other_parts),
        quarter,
        (far_sums[0],),
    )
    near_shared = swap(near_back)
    near_own = call(
        functools.partial(near_own_kernel, len(far_other)),
        [block] * 4,
        (cores,),
        (upper, *far_other, *own_parts),
        quarter,
        (near_back,),
    )
    near_sums = add(
        [(one, (near_shared, k * chip_rows)) for k, one in enumerate(near_own)]
    )
    across_total, distant_total = add(
        [(near_sums[3], arrived[0], arrived[1]), (far_sums[0], arrived[2])],
        (near_sums[0],),
    )
    late = [ring(distant_total, 2), pair(across_total)]
    (near_total,) = add(
        [(near_sums[0], ring(near_sums[1], -1), ring(near_sums[2], 1))],
        (),
        16 * quarter,
        jnp.float32,
    )
    parts = [near_total, *late]
    keep, give = call(
        final_kernel, [(rows, width)] * 2, (logit_scale, cores), (raw, *parts)
    )
    given = swap(give)
    image_grad = jnp.where(first_core, keep, given)
    text_grad = jnp.where(first_core, given, keep)
    return (image_grad, text_grad)


def solution(mesh):
    fine = Mesh(mesh.devices.reshape(extents), axes)
    split = P(axes, None)
    return jax.shard_map(
        on_device,
        mesh=fine,
        in_specs=(split, split, P(), P()),
        out_specs=(split, split),
        check_vma=False,
    )
```

```python
import functools

import jax
import jax.numpy as jnp
from jax import lax
from jax.experimental import pallas as pl
from jax.experimental.pallas import tpu as pltpu
from jax.sharding import Mesh, PartitionSpec as P

norm_eps = 1e-06
log2_e = 1.4426950408889634
axes = ("yh", "z", "x", "yl", "core")
extents = (2, 4, 4, 2, 2)
rows = 160
chip_rows = 2 * rows
chunk = 256


def pairs_of(move):
    pairs = []
    for yh in range(2):
        for z in range(4):
            for x in range(4):
                for yl in range(2):
                    for core in range(2):
                        place = (yh, z, x, yl, core)
                        pairs.append((linear(place), linear(move(*place))))
    return pairs


def linear(place):
    index = 0
    for value, extent in zip(place, extents):
        index = index * extent + value
    return index


def ring_move(steps):
    def move(yh, z, x, yl, core):
        if core == 0:
            return (yh, z, (x + steps) % 4, yl, core)
        return (yh, (z + steps) % 4, x, yl, core)

    return pairs_of(move)


def ring(value, steps):
    return lax.ppermute(value, axes, ring_move(steps))


def pair(value):
    def move(yh, z, x, yl, core):
        if core == 0:
            return (yh, z, x, 1 - yl, core)
        return (1 - yh, z, x, 1 - yl, core)

    return lax.ppermute(value, axes, pairs_of(move))


def swap(value):
    return lax.ppermute(value, "core", [(0, 1), (1, 0)])


def unit_rows(values):
    inverse = lax.rsqrt(jnp.sum(values * values, axis=1, keepdims=True) + norm_eps)
    return values * inverse, inverse


def pack_kernel(core_ref, keep_ref, got_ref, unit_ref, raw_ref):
    first_core = core_ref[0] == 0
    keep = keep_ref[...].astype(jnp.float32)
    got = got_ref[...].astype(jnp.float32)
    low = jnp.where(first_core, keep, got)
    high = jnp.where(first_core, got, keep)
    for half, values in enumerate((low, high)):
        place = pl.ds(half * rows, rows)
        unit_ref[place, :] = unit_rows(values)[0].astype(jnp.bfloat16)
        raw_ref[place, :] = values.astype(jnp.bfloat16)


def stacked(places, begin):
    return jnp.concatenate(
        [ref[pl.ds(first + begin, rows), :] for ref, first in places], axis=0
    )


def places_of(refs):
    return [
        (ref, first) for ref in refs for first in range(0, ref.shape[0], chip_rows)
    ]


def opposite_rows(core, half):
    return pl.multiple_of(jnp.where(core == 0, half, 1 - half) * rows, rows)


def spans(count):
    return [(begin, min(chunk, count - begin)) for begin in range(0, count, chunk)]


def weights_of(scale_ref, mine_rows, other_rows, matched=None):
    dots = lax.dot_general(
        mine_rows,
        other_rows,
        (((1,), (1,)), ((), ())),
        preferred_element_type=jnp.float32,
    )
    power = jnp.exp2(dots * scale_ref[0] + scale_ref[1])
    share = pl.reciprocal(1.0 + power, approx=True)
    if matched is not None:
        row = lax.broadcasted_iota(jnp.int32, dots.shape, 0)
        column = lax.broadcasted_iota(jnp.int32, dots.shape, 1)
        share = jnp.where((row == column) & (row < rows) & matched, -power * share, share)
    return share.astype(jnp.bfloat16)


def transposed_dot(weights, values):
    return lax.dot_general(
        weights, values, (((0,), (0,)), ((), ())), preferred_element_type=jnp.float32
    )


def early_kernel(half, pieces, scale_ref, core_ref, *refs):
    mine = places_of(refs[: pieces[0]])
    other = places_of(refs[pieces[0] : sum(pieces)])[: len(mine)]
    mine_sum, other_sum, weights_ref = refs[sum(pieces) :]
    core = core_ref[0]
    mine_rows = stacked(mine, half * rows)
    other_rows = stacked(other, opposite_rows(core, half))
    count = len(mine) * rows
    for begin, size in spans(count):
        weights_ref[:, pl.ds(begin, size)] = weights_of(
            scale_ref,
            mine_rows,
            other_rows[begin : begin + size],
            core == 0 if begin == 0 else None,
        )
    for begin, size in spans(count):
        other_sum[pl.ds(begin, size), :] = transposed_dot(
            weights_ref[:, pl.ds(begin, size)], mine_rows
        )
    mine_sum[...] = jnp.dot(
        weights_ref[...], other_rows, preferred_element_type=jnp.float32
    )


def store_chips(refs, first, begin, total):
    done = 0
    while done < total.shape[0]:
        chip, offset = divmod(begin + done, rows)
        size = min(rows - offset, total.shape[0] - done)
        ref, base = refs[chip]
        ref[pl.ds(base + first + offset, size), :] = total[done : done + size].astype(
            ref.dtype
        )
        done += size


def side_kernel(scale_ref, core_ref, *refs):
    mine, other = places_of(refs[:5]), places_of(refs[5:6])
    row_ref, column_ref = refs[6:]
    for half in range(2):
        mine_rows = stacked(mine, half * rows)
        other_rows = stacked(other, opposite_rows(core_ref[0], half))
        for begin, size in spans(4 * rows) + [(4 * rows, rows)]:
            place = pl.ds(begin, size)
            row_ref[half, :, place] = weights_of(
                scale_ref, mine_rows[4 * rows :], other_rows[begin : begin + size]
            )
            column_ref[half, :, place] = weights_of(
                scale_ref, other_rows[4 * rows :], mine_rows[begin : begin + size]
            )


def far_kernel(own, pieces, scale_ref, core_ref, *refs):
    mine, other = places_of(refs[: pieces[0]]), places_of(refs[pieces[0] : sum(pieces)])
    weights_ref, sums = refs[sum(pieces)], places_of(refs[sum(pieces) + 1 :])
    for half in range(2):
        opposite = opposite_rows(core_ref[0], half)
        mine_rows = stacked(mine, half * rows)
        other_rows = stacked(other, opposite)
        if own:
            far_rows, all_rows, first = mine_rows[5 * rows :], other_rows, half * rows
        else:
            far_rows, all_rows, first = other_rows[5 * rows :], mine_rows, opposite
        for begin, size in spans(8 * rows):
            weights_ref[half, :, pl.ds(begin, size)] = weights_of(
                scale_ref, far_rows, all_rows[begin : begin + size]
            )
        total = jnp.dot(
            weights_ref[half], all_rows, preferred_element_type=jnp.float32
        )
        store_chips(sums, first, 0, total)


def near_kernel(own, pieces, core_ref, far_ref, side_ref, line_ref, *refs):
    count = sum(pieces)
    mine, other = places_of(refs[: pieces[0]]), places_of(refs[pieces[0] : count])
    parts, sums = refs[count : count + 2], places_of(refs[count + 2 :])
    for half in range(2):
        opposite = opposite_rows(core_ref[0], half)
        if own:
            values, first = stacked(other, opposite), half * rows
        else:
            values, first = stacked(mine, half * rows), opposite
        near_values, side_values = values[: 4 * rows], values[4 * rows :]
        for begin, size in spans(4 * rows) + [(4 * rows, rows)]:
            place = pl.ds(begin, size)
            weights = jnp.concatenate(
                [side_ref[half, :, place], far_ref[half, :, place]], axis=0
            )
            total = transposed_dot(weights, side_values)
            if begin < 4 * rows:
                total = total + parts[half][place, :]
            else:
                total = total + jnp.dot(
                    line_ref[half, :, : 4 * rows],
                    near_values,
                    preferred_element_type=jnp.float32,
                )
            store_chips(sums, first, begin, total)


def joined_kernel(*refs):
    first = 0
    for ref in refs[:-1]:
        refs[-1][pl.ds(first, ref.shape[0]), :] = ref[...]
        first += ref.shape[0]


def joined(arrays, after=()):
    shape = (sum(array.shape[0] for array in arrays), arrays[0].shape[1])
    return call(joined_kernel, [shape], (), arrays, after=after)[0]


def final_kernel(scale_ref, core_ref, raw_ref, *refs):
    parts, (keep_ref, give_ref) = refs[:-2], refs[-2:]
    first_core = core_ref[0] == 0
    grads = []
    for half in range(2):
        place = pl.ds(half * rows, rows)
        unit, inverse = unit_rows(raw_ref[place, :].astype(jnp.float32))
        direction = parts[0][place, :].astype(jnp.float32)
        for part in parts[1:]:
            direction = direction + part[place, :].astype(jnp.float32)
        direction = direction * scale_ref[0]
        along = jnp.sum(unit * direction, axis=1, keepdims=True)
        grads.append(inverse * (direction - unit * along))
    low, high = grads
    keep_ref[...] = jnp.where(first_core, low, high).astype(jnp.bfloat16)
    give_ref[...] = jnp.where(first_core, high, low).astype(jnp.bfloat16)


def call(kernel, out_shape, scalars, arrays, flops=0, after=(), scratch=(), kind=jnp.bfloat16):
    used = len(scalars) + len(arrays)

    def body(*refs):
        kernel(*refs[:used], *refs[used + len(after) :])

    return pl.pallas_call(
        body,
        in_specs=[pl.BlockSpec(memory_space=pltpu.SMEM)] * len(scalars)
        + [pl.BlockSpec(memory_space=pltpu.VMEM)] * len(arrays)
        + [pl.BlockSpec(memory_space=pl.ANY)] * len(after),
        out_specs=[pl.BlockSpec(memory_space=pltpu.VMEM)] * len(out_shape),
        out_shape=[jax.ShapeDtypeStruct(shape, kind) for shape in out_shape],
        scratch_shapes=list(scratch),
        compiler_params=pltpu.CompilerParams(vmem_limit_bytes=8 * 2**20),
        cost_estimate=pl.CostEstimate(
            flops=flops, bytes_accessed=2**20, transcendentals=0
        ),
    )(*scalars, *arrays, *after)


def add_kernel(groups, *refs):
    count = len(groups)
    inputs, sums = refs[: -count], refs[-count:]
    for sum_ref, group in zip(sums, groups):
        total = None
        for index, first in group:
            part = inputs[index][pl.ds(first, chip_rows), :].astype(jnp.float32)
            total = part if total is None else total + part
        sum_ref[...] = total.astype(sum_ref.dtype)


def add(groups, after=(), flops=0, kind=jnp.bfloat16):
    arrays = []
    places = []
    for group in groups:
        place = []
        for part in group:
            array, first = part if isinstance(part, tuple) else (part, 0)
            if not any(array is known for known in arrays):
                arrays.append(array)
            index = [array is known for known in arrays].index(True)
            place.append((index, first))
        places.append(place)
    return call(
        functools.partial(add_kernel, places),
        [(chip_rows, arrays[0].shape[1])] * len(groups),
        (),
        arrays,
        flops,
        after,
        kind=kind,
    )


def on_device(image_embeds, text_embeds, log_scale, logit_bias):
    width = image_embeds.shape[1]
    core = lax.axis_index("core")
    first_core = core == 0
    cores = core.astype(jnp.int32).reshape(1)
    logit_scale = jnp.exp(log_scale)
    factors = jnp.concatenate([-log2_e * logit_scale, -log2_e * logit_bias])
    give = jnp.where(first_core, text_embeds, image_embeds)
    keep = jnp.where(first_core, image_embeds, text_embeds)
    got = swap(give)
    unit, raw = call(
        pack_kernel,
        [(chip_rows, width)] * 2,
        (cores,),
        (keep, got),
    )
    left, right, across = ring(unit, 1), ring(unit, -1), pair(unit)
    halves = [ring(left[:rows], 1), ring(right[rows:], -1)]
    far_left, far_right = ring(across, 1), ring(across, -1)
    distant = joined(halves)
    far_distant = pair(distant)
    near = [unit, left, right, across, distant]
    near_other = swap(joined(near))
    block = (chip_rows, width)
    share = 16 * rows * rows * width

    def early(half, after):
        return call(
            functools.partial(early_kernel, half, (4, 1)),
            [(4 * rows, width)] * 2,
            (factors, cores),
            (*near[:4], near_other),
            6 * share,
            after,
            [pltpu.VMEM((4 * rows, 4 * rows), jnp.bfloat16)],
            jnp.float32,
        )

    early_low = early(0, ())
    far = [far_left, far_right, far_distant]
    far_joined = joined(far, early_low[:1])
    early_high = early(1, (far_joined,))
    own_parts, other_parts = zip(early_low, early_high)
    row_side, column_side = call(
        side_kernel,
        [(2, rows, 5 * rows)] * 2,
        (factors, cores),
        (*near, near_other),
        2 * share,
        early_high[:1],
    )
    mine = near + far
    other = [near_other, swap(far_joined)]
    far_weights = (2, 3 * rows, 8 * rows)
    column_far, far_back = call(
        functools.partial(far_kernel, False, (len(mine), len(other))),
        [far_weights, (3 * chip_rows, width)],
        (factors, cores),
        (*mine, *other),
        12 * share,
        (row_side,),
    )
    far_shared = swap(far_back)
    row_far, *far_own = call(
        functools.partial(far_kernel, True, (len(mine), len(other))),
        [far_weights] + [block] * 3,
        (factors, cores),
        (*mine, *other),
        12 * share,
        (far_back,),
    )
    far_sums = add(
        [(one, (far_shared, k * chip_rows)) for k, one in enumerate(far_own)]
    )
    arrived = [ring(far_sums[0], -1), ring(far_sums[1], 1), pair(far_sums[2])]
    (near_back,) = call(
        functools.partial(near_kernel, False, (len(mine), 0)),
        [(5 * chip_rows, width)],
        (cores,),
        (row_far, row_side, column_side, *mine, *other_parts),
        5 * share,
        (far_sums[0],),
    )
    near_shared = swap(near_back)
    near_own = call(
        functools.partial(near_kernel, True, (0, len(other))),
        [block] * 5,
        (cores,),
        (column_far, column_side, row_side, *other, *own_parts),
        5 * share,
        (near_back,),
    )
    near_sums = add(
        [(one, (near_shared, k * chip_rows)) for k, one in enumerate(near_own)]
    )
    across_total, distant_total = add(
        [(near_sums[3], arrived[0], arrived[1]), (near_sums[4], arrived[2])],
        (near_sums[0],),
    )
    late = [ring(distant_total, 2), pair(across_total)]
    (near_total,) = add(
        [(near_sums[0], ring(near_sums[1], -1), ring(near_sums[2], 1))],
        (),
        64 * share,
        jnp.float32,
    )
    parts = [near_total, *late]
    keep, give = call(
        final_kernel, [(rows, width)] * 2, (logit_scale, cores), (raw, *parts)
    )
    given = swap(give)
    image_grad = jnp.where(first_core, keep, given)
    text_grad = jnp.where(first_core, given, keep)
    return (image_grad, text_grad)


def solution(mesh):
    fine = Mesh(mesh.devices.reshape(extents), axes)
    split = P(axes, None)
    return jax.shard_map(
        on_device,
        mesh=fine,
        in_specs=(split, split, P(), P()),
        out_specs=(split, split),
        check_vma=False,
    )
```

```python
import functools

import jax
import jax.numpy as jnp
from jax import lax
from jax.experimental import pallas as pl
from jax.experimental.pallas import tpu as pltpu
from jax.sharding import Mesh, PartitionSpec as P

norm_eps = 1e-06
log2_e = 1.4426950408889634
axes = ("yh", "z", "x", "yl", "core")
extents = (2, 4, 4, 2, 2)
rows = 160
chip_rows = 2 * rows
chunk = 256


def pairs_of(move):
    pairs = []
    for yh in range(2):
        for z in range(4):
            for x in range(4):
                for yl in range(2):
                    for core in range(2):
                        place = (yh, z, x, yl, core)
                        pairs.append((linear(place), linear(move(*place))))
    return pairs


def linear(place):
    index = 0
    for value, extent in zip(place, extents):
        index = index * extent + value
    return index


def ring_move(steps):
    def move(yh, z, x, yl, core):
        if core == 0:
            return (yh, z, (x + steps) % 4, yl, core)
        return (yh, (z + steps) % 4, x, yl, core)

    return pairs_of(move)


def ring(value, steps):
    return lax.ppermute(value, axes, ring_move(steps))


def pair(value):
    def move(yh, z, x, yl, core):
        if core == 0:
            return (yh, z, x, 1 - yl, core)
        return (1 - yh, z, x, 1 - yl, core)

    return lax.ppermute(value, axes, pairs_of(move))


def swap(value):
    return lax.ppermute(value, "core", [(0, 1), (1, 0)])


def unit_rows(values):
    inverse = lax.rsqrt(jnp.sum(values * values, axis=1, keepdims=True) + norm_eps)
    return values * inverse, inverse


def pack_kernel(core_ref, keep_ref, got_ref, unit_ref, raw_ref):
    first_core = core_ref[0] == 0
    keep = keep_ref[...].astype(jnp.float32)
    got = got_ref[...].astype(jnp.float32)
    low = jnp.where(first_core, keep, got)
    high = jnp.where(first_core, got, keep)
    for half, values in enumerate((low, high)):
        place = pl.ds(half * rows, rows)
        unit_ref[place, :] = unit_rows(values)[0].astype(jnp.bfloat16)
        raw_ref[place, :] = values.astype(jnp.bfloat16)


def stacked(places, begin):
    return jnp.concatenate(
        [ref[pl.ds(first + begin, rows), :] for ref, first in places], axis=0
    )


def places_of(refs):
    return [
        (ref, first) for ref in refs for first in range(0, ref.shape[0], chip_rows)
    ]


def opposite_rows(core, half):
    return pl.multiple_of(jnp.where(core == 0, half, 1 - half) * rows, rows)


def spans(count):
    return [(begin, min(chunk, count - begin)) for begin in range(0, count, chunk)]


def weights_of(scale_ref, mine_rows, other_rows, matched=None):
    dots = lax.dot_general(
        mine_rows,
        other_rows,
        (((1,), (1,)), ((), ())),
        preferred_element_type=jnp.float32,
    )
    power = jnp.exp2(dots * scale_ref[0] + scale_ref[1])
    share = pl.reciprocal(1.0 + power, approx=True)
    if matched is not None:
        row = lax.broadcasted_iota(jnp.int32, dots.shape, 0)
        column = lax.broadcasted_iota(jnp.int32, dots.shape, 1)
        share = jnp.where((row == column) & (row < rows) & matched, -power * share, share)
    return share.astype(jnp.bfloat16)


def transposed_dot(weights, values):
    return lax.dot_general(
        weights, values, (((0,), (0,)), ((), ())), preferred_element_type=jnp.float32
    )


def store_chips(refs, first, begin, total):
    done = 0
    while done < total.shape[0]:
        chip, offset = divmod(begin + done, rows)
        size = min(rows - offset, total.shape[0] - done)
        ref, base = refs[chip]
        ref[pl.ds(base + first + offset, size), :] = total[done : done + size].astype(
            ref.dtype
        )
        done += size


def main_kernel(pieces, scale_ref, core_ref, *refs):
    mine, other = places_of(refs[: pieces[0]]), places_of(refs[pieces[0] : sum(pieces)])
    weights_ref, sums = refs[sum(pieces)], places_of(refs[sum(pieces) + 1 :])
    core = core_ref[0]
    count = len(mine) * rows
    near = count - len(sums) * rows
    for half in range(2):
        opposite = opposite_rows(core, half)
        mine_rows = stacked(mine, half * rows)
        other_rows = stacked(other, opposite)
        for begin, size in spans(count):
            weights_ref[half, :, pl.ds(begin, size)] = weights_of(
                scale_ref,
                mine_rows,
                other_rows[begin : begin + size],
                core == 0 if begin == 0 else None,
            )
        for begin, size in spans(count - near):
            total = transposed_dot(
                weights_ref[half, :, pl.ds(near + begin, size)], mine_rows
            )
            store_chips(sums, opposite, begin, total)


def far_kernel(pieces, core_ref, weights_ref, *refs):
    other, sums = places_of(refs[:pieces]), places_of(refs[pieces:])
    count = len(other) * rows
    near = count - len(sums) * rows
    for half in range(2):
        other_rows = stacked(other, opposite_rows(core_ref[0], half))
        total = jnp.dot(
            weights_ref[half, pl.ds(near, count - near), :],
            other_rows,
            preferred_element_type=jnp.float32,
        )
        store_chips(sums, half * rows, 0, total)


def near_kernel(pieces, core_ref, weights_ref, *refs):
    mine, other = places_of(refs[: pieces[0]]), places_of(refs[pieces[0] : sum(pieces)])
    sums = places_of(refs[sum(pieces) :])
    near = len(sums) // 2
    for half in range(2):
        opposite = opposite_rows(core_ref[0], half)
        mine_rows = stacked(mine, half * rows)
        other_rows = stacked(other, opposite)
        for begin, size in spans(near * rows):
            place = pl.ds(begin, size)
            total = transposed_dot(weights_ref[half, :, place], mine_rows)
            store_chips(sums[:near], opposite, begin, total)
        total = jnp.dot(
            weights_ref[half, pl.ds(0, near * rows), :],
            other_rows,
            preferred_element_type=jnp.float32,
        )
        store_chips(sums[near:], half * rows, 0, total)


def joined_kernel(*refs):
    first = 0
    for ref in refs[:-1]:
        refs[-1][pl.ds(first, ref.shape[0]), :] = ref[...]
        first += ref.shape[0]


def joined(arrays, after=()):
    shape = (sum(array.shape[0] for array in arrays), arrays[0].shape[1])
    return call(joined_kernel, [shape], (), arrays, after=after)[0]


def final_kernel(scale_ref, core_ref, raw_ref, *refs):
    parts, (keep_ref, give_ref) = refs[:-2], refs[-2:]
    first_core = core_ref[0] == 0
    grads = []
    for half in range(2):
        place = pl.ds(half * rows, rows)
        unit, inverse = unit_rows(raw_ref[place, :].astype(jnp.float32))
        direction = parts[0][place, :].astype(jnp.float32)
        for part in parts[1:]:
            direction = direction + part[place, :].astype(jnp.float32)
        direction = direction * scale_ref[0]
        along = jnp.sum(unit * direction, axis=1, keepdims=True)
        grads.append(inverse * (direction - unit * along))
    low, high = grads
    keep_ref[...] = jnp.where(first_core, low, high).astype(jnp.bfloat16)
    give_ref[...] = jnp.where(first_core, high, low).astype(jnp.bfloat16)


def call(kernel, out_shape, scalars, arrays, flops=0, after=(), kind=jnp.bfloat16):
    used = len(scalars) + len(arrays)

    def body(*refs):
        kernel(*refs[:used], *refs[used + len(after) :])

    return pl.pallas_call(
        body,
        in_specs=[pl.BlockSpec(memory_space=pltpu.SMEM)] * len(scalars)
        + [pl.BlockSpec(memory_space=pltpu.VMEM)] * len(arrays)
        + [pl.BlockSpec(memory_space=pl.ANY)] * len(after),
        out_specs=[pl.BlockSpec(memory_space=pltpu.VMEM)] * len(out_shape),
        out_shape=[jax.ShapeDtypeStruct(shape, kind) for shape in out_shape],
        compiler_params=pltpu.CompilerParams(vmem_limit_bytes=16 * 2**20),
        cost_estimate=pl.CostEstimate(
            flops=flops, bytes_accessed=2**20, transcendentals=0
        ),
    )(*scalars, *arrays, *after)


def add_kernel(groups, *refs):
    count = len(groups)
    inputs, sums = refs[: -count], refs[-count:]
    for sum_ref, group in zip(sums, groups):
        total = None
        for index, first in group:
            part = inputs[index][pl.ds(first, chip_rows), :].astype(jnp.float32)
            total = part if total is None else total + part
        sum_ref[...] = total.astype(sum_ref.dtype)


def add(groups, after=(), flops=0, kind=jnp.bfloat16):
    arrays = []
    places = []
    for group in groups:
        place = []
        for part in group:
            array, first = part if isinstance(part, tuple) else (part, 0)
            if not any(array is known for known in arrays):
                arrays.append(array)
            index = [array is known for known in arrays].index(True)
            place.append((index, first))
        places.append(place)
    return call(
        functools.partial(add_kernel, places),
        [(chip_rows, arrays[0].shape[1])] * len(groups),
        (),
        arrays,
        flops,
        after,
        kind,
    )


def on_device(image_embeds, text_embeds, log_scale, logit_bias):
    width = image_embeds.shape[1]
    core = lax.axis_index("core")
    first_core = core == 0
    cores = core.astype(jnp.int32).reshape(1)
    logit_scale = jnp.exp(log_scale)
    factors = jnp.concatenate([-log2_e * logit_scale, -log2_e * logit_bias])
    give = jnp.where(first_core, text_embeds, image_embeds)
    keep = jnp.where(first_core, image_embeds, text_embeds)
    got = swap(give)
    unit, raw = call(
        pack_kernel,
        [(chip_rows, width)] * 2,
        (cores,),
        (keep, got),
    )
    left, right, across = ring(unit, 1), ring(unit, -1), pair(unit)
    distant = jnp.concatenate([ring(left[:rows], 1), ring(right[rows:], -1)], axis=0)
    near = [unit, left, right, across]
    far = [distant, ring(across, 1), ring(across, -1), pair(distant)]
    mine = near + far
    other = [
        swap(unit),
        swap(jnp.concatenate([left, right], axis=0)),
        swap(across),
        swap(distant),
        swap(jnp.concatenate(far[1:3], axis=0)),
        swap(far[3]),
    ]
    count = len(mine) * rows
    block = (chip_rows, width)
    four_blocks = (4 * chip_rows, width)
    quarter = count * count * width
    weights, far_back = call(
        functools.partial(main_kernel, (len(mine), len(other))),
        [(2, count, count), four_blocks],
        (factors, cores),
        (*mine, *other),
        6 * quarter,
    )
    far_shared = swap(far_back)
    far_own = call(
        functools.partial(far_kernel, len(other)),
        [block] * 4,
        (cores,),
        (weights, *other),
        2 * quarter,
    )
    far_sums = add(
        [(one, (far_shared, k * chip_rows)) for k, one in enumerate(far_own)]
    )
    arrived = [ring(far_sums[1], -1), ring(far_sums[2], 1), pair(far_sums[3])]
    near_back, *near_own = call(
        functools.partial(near_kernel, (len(mine), len(other))),
        [four_blocks] + [block] * 4,
        (cores,),
        (weights, *mine, *other),
        4 * quarter,
        (far_sums[0],),
    )
    distant_total, across_part = add(
        [(far_sums[0], arrived[2]), (near_own[3], arrived[0], arrived[1])], (near_back,)
    )
    near_shared = swap(joined([near_back], (distant_total,)))
    (near_part,) = add([(near_own[0], ring(distant_total, 2))], (), 0, jnp.float32)
    left_total, right_total, across_total = add(
        [(near_own[k], (near_shared, k * chip_rows)) for k in (1, 2)]
        + [(across_part, (near_shared, 3 * chip_rows))],
        (distant_total,),
    )
    parts = [
        near_part,
        near_shared[:chip_rows],
        ring(left_total, -1),
        ring(right_total, 1),
        pair(across_total),
    ]
    keep, give = call(
        final_kernel, [(rows, width)] * 2, (logit_scale, cores), (raw, *parts)
    )
    given = swap(give)
    image_grad = jnp.where(first_core, keep, given)
    text_grad = jnp.where(first_core, given, keep)
    return (image_grad, text_grad)


def solution(mesh):
    fine = Mesh(mesh.devices.reshape(extents), axes)
    split = P(axes, None)
    return jax.shard_map(
        on_device,
        mesh=fine,
        in_specs=(split, split, P(), P()),
        out_specs=(split, split),
        check_vma=False,
    )
```

```python
import functools

import jax
import jax.numpy as jnp
from jax import lax
from jax.experimental import pallas as pl
from jax.experimental.pallas import tpu as pltpu
from jax.sharding import Mesh, PartitionSpec as P

norm_eps = 1e-06
log2_e = 1.4426950408889634
axes = ("yh", "z", "x", "yl", "core")
extents = (2, 4, 4, 2, 2)
rows = 160
chip_rows = 2 * rows
chunk = 256


def pairs_of(move):
    pairs = []
    for yh in range(2):
        for z in range(4):
            for x in range(4):
                for yl in range(2):
                    for core in range(2):
                        place = (yh, z, x, yl, core)
                        pairs.append((linear(place), linear(move(*place))))
    return pairs


def linear(place):
    index = 0
    for value, extent in zip(place, extents):
        index = index * extent + value
    return index


def ring_move(steps):
    def move(yh, z, x, yl, core):
        if core == 0:
            return (yh, z, (x + steps) % 4, yl, core)
        return (yh, (z + steps) % 4, x, yl, core)

    return pairs_of(move)


def ring(value, steps):
    return lax.ppermute(value, axes, ring_move(steps))


def pair(value):
    def move(yh, z, x, yl, core):
        if core == 0:
            return (yh, z, x, 1 - yl, core)
        return (1 - yh, z, x, 1 - yl, core)

    return lax.ppermute(value, axes, pairs_of(move))


def swap(value):
    return lax.ppermute(value, "core", [(0, 1), (1, 0)])


def unit_rows(values):
    inverse = lax.rsqrt(jnp.sum(values * values, axis=1, keepdims=True) + norm_eps)
    return values * inverse, inverse


def pack_kernel(core_ref, keep_ref, got_ref, unit_ref, raw_ref):
    first_core = core_ref[0] == 0
    keep = keep_ref[...].astype(jnp.float32)
    got = got_ref[...].astype(jnp.float32)
    low = jnp.where(first_core, keep, got)
    high = jnp.where(first_core, got, keep)
    for half, values in enumerate((low, high)):
        place = pl.ds(half * rows, rows)
        unit_ref[place, :] = unit_rows(values)[0].astype(jnp.bfloat16)
        raw_ref[place, :] = values.astype(jnp.bfloat16)


def stacked(places, begin):
    return jnp.concatenate(
        [ref[pl.ds(first + begin, rows), :] for ref, first in places], axis=0
    )


def places_of(refs):
    return [
        (ref, first) for ref in refs for first in range(0, ref.shape[0], chip_rows)
    ]


def opposite_rows(core, half):
    return pl.multiple_of(jnp.where(core == 0, half, 1 - half) * rows, rows)


def spans(count):
    return [(begin, min(chunk, count - begin)) for begin in range(0, count, chunk)]


def weights_of(scale_ref, mine_rows, other_rows, matched=None):
    dots = lax.dot_general(
        mine_rows,
        other_rows,
        (((1,), (1,)), ((), ())),
        preferred_element_type=jnp.float32,
    )
    power = jnp.exp2(dots * scale_ref[0] + scale_ref[1])
    share = pl.reciprocal(1.0 + power, approx=True)
    if matched is not None:
        row = lax.broadcasted_iota(jnp.int32, dots.shape, 0)
        column = lax.broadcasted_iota(jnp.int32, dots.shape, 1)
        share = jnp.where((row == column) & (row < rows) & matched, -power * share, share)
    return share.astype(jnp.bfloat16)


def transposed_dot(weights, values):
    return lax.dot_general(
        weights, values, (((0,), (0,)), ((), ())), preferred_element_type=jnp.float32
    )


def store_chips(refs, first, begin, total):
    done = 0
    while done < total.shape[0]:
        chip, offset = divmod(begin + done, rows)
        size = min(rows - offset, total.shape[0] - done)
        ref, base = refs[chip]
        ref[pl.ds(base + first + offset, size), :] = total[done : done + size].astype(
            ref.dtype
        )
        done += size


def first_kernel(pieces, scale_ref, core_ref, *refs):
    mine, other = places_of(refs[: pieces[0]]), places_of(refs[pieces[0] : sum(pieces)])
    far_ref, near_ref = refs[sum(pieces) :]
    for half in range(2):
        mine_rows = stacked(mine, half * rows)
        other_rows = stacked(other, opposite_rows(core_ref[0], half))
        edge = 4 * rows - near_ref.shape[2]
        near_ref[half] = weights_of(scale_ref, mine_rows, other_rows[edge : 4 * rows])
        for begin, size in spans(4 * rows):
            place = pl.ds(begin, size)
            far_ref[half, :, place] = weights_of(
                scale_ref,
                mine_rows,
                other_rows[4 * rows + begin : 4 * rows + begin + size],
            )


def second_kernel(pieces, scale_ref, core_ref, far_ref, edge_ref, *refs):
    mine, other = places_of(refs[: pieces[0]]), places_of(refs[pieces[0] : sum(pieces)])
    near_ref, part_ref = refs[sum(pieces) :]
    core = core_ref[0]
    edge = 4 * rows - edge_ref.shape[2]
    for half in range(2):
        mine_rows = stacked(mine, half * rows)
        other_rows = stacked(other, opposite_rows(core, half))
        for begin, size in spans(edge):
            near_ref[half, :, pl.ds(begin, size)] = weights_of(
                scale_ref,
                mine_rows,
                other_rows[begin : begin + size],
                core == 0 if begin == 0 else None,
            )
        near_ref[half, :, pl.ds(edge, edge_ref.shape[2])] = edge_ref[half]
        place = pl.ds(4 * rows, 4 * rows)
        weights = jnp.concatenate(
            [near_ref[half, place, :], far_ref[half, place, :]], axis=1
        )
        part_ref[half] = jnp.dot(
            weights, other_rows, preferred_element_type=jnp.float32
        )


def received(core, half, weights_ref, other):
    its_half = jnp.where(core == 0, 1 - half, half)
    other_rows = stacked(other, pl.multiple_of(its_half * rows, rows))
    return transposed_dot(weights_ref[its_half], other_rows)


def far_kernel(pieces, core_ref, weights_ref, part_ref, *refs):
    other, sums = places_of(refs[:pieces]), places_of(refs[pieces:])
    for half in range(2):
        total = part_ref[half] + received(core_ref[0], half, weights_ref, other)
        store_chips(sums, half * rows, 0, total)


def near_kernel(pieces, core_ref, far_ref, near_ref, weights_ref, *refs):
    other, sums = places_of(refs[:pieces]), places_of(refs[pieces:])
    core = core_ref[0]
    for half in range(2):
        place = pl.ds(0, 4 * rows)
        weights = jnp.concatenate(
            [near_ref[half, place, :], far_ref[half, place, :]], axis=1
        )
        other_rows = stacked(other, opposite_rows(core, half))
        total = jnp.dot(weights, other_rows, preferred_element_type=jnp.float32)
        total = total + received(core, half, weights_ref, other)
        store_chips(sums, half * rows, 0, total)


def final_kernel(scale_ref, core_ref, raw_ref, *refs):
    parts, (keep_ref, give_ref) = refs[:-2], refs[-2:]
    first_core = core_ref[0] == 0
    grads = []
    for half in range(2):
        place = pl.ds(half * rows, rows)
        unit, inverse = unit_rows(raw_ref[place, :].astype(jnp.float32))
        direction = parts[0][place, :].astype(jnp.float32)
        for part in parts[1:]:
            direction = direction + part[place, :].astype(jnp.float32)
        direction = direction * scale_ref[0]
        along = jnp.sum(unit * direction, axis=1, keepdims=True)
        grads.append(inverse * (direction - unit * along))
    low, high = grads
    keep_ref[...] = jnp.where(first_core, low, high).astype(jnp.bfloat16)
    give_ref[...] = jnp.where(first_core, high, low).astype(jnp.bfloat16)


def call(kernel, out_shape, scalars, arrays, flops=0, after=(), kinds=None):
    kinds = kinds or [jnp.bfloat16] * len(out_shape)
    used = len(scalars) + len(arrays)

    def body(*refs):
        kernel(*refs[:used], *refs[used + len(after) :])

    return pl.pallas_call(
        body,
        in_specs=[pl.BlockSpec(memory_space=pltpu.SMEM)] * len(scalars)
        + [pl.BlockSpec(memory_space=pltpu.VMEM)] * len(arrays)
        + [pl.BlockSpec(memory_space=pl.ANY)] * len(after),
        out_specs=[pl.BlockSpec(memory_space=pltpu.VMEM)] * len(out_shape),
        out_shape=[
            jax.ShapeDtypeStruct(shape, kind_of)
            for shape, kind_of in zip(out_shape, kinds)
        ],
        compiler_params=pltpu.CompilerParams(vmem_limit_bytes=16 * 2**20),
        cost_estimate=pl.CostEstimate(
            flops=flops, bytes_accessed=2**20, transcendentals=0
        ),
    )(*scalars, *arrays, *after)


def add_kernel(groups, *refs):
    count = len(groups)
    inputs, sums = refs[: -count], refs[-count:]
    for sum_ref, group in zip(sums, groups):
        total = None
        for index, first in group:
            part = inputs[index][pl.ds(first, chip_rows), :].astype(jnp.float32)
            total = part if total is None else total + part
        sum_ref[...] = total.astype(sum_ref.dtype)


def add(groups, after=()):
    arrays = []
    places = []
    for group in groups:
        place = []
        for part in group:
            array, first = part if isinstance(part, tuple) else (part, 0)
            if not any(array is known for known in arrays):
                arrays.append(array)
            index = [array is known for known in arrays].index(True)
            place.append((index, first))
        places.append(place)
    return call(
        functools.partial(add_kernel, places),
        [(chip_rows, arrays[0].shape[1])] * len(groups),
        (),
        arrays,
        after=after,
    )


def on_device(image_embeds, text_embeds, log_scale, logit_bias):
    width = image_embeds.shape[1]
    core = lax.axis_index("core")
    first_core = core == 0
    cores = core.astype(jnp.int32).reshape(1)
    logit_scale = jnp.exp(log_scale)
    factors = jnp.concatenate([-log2_e * logit_scale, -log2_e * logit_bias])
    give = jnp.where(first_core, text_embeds, image_embeds)
    keep = jnp.where(first_core, image_embeds, text_embeds)
    got = swap(give)
    unit, raw = call(
        pack_kernel,
        [(chip_rows, width)] * 2,
        (cores,),
        (keep, got),
    )
    left, right, across = ring(unit, 1), ring(unit, -1), pair(unit)
    distant = jnp.concatenate([ring(left[:rows], 1), ring(right[rows:], -1)], axis=0)
    near = [unit, left, right, across]
    far = [distant, ring(across, 1), ring(across, -1), pair(distant)]
    mine = near + far
    other = [
        swap(unit),
        swap(jnp.concatenate([left, right], axis=0)),
        swap(across),
        swap(distant),
        swap(jnp.concatenate(far[1:3], axis=0)),
        swap(far[3]),
    ]
    near_rows, all_rows = 4 * rows, 8 * rows
    edge = near_rows % chunk
    block = (chip_rows, width)
    share = all_rows * all_rows * width
    sizes = (len(mine), len(other))
    far_weights, edge_weights = call(
        functools.partial(first_kernel, sizes),
        [(2, all_rows, near_rows), (2, all_rows, edge)],
        (factors, cores),
        (*mine, *other),
        2 * share,
    )
    far_received = swap(far_weights)
    near_weights, far_part = call(
        functools.partial(second_kernel, sizes),
        [(2, all_rows, near_rows), (2, near_rows, width)],
        (factors, cores),
        (far_weights, edge_weights, *mine, *other),
        4 * share,
        kinds=(jnp.bfloat16, jnp.float32),
    )
    near_received = swap(near_weights)
    far_sums = call(
        functools.partial(far_kernel, len(other)),
        [block] * 4,
        (cores,),
        (far_received, far_part, *other),
        2 * share,
    )
    arrived = [ring(far_sums[1], -1), ring(far_sums[2], 1), pair(far_sums[3])]
    near_sums = call(
        functools.partial(near_kernel, len(other)),
        [block] * 4,
        (cores,),
        (far_weights, near_weights, near_received, *other),
        4 * share,
    )
    distant_total, across_total = add(
        [(far_sums[0], arrived[2]), (near_sums[3], arrived[0], arrived[1])],
        (near_sums[0],),
    )
    parts = [
        near_sums[0],
        ring(near_sums[1], -1),
        ring(near_sums[2], 1),
        ring(distant_total, 2),
        pair(across_total),
    ]
    keep, give = call(
        final_kernel, [(rows, width)] * 2, (logit_scale, cores), (raw, *parts)
    )
    given = swap(give)
    image_grad = jnp.where(first_core, keep, given)
    text_grad = jnp.where(first_core, given, keep)
    return (image_grad, text_grad)


def solution(mesh):
    fine = Mesh(mesh.devices.reshape(extents), axes)
    split = P(axes, None)
    return jax.shard_map(
        on_device,
        mesh=fine,
        in_specs=(split, split, P(), P()),
        out_specs=(split, split),
        check_vma=False,
    )
```

```python
import functools

import jax
import jax.numpy as jnp
from jax import lax
from jax.experimental import pallas as pl
from jax.experimental.pallas import tpu as pltpu
from jax.sharding import Mesh, PartitionSpec as P

norm_eps = 1e-06
log2_e = 1.4426950408889634
axes = ("yh", "z", "x", "yl", "core")
extents = (2, 4, 4, 2, 2)
rows = 160
chip_rows = 2 * rows
chunk = 256


def pairs_of(move):
    pairs = []
    for yh in range(2):
        for z in range(4):
            for x in range(4):
                for yl in range(2):
                    for core in range(2):
                        place = (yh, z, x, yl, core)
                        pairs.append((linear(place), linear(move(*place))))
    return pairs


def linear(place):
    index = 0
    for value, extent in zip(place, extents):
        index = index * extent + value
    return index


def ring_move(steps):
    def move(yh, z, x, yl, core):
        if core == 0:
            return (yh, z, (x + steps) % 4, yl, core)
        return (yh, (z + steps) % 4, x, yl, core)

    return pairs_of(move)


def ring(value, steps):
    return lax.ppermute(value, axes, ring_move(steps))


def pair(value):
    def move(yh, z, x, yl, core):
        if core == 0:
            return (yh, z, x, 1 - yl, core)
        return (1 - yh, z, x, 1 - yl, core)

    return lax.ppermute(value, axes, pairs_of(move))


def swap(value):
    return lax.ppermute(value, "core", [(0, 1), (1, 0)])


def unit_rows(values):
    inverse = lax.rsqrt(jnp.sum(values * values, axis=1, keepdims=True) + norm_eps)
    return values * inverse, inverse


def pack_kernel(core_ref, keep_ref, got_ref, unit_ref, raw_ref):
    first_core = core_ref[0] == 0
    keep = keep_ref[...].astype(jnp.float32)
    got = got_ref[...].astype(jnp.float32)
    low = jnp.where(first_core, keep, got)
    high = jnp.where(first_core, got, keep)
    for half, values in enumerate((low, high)):
        place = pl.ds(half * rows, rows)
        unit_ref[place, :] = unit_rows(values)[0].astype(jnp.bfloat16)
        raw_ref[place, :] = values.astype(jnp.bfloat16)


def stacked(places, begin):
    return jnp.concatenate(
        [ref[pl.ds(first + begin, rows), :] for ref, first in places], axis=0
    )


def places_of(refs):
    return [
        (ref, first) for ref in refs for first in range(0, ref.shape[0], chip_rows)
    ]


def opposite_rows(core, half):
    return pl.multiple_of(jnp.where(core == 0, half, 1 - half) * rows, rows)


def spans(count):
    return [(begin, min(chunk, count - begin)) for begin in range(0, count, chunk)]


def weights_of(scale_ref, mine_rows, other_rows, matched=None):
    blocks = []
    for begin in range(0, mine_rows.shape[0], 2 * rows):
        dots = lax.dot_general(
            mine_rows[begin : begin + 2 * rows],
            other_rows,
            (((1,), (1,)), ((), ())),
            preferred_element_type=jnp.float32,
        )
        power = jnp.exp2(dots * scale_ref[0] + scale_ref[1])
        share = pl.reciprocal(1.0 + power, approx=True)
        if matched is not None and begin == 0:
            row = lax.broadcasted_iota(jnp.int32, dots.shape, 0)
            column = lax.broadcasted_iota(jnp.int32, dots.shape, 1)
            own = (row == column) & (row < rows) & matched
            share = jnp.where(own, -power * share, share)
        blocks.append(share.astype(jnp.bfloat16))
    return jnp.concatenate(blocks, axis=0)


def transposed_dot(weights, values):
    return lax.dot_general(
        weights, values, (((0,), (0,)), ((), ())), preferred_element_type=jnp.float32
    )


def store_chips(refs, first, begin, total):
    done = 0
    while done < total.shape[0]:
        chip, offset = divmod(begin + done, rows)
        size = min(rows - offset, total.shape[0] - done)
        ref, base = refs[chip]
        ref[pl.ds(base + first + offset, size), :] = total[done : done + size].astype(
            ref.dtype
        )
        done += size


def near_weights_kernel(pieces, scale_ref, core_ref, *refs):
    mine, other = places_of(refs[: pieces[0]]), places_of(refs[pieces[0] : sum(pieces)])
    (near_ref,) = refs[sum(pieces) :]
    core = core_ref[0]
    for half in range(2):
        mine_rows = stacked(mine, half * rows)
        other_rows = stacked(other, opposite_rows(core, half))
        for begin, size in spans(near_ref.shape[2]):
            near_ref[half, :, pl.ds(begin, size)] = weights_of(
                scale_ref,
                mine_rows,
                other_rows[begin : begin + size],
                core == 0 if begin == 0 else None,
            )


def far_weights_kernel(pieces, scale_ref, core_ref, *refs):
    mine, other = places_of(refs[: pieces[0]]), places_of(refs[pieces[0] : sum(pieces)])
    edge_ref, far_ref = refs[sum(pieces) :]
    edge = edge_ref.shape[2]
    first = 4 * rows - edge
    for half in range(2):
        mine_rows = stacked(mine, half * rows)
        other_rows = stacked(other, opposite_rows(core_ref[0], half))
        for begin, size in spans(edge + far_ref.shape[2]):
            start = first + begin
            weights = weights_of(
                scale_ref, mine_rows, other_rows[start : start + size]
            )
            if begin == 0:
                edge_ref[half] = weights[:, :edge]
                far_ref[half, :, pl.ds(0, size - edge)] = weights[:, edge:]
            else:
                far_ref[half, :, pl.ds(begin - edge, size)] = weights


def own_product(half, first, count, weights_refs, other_rows):
    weights = jnp.concatenate(
        [ref[half, pl.ds(first, count), :] for ref in weights_refs], axis=1
    )
    return jnp.dot(weights, other_rows, preferred_element_type=jnp.float32)


def own_kernel(pieces, core_ref, *refs):
    weights_refs, other = refs[:3], places_of(refs[3 : 3 + pieces])
    near_ref, far_ref, joined_ref = refs[3 + pieces :]
    edge = 4 * rows - weights_refs[1].shape[2]
    for half in range(2):
        other_rows = stacked(other, opposite_rows(core_ref[0], half))
        joined_ref[half, :, pl.ds(0, edge)] = weights_refs[0][half]
        joined_ref[half, :, pl.ds(edge, 4 * rows - edge)] = weights_refs[1][half]
        far_ref[half] = own_product(
            half, 4 * rows, 4 * rows, weights_refs, other_rows
        )
        near_ref[half] = own_product(half, rows, 3 * rows, weights_refs, other_rows)


def received(core, half, columns, other):
    its_half = jnp.where(core == 0, 1 - half, half)
    other_rows = stacked(other, pl.multiple_of(its_half * rows, rows))
    weights = jnp.concatenate(
        [ref[its_half, :, pl.ds(first, size)] for ref, first, size in columns], axis=1
    )
    return transposed_dot(weights, other_rows)


def far_kernel(pieces, core_ref, weights_ref, part_ref, *refs):
    other, sums = places_of(refs[:pieces]), places_of(refs[pieces:])
    for half in range(2):
        columns = [(weights_ref, 0, 4 * rows)]
        total = part_ref[half] + received(core_ref[0], half, columns, other)
        store_chips(sums, half * rows, 0, total)


def near_kernel(pieces, core_ref, weights_ref, part_ref, *refs):
    other, sums = places_of(refs[:pieces]), places_of(refs[pieces:])
    first = rows // 128 * 128
    columns = [(weights_ref, first, 4 * rows - first)]
    for half in range(2):
        total = received(core_ref[0], half, columns, other)
        total = total[rows - first :] + part_ref[half]
        store_chips(sums, half * rows, 0, total)


def self_kernel(pieces, core_ref, received_ref, *refs):
    weights_refs, other = refs[:3], places_of(refs[3 : 3 + pieces])
    sum_ref = refs[3 + pieces]
    core = core_ref[0]
    for half in range(2):
        other_rows = stacked(other, opposite_rows(core, half))
        total = own_product(half, 0, rows, weights_refs, other_rows)
        total = total + received(core, half, [(received_ref, 0, chunk)], other)[:rows]
        sum_ref[pl.ds(half * rows, rows), :] = total


def final_kernel(scale_ref, core_ref, raw_ref, *refs):
    parts, (keep_ref, give_ref) = refs[:-2], refs[-2:]
    first_core = core_ref[0] == 0
    grads = []
    for half in range(2):
        place = pl.ds(half * rows, rows)
        unit, inverse = unit_rows(raw_ref[place, :].astype(jnp.float32))
        direction = parts[0][place, :].astype(jnp.float32)
        for part in parts[1:]:
            direction = direction + part[place, :].astype(jnp.float32)
        direction = direction * scale_ref[0]
        along = jnp.sum(unit * direction, axis=1, keepdims=True)
        grads.append(inverse * (direction - unit * along))
    low, high = grads
    keep_ref[...] = jnp.where(first_core, low, high).astype(jnp.bfloat16)
    give_ref[...] = jnp.where(first_core, high, low).astype(jnp.bfloat16)


def call(kernel, out_shape, scalars, arrays, flops=0, after=(), kinds=None):
    kinds = kinds or [jnp.bfloat16] * len(out_shape)
    used = len(scalars) + len(arrays)

    def body(*refs):
        kernel(*refs[:used], *refs[used + len(after) :])

    return pl.pallas_call(
        body,
        in_specs=[pl.BlockSpec(memory_space=pltpu.SMEM)] * len(scalars)
        + [pl.BlockSpec(memory_space=pltpu.VMEM)] * len(arrays)
        + [pl.BlockSpec(memory_space=pl.ANY)] * len(after),
        out_specs=[pl.BlockSpec(memory_space=pltpu.VMEM)] * len(out_shape),
        out_shape=[
            jax.ShapeDtypeStruct(shape, kind_of)
            for shape, kind_of in zip(out_shape, kinds)
        ],
        compiler_params=pltpu.CompilerParams(vmem_limit_bytes=16 * 2**20),
        cost_estimate=pl.CostEstimate(
            flops=flops, bytes_accessed=2**20, transcendentals=0
        ),
    )(*scalars, *arrays, *after)


def add_kernel(groups, *refs):
    count = len(groups)
    inputs, sums = refs[: -count], refs[-count:]
    for sum_ref, group in zip(sums, groups):
        total = None
        for index, first in group:
            part = inputs[index][pl.ds(first, chip_rows), :].astype(jnp.float32)
            total = part if total is None else total + part
        sum_ref[...] = total.astype(sum_ref.dtype)


def add(groups, after=()):
    arrays = []
    places = []
    for group in groups:
        place = []
        for part in group:
            array, first = part if isinstance(part, tuple) else (part, 0)
            if not any(array is known for known in arrays):
                arrays.append(array)
            index = [array is known for known in arrays].index(True)
            place.append((index, first))
        places.append(place)
    return call(
        functools.partial(add_kernel, places),
        [(chip_rows, arrays[0].shape[1])] * len(groups),
        (),
        arrays,
        after=after,
    )


def on_device(image_embeds, text_embeds, log_scale, logit_bias):
    width = image_embeds.shape[1]
    core = lax.axis_index("core")
    first_core = core == 0
    cores = core.astype(jnp.int32).reshape(1)
    logit_scale = jnp.exp(log_scale)
    factors = jnp.concatenate([-log2_e * logit_scale, -log2_e * logit_bias])
    give = jnp.where(first_core, text_embeds, image_embeds)
    keep = jnp.where(first_core, image_embeds, text_embeds)
    got = swap(give)
    unit, raw = call(
        pack_kernel,
        [(chip_rows, width)] * 2,
        (cores,),
        (keep, got),
    )
    left, right, across = ring(unit, 1), ring(unit, -1), pair(unit)
    distant = jnp.concatenate([ring(left[:rows], 1), ring(right[rows:], -1)], axis=0)
    near = [unit, left, right, across]
    far = [distant, ring(across, 1), ring(across, -1), pair(distant)]
    mine = near + far
    other = [
        swap(unit),
        swap(jnp.concatenate([left, right], axis=0)),
        swap(across),
        swap(distant),
        swap(jnp.concatenate(far[1:3], axis=0)),
        swap(far[3]),
    ]
    near_rows, all_rows = 4 * rows, 8 * rows
    edge = near_rows % chunk
    block = (chip_rows, width)
    share = all_rows * all_rows * width // 5
    (near_weights,) = call(
        functools.partial(near_weights_kernel, (len(mine), 3)),
        [(2, all_rows, near_rows - edge)],
        (factors, cores),
        (*mine, *other[:3]),
        8 * share,
        (),
    )
    edge_weights, far_weights = call(
        functools.partial(far_weights_kernel, (len(mine), len(other))),
        [(2, all_rows, edge), (2, all_rows, near_rows)],
        (factors, cores),
        (*mine, *other),
        12 * share,
        (near_weights,),
    )
    far_received = swap(far_weights)
    weights = (near_weights, edge_weights, far_weights)
    near_part, far_part, near_joined = call(
        functools.partial(own_kernel, len(other)),
        [(2, 3 * rows, width), (2, 4 * rows, width), (2, all_rows, near_rows)],
        (cores,),
        (*weights, *other),
        18 * share,
        kinds=(jnp.float32, jnp.float32, jnp.bfloat16),
    )
    near_received = swap(near_joined)
    far_sums = call(
        functools.partial(far_kernel, len(other)),
        [block] * 4,
        (cores,),
        (far_received, far_part, *other),
        10 * share,
    )
    arrived = [ring(far_sums[1], -1), ring(far_sums[2], 1), pair(far_sums[3])]
    near_sums = call(
        functools.partial(near_kernel, len(other)),
        [block] * 3,
        (cores,),
        (near_received, near_part, *other),
        8 * share,
    )
    distant_total, across_total = add(
        [(far_sums[0], arrived[2]), (near_sums[2], arrived[0], arrived[1])],
        (near_sums[0],),
    )
    (own_sum,) = call(
        functools.partial(self_kernel, len(other)),
        [block],
        (cores,),
        (near_received, *weights, *other),
        5 * share,
        (distant_total,),
        (jnp.float32,),
    )
    parts = [
        own_sum,
        ring(near_sums[0], -1),
        ring(near_sums[1], 1),
        ring(distant_total, 2),
        pair(across_total),
    ]
    keep, give = call(
        final_kernel, [(rows, width)] * 2, (logit_scale, cores), (raw, *parts)
    )
    given = swap(give)
    image_grad = jnp.where(first_core, keep, given)
    text_grad = jnp.where(first_core, given, keep)
    return (image_grad, text_grad)


def solution(mesh):
    fine = Mesh(mesh.devices.reshape(extents), axes)
    split = P(axes, None)
    return jax.shard_map(
        on_device,
        mesh=fine,
        in_specs=(split, split, P(), P()),
        out_specs=(split, split),
        check_vma=False,
    )
```

```python
import functools

import jax
import jax.numpy as jnp
from jax import lax
from jax.experimental import pallas as pl
from jax.experimental.pallas import tpu as pltpu
from jax.sharding import Mesh, PartitionSpec as P

norm_eps = 1e-06
log2_e = 1.4426950408889634
axes = ("yh", "z", "x", "yl", "core")
extents = (2, 4, 4, 2, 2)
rows = 160
chip_rows = 2 * rows
chunk = 256


def pairs_of(move):
    pairs = []
    for yh in range(2):
        for z in range(4):
            for x in range(4):
                for yl in range(2):
                    for core in range(2):
                        place = (yh, z, x, yl, core)
                        pairs.append((linear(place), linear(move(*place))))
    return pairs


def linear(place):
    index = 0
    for value, extent in zip(place, extents):
        index = index * extent + value
    return index


def ring_move(steps):
    def move(yh, z, x, yl, core):
        if core == 0:
            return (yh, z, (x + steps) % 4, yl, core)
        return (yh, (z + steps) % 4, x, yl, core)

    return pairs_of(move)


def ring(value, steps):
    return lax.ppermute(value, axes, ring_move(steps))


def pair(value):
    def move(yh, z, x, yl, core):
        if core == 0:
            return (yh, z, x, 1 - yl, core)
        return (1 - yh, z, x, 1 - yl, core)

    return lax.ppermute(value, axes, pairs_of(move))


def swap(value):
    return lax.ppermute(value, "core", [(0, 1), (1, 0)])


def unit_rows(values):
    inverse = lax.rsqrt(jnp.sum(values * values, axis=1, keepdims=True) + norm_eps)
    return values * inverse, inverse


def pack_kernel(scale_ref, bias_ref, core_ref, keep_ref, got_ref, *refs):
    unit_ref, low_ref, high_ref, raw_ref, factors_ref = refs
    first_core = core_ref[0] == 0
    scale = jnp.exp(jnp.full((1, 128), scale_ref[0], jnp.float32))
    factors_ref[0:1, :] = -log2_e * scale
    factors_ref[1:2, :] = jnp.full((1, 128), -log2_e * bias_ref[0], jnp.float32)
    factors_ref[2:3, :] = scale
    keep = keep_ref[...].astype(jnp.float32)
    got = got_ref[...].astype(jnp.float32)
    low = jnp.where(first_core, keep, got)
    high = jnp.where(first_core, got, keep)
    for half, values in enumerate((low, high)):
        place = pl.ds(half * rows, rows)
        unit = unit_rows(values)[0].astype(jnp.bfloat16)
        unit_ref[place, :] = unit
        (low_ref, high_ref)[half][...] = unit
        raw_ref[place, :] = values.astype(jnp.bfloat16)


def stacked(places, begin):
    return jnp.concatenate(
        [ref[pl.ds(first + begin, rows), :] for ref, first in places], axis=0
    )


def places_of(refs):
    return [
        (ref, first) for ref in refs for first in range(0, ref.shape[0], chip_rows)
    ]


def opposite_rows(core, half):
    return pl.multiple_of(jnp.where(core == 0, half, 1 - half) * rows, rows)


def spans(count):
    return [(begin, min(chunk, count - begin)) for begin in range(0, count, chunk)]


def weights_of(factors_ref, mine_rows, other_rows, matched=None):
    blocks = []
    for begin in range(0, mine_rows.shape[0], 2 * rows):
        dots = lax.dot_general(
            mine_rows[begin : begin + 2 * rows],
            other_rows,
            (((1,), (1,)), ((), ())),
            preferred_element_type=jnp.float32,
        )
        power = jnp.exp2(dots * factors_ref[0:1, 0:1] + factors_ref[1:2, 0:1])
        share = pl.reciprocal(1.0 + power, approx=True)
        if matched is not None and begin == 0:
            row = lax.broadcasted_iota(jnp.int32, dots.shape, 0)
            column = lax.broadcasted_iota(jnp.int32, dots.shape, 1)
            own = (row == column) & (row < rows) & matched
            share = jnp.where(own, -power * share, share)
        blocks.append(share.astype(jnp.bfloat16))
    return jnp.concatenate(blocks, axis=0)


def transposed_dot(weights, values):
    return lax.dot_general(
        weights, values, (((0,), (0,)), ((), ())), preferred_element_type=jnp.float32
    )


def store_chips(refs, first, begin, total):
    done = 0
    while done < total.shape[0]:
        chip, offset = divmod(begin + done, rows)
        size = min(rows - offset, total.shape[0] - done)
        ref, base = refs[chip]
        ref[pl.ds(base + first + offset, size), :] = total[done : done + size].astype(
            ref.dtype
        )
        done += size


def near_weights_kernel(pieces, core_ref, factors_ref, *refs):
    mine, other = places_of(refs[: pieces[0]]), places_of(refs[pieces[0] : sum(pieces)])
    (near_ref,) = refs[sum(pieces) :]
    core = core_ref[0]
    for half in range(2):
        mine_rows = stacked(mine, half * rows)
        other_rows = stacked(other, opposite_rows(core, half))
        for begin, size in spans(near_ref.shape[2]):
            near_ref[half, :, pl.ds(begin, size)] = weights_of(
                factors_ref,
                mine_rows,
                other_rows[begin : begin + size],
                core == 0 if begin == 0 else None,
            )


def far_weights_kernel(pieces, core_ref, factors_ref, *refs):
    mine, other = places_of(refs[: pieces[0]]), places_of(refs[pieces[0] : sum(pieces)])
    edge_ref, far_ref = refs[sum(pieces) :]
    edge = edge_ref.shape[2]
    first = 4 * rows - edge
    for half in range(2):
        mine_rows = stacked(mine, half * rows)
        other_rows = stacked(other, opposite_rows(core_ref[0], half))
        for begin, size in spans(edge + far_ref.shape[2]):
            start = first + begin
            weights = weights_of(
                factors_ref, mine_rows, other_rows[start : start + size]
            )
            if begin == 0:
                edge_ref[half] = weights[:, :edge]
                far_ref[half, :, pl.ds(0, size - edge)] = weights[:, edge:]
            else:
                far_ref[half, :, pl.ds(begin - edge, size)] = weights


def own_product(half, first, count, weights_refs, other_rows):
    weights = jnp.concatenate(
        [ref[half, pl.ds(first, count), :] for ref in weights_refs], axis=1
    )
    return jnp.dot(weights, other_rows, preferred_element_type=jnp.float32)


def own_kernel(pieces, core_ref, *refs):
    weights_refs, other = refs[:3], places_of(refs[3 : 3 + pieces])
    near_ref, far_ref, joined_ref = refs[3 + pieces :]
    edge = 4 * rows - weights_refs[1].shape[2]
    for half in range(2):
        other_rows = stacked(other, opposite_rows(core_ref[0], half))
        joined_ref[half, :, pl.ds(0, edge)] = weights_refs[0][half]
        joined_ref[half, :, pl.ds(edge, 4 * rows - edge)] = weights_refs[1][half]
        far_ref[half] = own_product(
            half, 4 * rows, 4 * rows, weights_refs, other_rows
        )
        near_ref[half] = own_product(half, rows, 3 * rows, weights_refs, other_rows)


def received(core, half, columns, other):
    its_half = jnp.where(core == 0, 1 - half, half)
    other_rows = stacked(other, pl.multiple_of(its_half * rows, rows))
    weights = jnp.concatenate(
        [ref[its_half, :, pl.ds(first, size)] for ref, first, size in columns], axis=1
    )
    return transposed_dot(weights, other_rows)


def far_kernel(pieces, core_ref, weights_ref, part_ref, *refs):
    other, sums = places_of(refs[:pieces]), places_of(refs[pieces:])
    for half in range(2):
        columns = [(weights_ref, 0, 4 * rows)]
        total = part_ref[half] + received(core_ref[0], half, columns, other)
        store_chips(sums, half * rows, 0, total)


def near_kernel(pieces, core_ref, weights_ref, part_ref, *refs):
    other, sums = places_of(refs[:pieces]), places_of(refs[pieces:])
    first = rows // 128 * 128
    columns = [(weights_ref, first, 4 * rows - first)]
    for half in range(2):
        total = received(core_ref[0], half, columns, other)
        total = total[rows - first :] + part_ref[half]
        store_chips(sums, half * rows, 0, total)


def self_kernel(pieces, core_ref, received_ref, *refs):
    weights_refs, other = refs[:3], places_of(refs[3 : 3 + pieces])
    sum_ref = refs[3 + pieces]
    core = core_ref[0]
    for half in range(2):
        other_rows = stacked(other, opposite_rows(core, half))
        total = own_product(half, 0, rows, weights_refs, other_rows)
        total = total + received(core, half, [(received_ref, 0, chunk)], other)[:rows]
        sum_ref[pl.ds(half * rows, rows), :] = total


def final_kernel(kept, core_ref, factors_ref, raw_ref, *refs):
    parts, grad_ref = refs[:-1], refs[-1]
    half = jnp.where(core_ref[0] == 0, 1 - kept, kept)
    place = pl.ds(pl.multiple_of(half * rows, rows), rows)
    unit, inverse = unit_rows(raw_ref[place, :].astype(jnp.float32))
    direction = parts[0][place, :].astype(jnp.float32)
    for part in parts[1:]:
        direction = direction + part[place, :].astype(jnp.float32)
    direction = direction * factors_ref[2:3, 0:1]
    along = jnp.sum(unit * direction, axis=1, keepdims=True)
    grad_ref[...] = (inverse * (direction - unit * along)).astype(jnp.bfloat16)


def call(kernel, out_shape, scalars, arrays, flops=0, after=(), kinds=None):
    kinds = kinds or [jnp.bfloat16] * len(out_shape)
    used = len(scalars) + len(arrays)

    def body(*refs):
        kernel(*refs[:used], *refs[used + len(after) :])

    return pl.pallas_call(
        body,
        in_specs=[pl.BlockSpec(memory_space=pltpu.SMEM)] * len(scalars)
        + [pl.BlockSpec(memory_space=pltpu.VMEM)] * len(arrays)
        + [pl.BlockSpec(memory_space=pl.ANY)] * len(after),
        out_specs=[pl.BlockSpec(memory_space=pltpu.VMEM)] * len(out_shape),
        out_shape=[
            jax.ShapeDtypeStruct(shape, kind_of)
            for shape, kind_of in zip(out_shape, kinds)
        ],
        compiler_params=pltpu.CompilerParams(vmem_limit_bytes=16 * 2**20),
        cost_estimate=pl.CostEstimate(
            flops=flops, bytes_accessed=2**20, transcendentals=0
        ),
    )(*scalars, *arrays, *after)


def add_kernel(groups, *refs):
    count = len(groups)
    inputs, sums = refs[: -count], refs[-count:]
    for sum_ref, group in zip(sums, groups):
        total = None
        for index, first in group:
            part = inputs[index][pl.ds(first, chip_rows), :].astype(jnp.float32)
            total = part if total is None else total + part
        sum_ref[...] = total.astype(sum_ref.dtype)


def add(groups, after=(), kind=jnp.bfloat16):
    arrays = []
    places = []
    for group in groups:
        place = []
        for part in group:
            array, first = part if isinstance(part, tuple) else (part, 0)
            if not any(array is known for known in arrays):
                arrays.append(array)
            index = [array is known for known in arrays].index(True)
            place.append((index, first))
        places.append(place)
    return call(
        functools.partial(add_kernel, places),
        [(chip_rows, arrays[0].shape[1])] * len(groups),
        (),
        arrays,
        after=after,
        kinds=[kind] * len(groups),
    )


def on_device(image_embeds, text_embeds, log_scale, logit_bias):
    width = image_embeds.shape[1]
    core = lax.axis_index("core")
    first_core = core == 0
    cores = core.astype(jnp.int32).reshape(1)
    give = jnp.where(first_core, text_embeds, image_embeds)
    keep = jnp.where(first_core, image_embeds, text_embeds)
    got = swap(give)
    unit, low, high, raw, factors = call(
        pack_kernel,
        [(chip_rows, width)] + [(rows, width)] * 2 + [(chip_rows, width), (8, 128)],
        (log_scale, logit_bias, cores),
        (keep, got),
        kinds=(jnp.bfloat16,) * 4 + (jnp.float32,),
    )
    left_low, right_high = ring(low, 1), ring(high, -1)
    left = jnp.concatenate([left_low, ring(high, 1)], axis=0)
    right = jnp.concatenate([ring(low, -1), right_high], axis=0)
    across = pair(unit)
    distant = jnp.concatenate([ring(left_low, 1), ring(right_high, -1)], axis=0)
    near = [unit, left, right, across]
    far = [distant, ring(across, 1), ring(across, -1), pair(distant)]
    mine = near + far
    other = [
        swap(unit),
        swap(jnp.concatenate([left, right], axis=0)),
        swap(across),
        swap(distant),
        swap(jnp.concatenate(far[1:3], axis=0)),
        swap(far[3]),
    ]
    near_rows, all_rows = 4 * rows, 8 * rows
    edge = near_rows % chunk
    block = (chip_rows, width)
    share = all_rows * all_rows * width // 5
    (near_weights,) = call(
        functools.partial(near_weights_kernel, (len(mine), 3)),
        [(2, all_rows, near_rows - edge)],
        (cores,),
        (factors, *mine, *other[:3]),
        8 * share,
        (),
    )
    edge_weights, far_weights = call(
        functools.partial(far_weights_kernel, (len(mine), len(other))),
        [(2, all_rows, edge), (2, all_rows, near_rows)],
        (cores,),
        (factors, *mine, *other),
        12 * share,
        (near_weights,),
    )
    far_received = swap(far_weights)
    weights = (near_weights, edge_weights, far_weights)
    near_part, far_part, near_joined = call(
        functools.partial(own_kernel, len(other)),
        [(2, 3 * rows, width), (2, 4 * rows, width), (2, all_rows, near_rows)],
        (cores,),
        (*weights, *other),
        18 * share,
        kinds=(jnp.float32, jnp.float32, jnp.bfloat16),
    )
    near_received = swap(near_joined)
    far_sums = call(
        functools.partial(far_kernel, len(other)),
        [block] * 4,
        (cores,),
        (far_received, far_part, *other),
        10 * share,
    )
    arrived = [ring(far_sums[1], -1), ring(far_sums[2], 1), pair(far_sums[3])]
    near_sums = call(
        functools.partial(near_kernel, len(other)),
        [block] * 3,
        (cores,),
        (near_received, near_part, *other),
        8 * share,
    )
    (distant_total,) = add([(far_sums[0], arrived[2])], (near_sums[0],))
    (own_sum,) = call(
        functools.partial(self_kernel, len(other)),
        [block],
        (cores,),
        (near_received, *weights, *other),
        5 * share,
        (distant_total,),
        (jnp.float32,),
    )
    (across_total,) = add([(near_sums[2], arrived[0], arrived[1])], (own_sum,))
    (own_part,) = add([(own_sum, ring(distant_total, 2))], kind=jnp.float32)
    parts = [
        own_part,
        ring(near_sums[0], -1),
        ring(near_sums[1], 1),
        pair(across_total),
    ]
    (give,) = call(
        functools.partial(final_kernel, 0),
        [(rows, width)],
        (cores,),
        (factors, raw, *parts),
    )
    given = swap(give)
    (keep,) = call(
        functools.partial(final_kernel, 1),
        [(rows, width)],
        (cores,),
        (factors, raw, *parts),
        after=(give,),
    )
    image_grad = jnp.where(first_core, keep, given)
    text_grad = jnp.where(first_core, given, keep)
    return (image_grad, text_grad)


def solution(mesh):
    fine = Mesh(mesh.devices.reshape(extents), axes)
    split = P(axes, None)
    return jax.shard_map(
        on_device,
        mesh=fine,
        in_specs=(split, split, P(), P()),
        out_specs=(split, split),
        check_vma=False,
    )
```

```python
import functools

import jax
import jax.numpy as jnp
from jax import lax
from jax.experimental import pallas as pl
from jax.experimental.pallas import tpu as pltpu
from jax.sharding import Mesh, PartitionSpec as P

norm_eps = 1e-06
log2_e = 1.4426950408889634
axes = ("yh", "z", "x", "yl", "core")
extents = (2, 4, 4, 2, 2)
rows = 160
chip_rows = 2 * rows
chunk = 256


def pairs_of(move):
    pairs = []
    for yh in range(2):
        for z in range(4):
            for x in range(4):
                for yl in range(2):
                    for core in range(2):
                        place = (yh, z, x, yl, core)
                        pairs.append((linear(place), linear(move(*place))))
    return pairs


def linear(place):
    index = 0
    for value, extent in zip(place, extents):
        index = index * extent + value
    return index


def ring_move(steps):
    def move(yh, z, x, yl, core):
        if core == 0:
            return (yh, z, (x + steps) % 4, yl, core)
        return (yh, (z + steps) % 4, x, yl, core)

    return pairs_of(move)


def ring(value, steps):
    return lax.ppermute(value, axes, ring_move(steps))


def pair(value):
    def move(yh, z, x, yl, core):
        if core == 0:
            return (yh, z, x, 1 - yl, core)
        return (1 - yh, z, x, 1 - yl, core)

    return lax.ppermute(value, axes, pairs_of(move))


def swap(value):
    return lax.ppermute(value, "core", [(0, 1), (1, 0)])


def unit_rows(values):
    inverse = lax.rsqrt(jnp.sum(values * values, axis=1, keepdims=True) + norm_eps)
    return values * inverse, inverse


def pack_kernel(scale_ref, bias_ref, core_ref, keep_ref, got_ref, *refs):
    unit_ref, low_ref, high_ref, raw_ref, factors_ref = refs
    first_core = core_ref[0] == 0
    scale = jnp.exp(jnp.full((1, 128), scale_ref[0], jnp.float32))
    factors_ref[0:1, :] = -log2_e * scale
    factors_ref[1:2, :] = jnp.full((1, 128), -log2_e * bias_ref[0], jnp.float32)
    factors_ref[2:3, :] = scale
    keep = keep_ref[...].astype(jnp.float32)
    got = got_ref[...].astype(jnp.float32)
    low = jnp.where(first_core, keep, got)
    high = jnp.where(first_core, got, keep)
    for half, values in enumerate((low, high)):
        place = pl.ds(half * rows, rows)
        unit = unit_rows(values)[0].astype(jnp.bfloat16)
        unit_ref[place, :] = unit
        (low_ref, high_ref)[half][...] = unit
        raw_ref[place, :] = values.astype(jnp.bfloat16)


def stacked(places, begin):
    return jnp.concatenate(
        [ref[pl.ds(first + begin, rows), :] for ref, first in places], axis=0
    )


def places_of(refs):
    return [
        (ref, first) for ref in refs for first in range(0, ref.shape[0], chip_rows)
    ]


def opposite_rows(core, half):
    return pl.multiple_of(jnp.where(core == 0, half, 1 - half) * rows, rows)


def spans(count):
    return [(begin, min(chunk, count - begin)) for begin in range(0, count, chunk)]


def weights_of(factors_ref, mine_rows, other_rows, matched=None):
    blocks = []
    for begin in range(0, mine_rows.shape[0], 2 * rows):
        dots = lax.dot_general(
            mine_rows[begin : begin + 2 * rows],
            other_rows,
            (((1,), (1,)), ((), ())),
            preferred_element_type=jnp.float32,
        )
        power = jnp.exp2(dots * factors_ref[0:1, 0:1] + factors_ref[1:2, 0:1])
        share = pl.reciprocal(1.0 + power, approx=True)
        if matched is not None and begin == 0:
            row = lax.broadcasted_iota(jnp.int32, dots.shape, 0)
            column = lax.broadcasted_iota(jnp.int32, dots.shape, 1)
            own = (row == column) & (row < rows) & matched
            share = jnp.where(own, -power * share, share)
        blocks.append(share.astype(jnp.bfloat16))
    return jnp.concatenate(blocks, axis=0)


def transposed_dot(weights, values):
    return lax.dot_general(
        weights, values, (((0,), (0,)), ((), ())), preferred_element_type=jnp.float32
    )


def store_chips(refs, first, begin, total):
    done = 0
    while done < total.shape[0]:
        chip, offset = divmod(begin + done, rows)
        size = min(rows - offset, total.shape[0] - done)
        ref, base = refs[chip]
        ref[pl.ds(base + first + offset, size), :] = total[done : done + size].astype(
            ref.dtype
        )
        done += size


def near_weights_kernel(pieces, core_ref, factors_ref, *refs):
    mine, other = places_of(refs[: pieces[0]]), places_of(refs[pieces[0] : sum(pieces)])
    near_ref, begun_ref = refs[sum(pieces) :]
    core = core_ref[0]
    count = near_ref.shape[2]
    for half in range(2):
        mine_rows = stacked(mine, half * rows)
        other_rows = stacked(other, opposite_rows(core, half))
        for begin, size in spans(count):
            near_ref[half, :, pl.ds(begin, size)] = weights_of(
                factors_ref,
                mine_rows,
                other_rows[begin : begin + size],
                core == 0 if begin == 0 else None,
            )
        begun_ref[half] = jnp.dot(
            near_ref[half, pl.ds(4 * rows, 4 * rows), :],
            other_rows[:count],
            preferred_element_type=jnp.float32,
        )


def far_weights_kernel(pieces, core_ref, factors_ref, *refs):
    mine, other = places_of(refs[: pieces[0]]), places_of(refs[pieces[0] : sum(pieces)])
    edge_ref, far_ref = refs[sum(pieces) :]
    edge = edge_ref.shape[2]
    first = 4 * rows - edge
    for half in range(2):
        mine_rows = stacked(mine, half * rows)
        other_rows = stacked(other, opposite_rows(core_ref[0], half))
        for begin, size in spans(edge + far_ref.shape[2]):
            start = first + begin
            weights = weights_of(
                factors_ref, mine_rows, other_rows[start : start + size]
            )
            if begin == 0:
                edge_ref[half] = weights[:, :edge]
                far_ref[half, :, pl.ds(0, size - edge)] = weights[:, edge:]
            else:
                far_ref[half, :, pl.ds(begin - edge, size)] = weights


def own_product(half, first, count, weights_refs, other_rows):
    weights = jnp.concatenate(
        [ref[half, pl.ds(first, count), :] for ref in weights_refs], axis=1
    )
    return jnp.dot(weights, other_rows, preferred_element_type=jnp.float32)


def own_kernel(pieces, core_ref, *refs):
    weights_refs, begun_ref, other = refs[:3], refs[3], places_of(refs[4 : 4 + pieces])
    near_ref, far_ref, joined_ref = refs[4 + pieces :]
    count = weights_refs[0].shape[2]
    edge = 4 * rows - weights_refs[1].shape[2]
    for half in range(2):
        other_rows = stacked(other, opposite_rows(core_ref[0], half))
        joined_ref[half, :, pl.ds(0, edge)] = weights_refs[0][half]
        joined_ref[half, :, pl.ds(edge, 4 * rows - edge)] = weights_refs[1][half]
        far_ref[half] = begun_ref[half] + own_product(
            half, 4 * rows, 4 * rows, weights_refs[1:], other_rows[count:]
        )
        near_ref[half] = own_product(half, rows, 3 * rows, weights_refs, other_rows)


def received(core, half, columns, other):
    its_half = jnp.where(core == 0, 1 - half, half)
    other_rows = stacked(other, pl.multiple_of(its_half * rows, rows))
    weights = jnp.concatenate(
        [ref[its_half, :, pl.ds(first, size)] for ref, first, size in columns], axis=1
    )
    return transposed_dot(weights, other_rows)


def far_kernel(pieces, core_ref, weights_ref, part_ref, *refs):
    other, sums = places_of(refs[:pieces]), places_of(refs[pieces:])
    for half in range(2):
        columns = [(weights_ref, 0, 4 * rows)]
        total = part_ref[half] + received(core_ref[0], half, columns, other)
        store_chips(sums, half * rows, 0, total)


def near_kernel(pieces, core_ref, weights_ref, part_ref, *refs):
    other, sums = places_of(refs[:pieces]), places_of(refs[pieces:])
    first = rows // 128 * 128
    columns = [(weights_ref, first, 4 * rows - first)]
    for half in range(2):
        total = received(core_ref[0], half, columns, other)
        total = total[rows - first :] + part_ref[half]
        store_chips(sums, half * rows, 0, total)


def self_kernel(pieces, core_ref, received_ref, *refs):
    weights_refs, other = refs[:3], places_of(refs[3 : 3 + pieces])
    sum_ref = refs[3 + pieces]
    core = core_ref[0]
    for half in range(2):
        other_rows = stacked(other, opposite_rows(core, half))
        total = own_product(half, 0, rows, weights_refs, other_rows)
        total = total + received(core, half, [(received_ref, 0, chunk)], other)[:rows]
        sum_ref[pl.ds(half * rows, rows), :] = total


def final_kernel(kept, core_ref, factors_ref, raw_ref, *refs):
    parts, grad_ref = refs[:-1], refs[-1]
    half = jnp.where(core_ref[0] == 0, 1 - kept, kept)
    place = pl.ds(pl.multiple_of(half * rows, rows), rows)
    unit, inverse = unit_rows(raw_ref[place, :].astype(jnp.float32))
    direction = parts[0][place, :].astype(jnp.float32)
    for part in parts[1:]:
        direction = direction + part[place, :].astype(jnp.float32)
    direction = direction * factors_ref[2:3, 0:1]
    along = jnp.sum(unit * direction, axis=1, keepdims=True)
    grad_ref[...] = (inverse * (direction - unit * along)).astype(jnp.bfloat16)


def call(kernel, out_shape, scalars, arrays, flops=0, after=(), kinds=None):
    kinds = kinds or [jnp.bfloat16] * len(out_shape)
    used = len(scalars) + len(arrays)

    def body(*refs):
        kernel(*refs[:used], *refs[used + len(after) :])

    return pl.pallas_call(
        body,
        in_specs=[pl.BlockSpec(memory_space=pltpu.SMEM)] * len(scalars)
        + [pl.BlockSpec(memory_space=pltpu.VMEM)] * len(arrays)
        + [pl.BlockSpec(memory_space=pl.ANY)] * len(after),
        out_specs=[pl.BlockSpec(memory_space=pltpu.VMEM)] * len(out_shape),
        out_shape=[
            jax.ShapeDtypeStruct(shape, kind_of)
            for shape, kind_of in zip(out_shape, kinds)
        ],
        compiler_params=pltpu.CompilerParams(vmem_limit_bytes=8 * 2**20),
        cost_estimate=pl.CostEstimate(
            flops=flops, bytes_accessed=2**20, transcendentals=0
        ),
    )(*scalars, *arrays, *after)


def add_kernel(groups, *refs):
    count = len(groups)
    inputs, sums = refs[: -count], refs[-count:]
    for sum_ref, group in zip(sums, groups):
        total = None
        for index, first in group:
            part = inputs[index][pl.ds(first, chip_rows), :].astype(jnp.float32)
            total = part if total is None else total + part
        sum_ref[...] = total.astype(sum_ref.dtype)


def add(groups, after=(), kind=jnp.bfloat16):
    arrays = []
    places = []
    for group in groups:
        place = []
        for part in group:
            array, first = part if isinstance(part, tuple) else (part, 0)
            if not any(array is known for known in arrays):
                arrays.append(array)
            index = [array is known for known in arrays].index(True)
            place.append((index, first))
        places.append(place)
    return call(
        functools.partial(add_kernel, places),
        [(chip_rows, arrays[0].shape[1])] * len(groups),
        (),
        arrays,
        after=after,
        kinds=[kind] * len(groups),
    )


def on_device(image_embeds, text_embeds, log_scale, logit_bias):
    width = image_embeds.shape[1]
    core = lax.axis_index("core")
    first_core = core == 0
    cores = core.astype(jnp.int32).reshape(1)
    give = jnp.where(first_core, text_embeds, image_embeds)
    keep = jnp.where(first_core, image_embeds, text_embeds)
    got = swap(give)
    unit, low, high, raw, factors = call(
        pack_kernel,
        [(chip_rows, width)] + [(rows, width)] * 2 + [(chip_rows, width), (8, 128)],
        (log_scale, logit_bias, cores),
        (keep, got),
        kinds=(jnp.bfloat16,) * 4 + (jnp.float32,),
    )
    left_low, right_high = ring(low, 1), ring(high, -1)
    left = jnp.concatenate([left_low, ring(high, 1)], axis=0)
    right = jnp.concatenate([ring(low, -1), right_high], axis=0)
    across = pair(unit)
    distant_low, distant_high = ring(left_low, 1), ring(right_high, -1)
    distant = jnp.concatenate([distant_low, distant_high], axis=0)
    far_distant = jnp.concatenate([pair(distant_low), pair(distant_high)], axis=0)
    near = [unit, left, right, across]
    far = [distant, ring(across, 1), ring(across, -1), far_distant]
    mine = near + far
    other = [
        swap(jnp.concatenate(near, axis=0)),
        swap(jnp.concatenate(far, axis=0)),
    ]
    near_rows, all_rows = 4 * rows, 8 * rows
    edge = near_rows % chunk
    block = (chip_rows, width)
    share = all_rows * all_rows * width // 5
    near_weights, far_begun = call(
        functools.partial(near_weights_kernel, (len(mine), 1)),
        [(2, all_rows, near_rows - edge), (2, near_rows, width)],
        (cores,),
        (factors, *mine, other[0]),
        12 * share,
        kinds=(jnp.bfloat16, jnp.float32),
    )
    edge_weights, far_weights = call(
        functools.partial(far_weights_kernel, (len(mine), len(other))),
        [(2, all_rows, edge), (2, all_rows, near_rows)],
        (cores,),
        (factors, *mine, *other),
        12 * share,
        (near_weights,),
    )
    far_received = swap(far_weights)
    weights = (near_weights, edge_weights, far_weights)
    near_part, far_part, near_joined = call(
        functools.partial(own_kernel, len(other)),
        [(2, 3 * rows, width), (2, 4 * rows, width), (2, all_rows, near_rows)],
        (cores,),
        (*weights, far_begun, *other),
        14 * share,
        kinds=(jnp.float32, jnp.float32, jnp.bfloat16),
    )
    near_received = swap(near_joined)
    far_sums = call(
        functools.partial(far_kernel, len(other)),
        [block] * 4,
        (cores,),
        (far_received, far_part, *other),
        10 * share,
    )
    arrived = [ring(far_sums[1], -1), ring(far_sums[2], 1), pair(far_sums[3])]
    near_sums = call(
        functools.partial(near_kernel, len(other)),
        [block] * 3,
        (cores,),
        (near_received, near_part, *other),
        8 * share,
    )
    (distant_total,) = add([(far_sums[0], arrived[2])], (near_sums[0],))
    (own_sum,) = call(
        functools.partial(self_kernel, len(other)),
        [block],
        (cores,),
        (near_received, *weights, *other),
        5 * share,
        (distant_total,),
        (jnp.float32,),
    )
    (across_total,) = add([(near_sums[2], arrived[0], arrived[1])], (own_sum,))
    (own_part,) = add([(own_sum, ring(distant_total, 2))], kind=jnp.float32)
    parts = [
        own_part,
        ring(near_sums[0], -1),
        ring(near_sums[1], 1),
        pair(across_total),
    ]
    (give,) = call(
        functools.partial(final_kernel, 0),
        [(rows, width)],
        (cores,),
        (factors, raw, *parts),
    )
    given = swap(give)
    (keep,) = call(
        functools.partial(final_kernel, 1),
        [(rows, width)],
        (cores,),
        (factors, raw, *parts),
        after=(give,),
    )
    image_grad = jnp.where(first_core, keep, given)
    text_grad = jnp.where(first_core, given, keep)
    return (image_grad, text_grad)


def solution(mesh):
    fine = Mesh(mesh.devices.reshape(extents), axes)
    split = P(axes, None)
    return jax.shard_map(
        on_device,
        mesh=fine,
        in_specs=(split, split, P(), P()),
        out_specs=(split, split),
        check_vma=False,
    )
```

```python
import functools

import jax
import jax.numpy as jnp
from jax import lax
from jax.experimental import pallas as pl
from jax.experimental.pallas import tpu as pltpu
from jax.sharding import Mesh, PartitionSpec as P

norm_eps = 1e-06
log2_e = 1.4426950408889634
axes = ("yh", "z", "x", "yl", "core")
extents = (2, 4, 4, 2, 2)
rows = 160
chip_rows = 2 * rows
chunk = 256


def pairs_of(move):
    pairs = []
    for yh in range(2):
        for z in range(4):
            for x in range(4):
                for yl in range(2):
                    for core in range(2):
                        place = (yh, z, x, yl, core)
                        pairs.append((linear(place), linear(move(*place))))
    return pairs


def linear(place):
    index = 0
    for value, extent in zip(place, extents):
        index = index * extent + value
    return index


def ring_move(steps):
    def move(yh, z, x, yl, core):
        if core == 0:
            return (yh, z, (x + steps) % 4, yl, core)
        return (yh, (z + steps) % 4, x, yl, core)

    return pairs_of(move)


def ring(value, steps):
    return lax.ppermute(value, axes, ring_move(steps))


def pair(value):
    def move(yh, z, x, yl, core):
        if core == 0:
            return (yh, z, x, 1 - yl, core)
        return (1 - yh, z, x, 1 - yl, core)

    return lax.ppermute(value, axes, pairs_of(move))


def swap(value):
    return lax.ppermute(value, "core", [(0, 1), (1, 0)])


def unit_rows(values):
    inverse = lax.rsqrt(jnp.sum(values * values, axis=1, keepdims=True) + norm_eps)
    return values * inverse, inverse


def pack_kernel(scale_ref, bias_ref, core_ref, keep_ref, got_ref, *refs):
    unit_ref, low_ref, high_ref, raw_ref, factors_ref = refs
    first_core = core_ref[0] == 0
    scale = jnp.exp(jnp.full((1, 128), scale_ref[0], jnp.float32))
    factors_ref[0:1, :] = -log2_e * scale
    factors_ref[1:2, :] = jnp.full((1, 128), -log2_e * bias_ref[0], jnp.float32)
    factors_ref[2:3, :] = scale
    keep = keep_ref[...].astype(jnp.float32)
    got = got_ref[...].astype(jnp.float32)
    low = jnp.where(first_core, keep, got)
    high = jnp.where(first_core, got, keep)
    for half, values in enumerate((low, high)):
        place = pl.ds(half * rows, rows)
        unit = unit_rows(values)[0].astype(jnp.bfloat16)
        unit_ref[place, :] = unit
        (low_ref, high_ref)[half][...] = unit
        raw_ref[place, :] = values.astype(jnp.bfloat16)


def stacked(places, begin):
    return jnp.concatenate(
        [ref[pl.ds(first + begin, rows), :] for ref, first in places], axis=0
    )


def places_of(refs):
    return [
        (ref, first) for ref in refs for first in range(0, ref.shape[0], chip_rows)
    ]


def opposite_rows(core, half):
    return pl.multiple_of(jnp.where(core == 0, half, 1 - half) * rows, rows)


def spans(count):
    return [(begin, min(chunk, count - begin)) for begin in range(0, count, chunk)]


def weights_of(factors_ref, mine_rows, other_rows, matched=None):
    blocks = []
    for begin in range(0, mine_rows.shape[0], 2 * rows):
        dots = lax.dot_general(
            mine_rows[begin : begin + 2 * rows],
            other_rows,
            (((1,), (1,)), ((), ())),
            preferred_element_type=jnp.float32,
        )
        power = jnp.exp2(dots * factors_ref[0:1, 0:1] + factors_ref[1:2, 0:1])
        share = pl.reciprocal(1.0 + power, approx=True)
        if matched is not None and begin == 0:
            row = lax.broadcasted_iota(jnp.int32, dots.shape, 0)
            column = lax.broadcasted_iota(jnp.int32, dots.shape, 1)
            own = (row == column) & (row < rows) & matched
            share = jnp.where(own, -power * share, share)
        blocks.append(share.astype(jnp.bfloat16))
    return jnp.concatenate(blocks, axis=0)


def transposed_dot(weights, values):
    return lax.dot_general(
        weights, values, (((0,), (0,)), ((), ())), preferred_element_type=jnp.float32
    )


def store_chips(refs, first, begin, total):
    done = 0
    while done < total.shape[0]:
        chip, offset = divmod(begin + done, rows)
        size = min(rows - offset, total.shape[0] - done)
        ref, base = refs[chip]
        ref[pl.ds(base + first + offset, size), :] = total[done : done + size].astype(
            ref.dtype
        )
        done += size


def near_weights_kernel(pieces, core_ref, factors_ref, *refs):
    mine, other = places_of(refs[: pieces[0]]), places_of(refs[pieces[0] : sum(pieces)])
    near_ref, begun_ref = refs[sum(pieces) :]
    core = core_ref[0]
    count = near_ref.shape[2]
    for half in range(2):
        mine_rows = stacked(mine, half * rows)
        other_rows = stacked(other, opposite_rows(core, half))
        for begin, size in spans(count):
            near_ref[half, :, pl.ds(begin, size)] = weights_of(
                factors_ref,
                mine_rows,
                other_rows[begin : begin + size],
                core == 0 if begin == 0 else None,
            )
        begun_ref[half] = jnp.dot(
            near_ref[half, pl.ds(4 * rows, 4 * rows), :],
            other_rows[:count],
            preferred_element_type=jnp.float32,
        )


def far_weights_kernel(pieces, core_ref, factors_ref, *refs):
    mine, other = places_of(refs[: pieces[0]]), places_of(refs[pieces[0] : sum(pieces)])
    edge_ref, far_ref = refs[sum(pieces) :]
    edge = edge_ref.shape[2]
    first = 4 * rows - edge
    for half in range(2):
        mine_rows = stacked(mine, half * rows)
        other_rows = stacked(other, opposite_rows(core_ref[0], half))
        for begin, size in spans(edge + far_ref.shape[2]):
            start = first + begin
            weights = weights_of(
                factors_ref, mine_rows, other_rows[start : start + size]
            )
            if begin == 0:
                edge_ref[half] = weights[:, :edge]
                far_ref[half, :, pl.ds(0, size - edge)] = weights[:, edge:]
            else:
                far_ref[half, :, pl.ds(begin - edge, size)] = weights


def own_product(half, first, count, weights_refs, other_rows):
    weights = jnp.concatenate(
        [ref[half, pl.ds(first, count), :] for ref in weights_refs], axis=1
    )
    return jnp.dot(weights, other_rows, preferred_element_type=jnp.float32)


def own_kernel(pieces, core_ref, *refs):
    weights_refs, begun_ref, other = refs[:3], refs[3], places_of(refs[4 : 4 + pieces])
    near_ref, far_ref, joined_ref = refs[4 + pieces :]
    count = weights_refs[0].shape[2]
    edge = 4 * rows - weights_refs[1].shape[2]
    for half in range(2):
        other_rows = stacked(other, opposite_rows(core_ref[0], half))
        joined_ref[half, :, pl.ds(0, edge)] = weights_refs[0][half]
        joined_ref[half, :, pl.ds(edge, 4 * rows - edge)] = weights_refs[1][half]
        far_ref[half] = begun_ref[half] + own_product(
            half, 4 * rows, 4 * rows, weights_refs[1:], other_rows[count:]
        )
        near_ref[half] = own_product(half, rows, 3 * rows, weights_refs, other_rows)


def received(core, half, columns, other):
    its_half = jnp.where(core == 0, 1 - half, half)
    other_rows = stacked(other, pl.multiple_of(its_half * rows, rows))
    weights = jnp.concatenate(
        [ref[its_half, :, pl.ds(first, size)] for ref, first, size in columns], axis=1
    )
    return transposed_dot(weights, other_rows)


def far_kernel(pieces, core_ref, weights_ref, part_ref, *refs):
    other, sums = places_of(refs[:pieces]), places_of(refs[pieces:])
    for half in range(2):
        columns = [(weights_ref, 0, 4 * rows)]
        total = part_ref[half] + received(core_ref[0], half, columns, other)
        store_chips(sums, half * rows, 0, total)


def near_kernel(pieces, core_ref, weights_ref, part_ref, *refs):
    other, sums = places_of(refs[:pieces]), places_of(refs[pieces:])
    first = rows // 128 * 128
    columns = [(weights_ref, first, 4 * rows - first)]
    for half in range(2):
        total = received(core_ref[0], half, columns, other)
        total = total[rows - first :] + part_ref[half]
        store_chips(sums, half * rows, 0, total)


def self_kernel(pieces, core_ref, received_ref, *refs):
    weights_refs, other = refs[:3], places_of(refs[3 : 3 + pieces])
    sum_ref = refs[3 + pieces]
    core = core_ref[0]
    for half in range(2):
        other_rows = stacked(other, opposite_rows(core, half))
        total = own_product(half, 0, rows, weights_refs, other_rows)
        total = total + received(core, half, [(received_ref, 0, chunk)], other)[:rows]
        sum_ref[pl.ds(half * rows, rows), :] = total


def final_kernel(kept, core_ref, factors_ref, raw_ref, *refs):
    parts, grad_ref = refs[:-1], refs[-1]
    half = jnp.where(core_ref[0] == 0, 1 - kept, kept)
    place = pl.ds(pl.multiple_of(half * rows, rows), rows)
    unit, inverse = unit_rows(raw_ref[place, :].astype(jnp.float32))
    direction = parts[0][place, :].astype(jnp.float32)
    for part in parts[1:]:
        direction = direction + part[place, :].astype(jnp.float32)
    direction = direction * factors_ref[2:3, 0:1]
    along = jnp.sum(unit * direction, axis=1, keepdims=True)
    grad_ref[...] = (inverse * (direction - unit * along)).astype(jnp.bfloat16)


def call(kernel, out_shape, scalars, arrays, flops=0, after=(), kinds=None):
    kinds = kinds or [jnp.bfloat16] * len(out_shape)
    used = len(scalars) + len(arrays)

    def body(*refs):
        kernel(*refs[:used], *refs[used + len(after) :])

    return pl.pallas_call(
        body,
        in_specs=[pl.BlockSpec(memory_space=pltpu.SMEM)] * len(scalars)
        + [pl.BlockSpec(memory_space=pltpu.VMEM)] * len(arrays)
        + [pl.BlockSpec(memory_space=pl.ANY)] * len(after),
        out_specs=[pl.BlockSpec(memory_space=pltpu.VMEM)] * len(out_shape),
        out_shape=[
            jax.ShapeDtypeStruct(shape, kind_of)
            for shape, kind_of in zip(out_shape, kinds)
        ],
        compiler_params=pltpu.CompilerParams(vmem_limit_bytes=8 * 2**20),
        cost_estimate=pl.CostEstimate(
            flops=flops, bytes_accessed=2**20, transcendentals=0
        ),
    )(*scalars, *arrays, *after)


def add_kernel(groups, *refs):
    count = len(groups)
    inputs, sums = refs[: -count], refs[-count:]
    for sum_ref, group in zip(sums, groups):
        total = None
        for index, first in group:
            part = inputs[index][pl.ds(first, chip_rows), :].astype(jnp.float32)
            total = part if total is None else total + part
        sum_ref[...] = total.astype(sum_ref.dtype)


def add(groups, after=(), kind=jnp.bfloat16):
    arrays = []
    places = []
    for group in groups:
        place = []
        for part in group:
            array, first = part if isinstance(part, tuple) else (part, 0)
            if not any(array is known for known in arrays):
                arrays.append(array)
            index = [array is known for known in arrays].index(True)
            place.append((index, first))
        places.append(place)
    return call(
        functools.partial(add_kernel, places),
        [(chip_rows, arrays[0].shape[1])] * len(groups),
        (),
        arrays,
        after=after,
        kinds=[kind] * len(groups),
    )


def on_device(image_embeds, text_embeds, log_scale, logit_bias):
    width = image_embeds.shape[1]
    core = lax.axis_index("core")
    first_core = core == 0
    cores = core.astype(jnp.int32).reshape(1)
    give = jnp.where(first_core, text_embeds, image_embeds)
    keep = jnp.where(first_core, image_embeds, text_embeds)
    got = swap(give)
    unit, low, high, raw, factors = call(
        pack_kernel,
        [(chip_rows, width)] + [(rows, width)] * 2 + [(chip_rows, width), (8, 128)],
        (log_scale, logit_bias, cores),
        (keep, got),
        kinds=(jnp.bfloat16,) * 4 + (jnp.float32,),
    )
    across = pair(unit)
    left_low, right_high = ring(low, 1), ring(high, -1)
    late_high, late_low, _ = lax.optimization_barrier((high, low, left_low[:8]))
    left_high, right_low = ring(late_high, 1), ring(late_low, -1)
    distant_low, distant_high = ring(left_low, 1), ring(right_high, -1)
    far_left, far_right = ring(across, 1), ring(across, -1)
    low_far, high_far = pair(distant_low), pair(distant_high)
    left = jnp.concatenate([left_low, left_high], axis=0)
    right = jnp.concatenate([right_low, right_high], axis=0)
    distant = jnp.concatenate([distant_low, distant_high], axis=0)
    far_distant = jnp.concatenate([low_far, high_far], axis=0)
    near = [unit, left, right, across]
    far = [distant, far_left, far_right, far_distant]
    mine = near + far
    other = [
        swap(jnp.concatenate(near, axis=0)),
        swap(jnp.concatenate(far, axis=0)),
    ]
    near_rows, all_rows = 4 * rows, 8 * rows
    edge = near_rows % chunk
    block = (chip_rows, width)
    share = all_rows * all_rows * width // 5
    near_weights, far_begun = call(
        functools.partial(near_weights_kernel, (len(mine), 1)),
        [(2, all_rows, near_rows - edge), (2, near_rows, width)],
        (cores,),
        (factors, *mine, other[0]),
        12 * share,
        kinds=(jnp.bfloat16, jnp.float32),
    )
    edge_weights, far_weights = call(
        functools.partial(far_weights_kernel, (len(mine), len(other))),
        [(2, all_rows, edge), (2, all_rows, near_rows)],
        (cores,),
        (factors, *mine, *other),
        12 * share,
        (near_weights,),
    )
    far_received = swap(far_weights)
    weights = (near_weights, edge_weights, far_weights)
    near_part, far_part, near_joined = call(
        functools.partial(own_kernel, len(other)),
        [(2, 3 * rows, width), (2, 4 * rows, width), (2, all_rows, near_rows)],
        (cores,),
        (*weights, far_begun, *other),
        14 * share,
        kinds=(jnp.float32, jnp.float32, jnp.bfloat16),
    )
    near_received = swap(near_joined)
    far_sums = call(
        functools.partial(far_kernel, len(other)),
        [block] * 4,
        (cores,),
        (far_received, far_part, *other),
        10 * share,
    )
    arrived = [ring(far_sums[1], -1), ring(far_sums[2], 1), pair(far_sums[3])]
    near_sums = call(
        functools.partial(near_kernel, len(other)),
        [block] * 3,
        (cores,),
        (near_received, near_part, *other),
        8 * share,
    )
    (distant_total,) = add([(far_sums[0], arrived[2])], (near_sums[0],))
    (own_sum,) = call(
        functools.partial(self_kernel, len(other)),
        [block],
        (cores,),
        (near_received, *weights, *other),
        5 * share,
        (distant_total,),
        (jnp.float32,),
    )
    (across_total,) = add([(near_sums[2], arrived[0], arrived[1])], (own_sum,))
    (own_part,) = add([(own_sum, ring(distant_total, 2))], kind=jnp.float32)
    parts = [
        own_part,
        ring(near_sums[0], -1),
        ring(near_sums[1], 1),
        pair(across_total),
    ]
    (give,) = call(
        functools.partial(final_kernel, 0),
        [(rows, width)],
        (cores,),
        (factors, raw, *parts),
    )
    given = swap(give)
    (keep,) = call(
        functools.partial(final_kernel, 1),
        [(rows, width)],
        (cores,),
        (factors, raw, *parts),
        after=(give,),
    )
    image_grad = jnp.where(first_core, keep, given)
    text_grad = jnp.where(first_core, given, keep)
    return (image_grad, text_grad)


def solution(mesh):
    fine = Mesh(mesh.devices.reshape(extents), axes)
    split = P(axes, None)
    return jax.shard_map(
        on_device,
        mesh=fine,
        in_specs=(split, split, P(), P()),
        out_specs=(split, split),
        check_vma=False,
    )
```

```python
import functools

import jax
import jax.numpy as jnp
from jax import lax
from jax.experimental import pallas as pl
from jax.experimental.pallas import tpu as pltpu
from jax.sharding import Mesh, PartitionSpec as P

norm_eps = 1e-06
log2_e = 1.4426950408889634
axes = ("yh", "z", "x", "yl", "core")
extents = (2, 4, 4, 2, 2)
rows = 160
chip_rows = 2 * rows
chunk = 256


def pairs_of(move):
    pairs = []
    for yh in range(2):
        for z in range(4):
            for x in range(4):
                for yl in range(2):
                    for core in range(2):
                        place = (yh, z, x, yl, core)
                        pairs.append((linear(place), linear(move(*place))))
    return pairs


def linear(place):
    index = 0
    for value, extent in zip(place, extents):
        index = index * extent + value
    return index


def ring_move(steps):
    def move(yh, z, x, yl, core):
        if core == 0:
            return (yh, z, (x + steps) % 4, yl, core)
        return (yh, (z + steps) % 4, x, yl, core)

    return pairs_of(move)


def ring(value, steps):
    return lax.ppermute(value, axes, ring_move(steps))


def pair(value):
    def move(yh, z, x, yl, core):
        if core == 0:
            return (yh, z, x, 1 - yl, core)
        return (1 - yh, z, x, 1 - yl, core)

    return lax.ppermute(value, axes, pairs_of(move))


def swap(value):
    return lax.ppermute(value, "core", [(0, 1), (1, 0)])


def unit_rows(values):
    inverse = lax.rsqrt(jnp.sum(values * values, axis=1, keepdims=True) + norm_eps)
    return values * inverse, inverse


def pack_kernel(scale_ref, bias_ref, core_ref, keep_ref, got_ref, *refs):
    unit_ref, low_ref, high_ref, raw_ref, factors_ref = refs
    first_core = core_ref[0] == 0
    scale = jnp.exp(jnp.full((1, 128), scale_ref[0], jnp.float32))
    factors_ref[0:1, :] = -log2_e * scale
    factors_ref[1:2, :] = jnp.full((1, 128), -log2_e * bias_ref[0], jnp.float32)
    factors_ref[2:3, :] = scale
    keep = keep_ref[...].astype(jnp.float32)
    got = got_ref[...].astype(jnp.float32)
    low = jnp.where(first_core, keep, got)
    high = jnp.where(first_core, got, keep)
    for half, values in enumerate((low, high)):
        place = pl.ds(half * rows, rows)
        unit = unit_rows(values)[0].astype(jnp.bfloat16)
        unit_ref[place, :] = unit
        (low_ref, high_ref)[half][...] = unit
        raw_ref[place, :] = values.astype(jnp.bfloat16)


def stacked(places, begin):
    return jnp.concatenate(
        [ref[pl.ds(first + begin, rows), :] for ref, first in places], axis=0
    )


def places_of(refs):
    return [
        (ref, first) for ref in refs for first in range(0, ref.shape[0], chip_rows)
    ]


def opposite_rows(core, half):
    return pl.multiple_of(jnp.where(core == 0, half, 1 - half) * rows, rows)


def spans(count):
    return [(begin, min(chunk, count - begin)) for begin in range(0, count, chunk)]


def weights_of(factors_ref, mine_rows, other_rows, matched=None):
    blocks = []
    for begin in range(0, mine_rows.shape[0], 2 * rows):
        dots = lax.dot_general(
            mine_rows[begin : begin + 2 * rows],
            other_rows,
            (((1,), (1,)), ((), ())),
            preferred_element_type=jnp.float32,
        )
        power = jnp.exp2(dots * factors_ref[0:1, 0:1] + factors_ref[1:2, 0:1])
        share = pl.reciprocal(1.0 + power, approx=True)
        if matched is not None and begin == 0:
            row = lax.broadcasted_iota(jnp.int32, dots.shape, 0)
            column = lax.broadcasted_iota(jnp.int32, dots.shape, 1)
            own = (row == column) & (row < rows) & matched
            share = jnp.where(own, -power * share, share)
        blocks.append(share.astype(jnp.bfloat16))
    return jnp.concatenate(blocks, axis=0)


def transposed_dot(weights, values):
    return lax.dot_general(
        weights, values, (((0,), (0,)), ((), ())), preferred_element_type=jnp.float32
    )


def store_chips(refs, first, begin, total):
    done = 0
    while done < total.shape[0]:
        chip, offset = divmod(begin + done, rows)
        size = min(rows - offset, total.shape[0] - done)
        ref, base = refs[chip]
        ref[pl.ds(base + first + offset, size), :] = total[done : done + size].astype(
            ref.dtype
        )
        done += size


def near_weights_kernel(pieces, core_ref, factors_ref, *refs):
    mine, other = places_of(refs[: pieces[0]]), places_of(refs[pieces[0] : sum(pieces)])
    near_ref, begun_ref = refs[sum(pieces) :]
    core = core_ref[0]
    count = near_ref.shape[2]
    for half in range(2):
        mine_rows = stacked(mine, half * rows)
        other_rows = stacked(other, opposite_rows(core, half))
        for begin, size in spans(count):
            near_ref[half, :, pl.ds(begin, size)] = weights_of(
                factors_ref,
                mine_rows,
                other_rows[begin : begin + size],
                core == 0 if begin == 0 else None,
            )
        begun_ref[half] = jnp.dot(
            near_ref[half, pl.ds(4 * rows, 4 * rows), :],
            other_rows[:count],
            preferred_element_type=jnp.float32,
        )


def far_weights_kernel(pieces, core_ref, factors_ref, *refs):
    mine, other = places_of(refs[: pieces[0]]), places_of(refs[pieces[0] : sum(pieces)])
    edge_ref, far_ref = refs[sum(pieces) :]
    edge = edge_ref.shape[2]
    first = 4 * rows - edge
    for half in range(2):
        mine_rows = stacked(mine, half * rows)
        other_rows = stacked(other, opposite_rows(core_ref[0], half))
        for begin, size in spans(edge + far_ref.shape[2]):
            start = first + begin
            weights = weights_of(
                factors_ref, mine_rows, other_rows[start : start + size]
            )
            if begin == 0:
                edge_ref[half] = weights[:, :edge]
                far_ref[half, :, pl.ds(0, size - edge)] = weights[:, edge:]
            else:
                far_ref[half, :, pl.ds(begin - edge, size)] = weights


def own_product(half, first, count, weights_refs, other_rows):
    weights = jnp.concatenate(
        [ref[half, pl.ds(first, count), :] for ref in weights_refs], axis=1
    )
    return jnp.dot(weights, other_rows, preferred_element_type=jnp.float32)


def own_kernel(pieces, core_ref, *refs):
    weights_refs, begun_ref, other = refs[:3], refs[3], places_of(refs[4 : 4 + pieces])
    near_ref, far_ref, joined_ref = refs[4 + pieces :]
    count = weights_refs[0].shape[2]
    edge = 4 * rows - weights_refs[1].shape[2]
    for half in range(2):
        other_rows = stacked(other, opposite_rows(core_ref[0], half))
        joined_ref[half, :, pl.ds(0, edge)] = weights_refs[0][half]
        joined_ref[half, :, pl.ds(edge, 4 * rows - edge)] = weights_refs[1][half]
        far_ref[half] = begun_ref[half] + own_product(
            half, 4 * rows, 4 * rows, weights_refs[1:], other_rows[count:]
        )
        near_ref[half] = own_product(half, rows, 3 * rows, weights_refs, other_rows)


def received(core, half, columns, other):
    its_half = jnp.where(core == 0, 1 - half, half)
    other_rows = stacked(other, pl.multiple_of(its_half * rows, rows))
    weights = jnp.concatenate(
        [ref[its_half, :, pl.ds(first, size)] for ref, first, size in columns], axis=1
    )
    return transposed_dot(weights, other_rows)


def far_kernel(pieces, core_ref, weights_ref, part_ref, *refs):
    other, sums = places_of(refs[:pieces]), places_of(refs[pieces:])
    for half in range(2):
        columns = [(weights_ref, 0, 4 * rows)]
        total = part_ref[half] + received(core_ref[0], half, columns, other)
        store_chips(sums, half * rows, 0, total)


def near_kernel(pieces, core_ref, weights_ref, part_ref, *refs):
    other, sums = places_of(refs[:pieces]), places_of(refs[pieces:])
    first = rows // 128 * 128
    columns = [(weights_ref, first, 4 * rows - first)]
    for half in range(2):
        total = received(core_ref[0], half, columns, other)
        total = total[rows - first :] + part_ref[half]
        store_chips(sums, half * rows, 0, total)


def self_kernel(pieces, core_ref, received_ref, *refs):
    weights_refs, other = refs[:3], places_of(refs[3 : 3 + pieces])
    sum_ref = refs[3 + pieces]
    core = core_ref[0]
    for half in range(2):
        other_rows = stacked(other, opposite_rows(core, half))
        total = own_product(half, 0, rows, weights_refs, other_rows)
        total = total + received(core, half, [(received_ref, 0, chunk)], other)[:rows]
        sum_ref[pl.ds(half * rows, rows), :] = total


def final_kernel(kept, core_ref, factors_ref, raw_ref, *refs):
    parts, grad_ref = refs[:-1], refs[-1]
    half = jnp.where(core_ref[0] == 0, 1 - kept, kept)
    place = pl.ds(pl.multiple_of(half * rows, rows), rows)
    unit, inverse = unit_rows(raw_ref[place, :].astype(jnp.float32))
    direction = parts[0][place, :].astype(jnp.float32)
    for part in parts[1:]:
        direction = direction + part[place, :].astype(jnp.float32)
    direction = direction * factors_ref[2:3, 0:1]
    along = jnp.sum(unit * direction, axis=1, keepdims=True)
    grad_ref[...] = (inverse * (direction - unit * along)).astype(jnp.bfloat16)


def call(kernel, out_shape, scalars, arrays, flops=0, after=(), kinds=None):
    kinds = kinds or [jnp.bfloat16] * len(out_shape)
    used = len(scalars) + len(arrays)

    def body(*refs):
        kernel(*refs[:used], *refs[used + len(after) :])

    return pl.pallas_call(
        body,
        in_specs=[pl.BlockSpec(memory_space=pltpu.SMEM)] * len(scalars)
        + [pl.BlockSpec(memory_space=pltpu.VMEM)] * len(arrays)
        + [pl.BlockSpec(memory_space=pl.ANY)] * len(after),
        out_specs=[pl.BlockSpec(memory_space=pltpu.VMEM)] * len(out_shape),
        out_shape=[
            jax.ShapeDtypeStruct(shape, kind_of)
            for shape, kind_of in zip(out_shape, kinds)
        ],
        compiler_params=pltpu.CompilerParams(vmem_limit_bytes=8 * 2**20),
        cost_estimate=pl.CostEstimate(
            flops=flops, bytes_accessed=2**20, transcendentals=0
        ),
    )(*scalars, *arrays, *after)


def add_kernel(groups, *refs):
    count = len(groups)
    inputs, sums = refs[: -count], refs[-count:]
    for sum_ref, group in zip(sums, groups):
        total = None
        for index, first in group:
            part = inputs[index][pl.ds(first, chip_rows), :].astype(jnp.float32)
            total = part if total is None else total + part
        sum_ref[...] = total.astype(sum_ref.dtype)


def add(groups, after=(), kind=jnp.bfloat16):
    arrays = []
    places = []
    for group in groups:
        place = []
        for part in group:
            array, first = part if isinstance(part, tuple) else (part, 0)
            if not any(array is known for known in arrays):
                arrays.append(array)
            index = [array is known for known in arrays].index(True)
            place.append((index, first))
        places.append(place)
    return call(
        functools.partial(add_kernel, places),
        [(chip_rows, arrays[0].shape[1])] * len(groups),
        (),
        arrays,
        after=after,
        kinds=[kind] * len(groups),
    )


def on_device(image_embeds, text_embeds, log_scale, logit_bias):
    width = image_embeds.shape[1]
    core = lax.axis_index("core")
    first_core = core == 0
    cores = core.astype(jnp.int32).reshape(1)
    give = jnp.where(first_core, text_embeds, image_embeds)
    first_image, first_text = lax.optimization_barrier((image_embeds, text_embeds))
    keep = jnp.where(first_core, first_image, first_text)
    got = swap(give)
    unit, low, high, raw, factors = call(
        pack_kernel,
        [(chip_rows, width)] + [(rows, width)] * 2 + [(chip_rows, width), (8, 128)],
        (log_scale, logit_bias, cores),
        (keep, got),
        kinds=(jnp.bfloat16,) * 4 + (jnp.float32,),
    )
    across = pair(unit)
    left_low, right_high = ring(low, 1), ring(high, -1)
    late_high, late_low, _ = lax.optimization_barrier((high, low, left_low[:8]))
    left_high, right_low = ring(late_high, 1), ring(late_low, -1)
    distant_low, distant_high = ring(left_low, 1), ring(right_high, -1)
    far_left, far_right = ring(across, 1), ring(across, -1)
    low_far, high_far = pair(distant_low), pair(distant_high)
    left = jnp.concatenate([left_low, left_high], axis=0)
    right = jnp.concatenate([right_low, right_high], axis=0)
    distant = jnp.concatenate([distant_low, distant_high], axis=0)
    far_distant = jnp.concatenate([low_far, high_far], axis=0)
    near = [unit, left, right, across]
    far = [distant, far_left, far_right, far_distant]
    mine = near + far
    other = [
        swap(jnp.concatenate(near, axis=0)),
        swap(jnp.concatenate(far, axis=0)),
    ]
    near_rows, all_rows = 4 * rows, 8 * rows
    edge = near_rows % chunk
    block = (chip_rows, width)
    share = all_rows * all_rows * width // 5
    near_weights, far_begun = call(
        functools.partial(near_weights_kernel, (len(mine), 1)),
        [(2, all_rows, near_rows - edge), (2, near_rows, width)],
        (cores,),
        (factors, *mine, other[0]),
        12 * share,
        kinds=(jnp.bfloat16, jnp.float32),
    )
    edge_weights, far_weights = call(
        functools.partial(far_weights_kernel, (len(mine), len(other))),
        [(2, all_rows, edge), (2, all_rows, near_rows)],
        (cores,),
        (factors, *mine, *other),
        12 * share,
        (near_weights,),
    )
    far_received = swap(far_weights)
    weights = (near_weights, edge_weights, far_weights)
    near_part, far_part, near_joined = call(
        functools.partial(own_kernel, len(other)),
        [(2, 3 * rows, width), (2, 4 * rows, width), (2, all_rows, near_rows)],
        (cores,),
        (*weights, far_begun, *other),
        14 * share,
        kinds=(jnp.float32, jnp.float32, jnp.bfloat16),
    )
    near_received = swap(near_joined)
    far_sums = call(
        functools.partial(far_kernel, len(other)),
        [block] * 4,
        (cores,),
        (far_received, far_part, *other),
        10 * share,
    )
    arrived = [ring(far_sums[1], -1), ring(far_sums[2], 1), pair(far_sums[3])]
    near_sums = call(
        functools.partial(near_kernel, len(other)),
        [block] * 3,
        (cores,),
        (near_received, near_part, *other),
        8 * share,
    )
    (across_total,) = add([(near_sums[2], arrived[0], arrived[1])], (near_sums[0],))
    (distant_total,) = add([(far_sums[0], arrived[2])], (across_total,))
    (own_sum,) = call(
        functools.partial(self_kernel, len(other)),
        [block],
        (cores,),
        (near_received, *weights, *other),
        5 * share,
        (distant_total,),
        (jnp.float32,),
    )
    parts = [
        own_sum,
        ring(distant_total, 2),
        ring(near_sums[0], -1),
        ring(near_sums[1], 1),
        pair(across_total),
    ]
    (give,) = call(
        functools.partial(final_kernel, 0),
        [(rows, width)],
        (cores,),
        (factors, raw, *parts),
    )
    given = swap(give)
    (keep,) = call(
        functools.partial(final_kernel, 1),
        [(rows, width)],
        (cores,),
        (factors, raw, *parts),
        after=(give,),
    )
    image_grad = jnp.where(first_core, keep, given)
    text_grad = jnp.where(first_core, given, keep)
    return (image_grad, text_grad)


def solution(mesh):
    fine = Mesh(mesh.devices.reshape(extents), axes)
    split = P(axes, None)
    return jax.shard_map(
        on_device,
        mesh=fine,
        in_specs=(split, split, P(), P()),
        out_specs=(split, split),
        check_vma=False,
    )
```

```python
import functools

import jax
import jax.numpy as jnp
from jax import lax
from jax.experimental import pallas as pl
from jax.experimental.pallas import tpu as pltpu
from jax.sharding import Mesh, PartitionSpec as P

norm_eps = 1e-06
log2_e = 1.4426950408889634
axes = ("yh", "z", "x", "yl", "core")
extents = (2, 4, 4, 2, 2)
rows = 160
chip_rows = 2 * rows
chunk = 256


def pairs_of(move):
    pairs = []
    for yh in range(2):
        for z in range(4):
            for x in range(4):
                for yl in range(2):
                    for core in range(2):
                        place = (yh, z, x, yl, core)
                        pairs.append((linear(place), linear(move(*place))))
    return pairs


def linear(place):
    index = 0
    for value, extent in zip(place, extents):
        index = index * extent + value
    return index


def ring_move(steps):
    def move(yh, z, x, yl, core):
        if core == 0:
            return (yh, z, (x + steps) % 4, yl, core)
        return (yh, (z + steps) % 4, x, yl, core)

    return pairs_of(move)


def ring(value, steps):
    return lax.ppermute(value, axes, ring_move(steps))


def pair(value):
    def move(yh, z, x, yl, core):
        if core == 0:
            return (yh, z, x, 1 - yl, core)
        return (1 - yh, z, x, 1 - yl, core)

    return lax.ppermute(value, axes, pairs_of(move))


def swap(value):
    return lax.ppermute(value, "core", [(0, 1), (1, 0)])


def unit_rows(values):
    inverse = lax.rsqrt(jnp.sum(values * values, axis=1, keepdims=True) + norm_eps)
    return values * inverse, inverse


def pack_kernel(scale_ref, bias_ref, core_ref, keep_ref, got_ref, *refs):
    unit_ref, low_ref, high_ref, raw_ref, factors_ref = refs
    first_core = core_ref[0] == 0
    scale = jnp.exp(jnp.full((1, 128), scale_ref[0], jnp.float32))
    factors_ref[0:1, :] = -log2_e * scale
    factors_ref[1:2, :] = jnp.full((1, 128), -log2_e * bias_ref[0], jnp.float32)
    factors_ref[2:3, :] = scale
    keep = keep_ref[...].astype(jnp.float32)
    got = got_ref[...].astype(jnp.float32)
    low = jnp.where(first_core, keep, got)
    high = jnp.where(first_core, got, keep)
    for half, values in enumerate((low, high)):
        place = pl.ds(half * rows, rows)
        unit = unit_rows(values)[0].astype(jnp.bfloat16)
        unit_ref[place, :] = unit
        (low_ref, high_ref)[half][...] = unit
        raw_ref[place, :] = values.astype(jnp.bfloat16)


def stacked(places, begin):
    return jnp.concatenate(
        [ref[pl.ds(first + begin, rows), :] for ref, first in places], axis=0
    )


def places_of(refs):
    return [
        (ref, first) for ref in refs for first in range(0, ref.shape[0], chip_rows)
    ]


def opposite_rows(core, half):
    return pl.multiple_of(jnp.where(core == 0, half, 1 - half) * rows, rows)


def spans(count):
    return [(begin, min(chunk, count - begin)) for begin in range(0, count, chunk)]


def weights_of(factors_ref, mine_rows, other_rows, matched=None):
    blocks = []
    for begin in range(0, mine_rows.shape[0], 2 * rows):
        dots = lax.dot_general(
            mine_rows[begin : begin + 2 * rows],
            other_rows,
            (((1,), (1,)), ((), ())),
            preferred_element_type=jnp.float32,
        )
        power = jnp.exp2(dots * factors_ref[0:1, 0:1] + factors_ref[1:2, 0:1])
        share = pl.reciprocal(1.0 + power, approx=True)
        if matched is not None and begin == 0:
            row = lax.broadcasted_iota(jnp.int32, dots.shape, 0)
            column = lax.broadcasted_iota(jnp.int32, dots.shape, 1)
            own = (row == column) & (row < rows) & matched
            share = jnp.where(own, -power * share, share)
        blocks.append(share.astype(jnp.bfloat16))
    return jnp.concatenate(blocks, axis=0)


def transposed_dot(weights, values):
    return lax.dot_general(
        weights, values, (((0,), (0,)), ((), ())), preferred_element_type=jnp.float32
    )


def store_chips(refs, first, begin, total):
    done = 0
    while done < total.shape[0]:
        chip, offset = divmod(begin + done, rows)
        size = min(rows - offset, total.shape[0] - done)
        ref, base = refs[chip]
        ref[pl.ds(base + first + offset, size), :] = total[done : done + size].astype(
            ref.dtype
        )
        done += size


def near_weights_kernel(pieces, core_ref, factors_ref, *refs):
    mine, other = places_of(refs[: pieces[0]]), places_of(refs[pieces[0] : sum(pieces)])
    near_ref, begun_ref = refs[sum(pieces) :]
    core = core_ref[0]
    count = near_ref.shape[2]
    for half in range(2):
        mine_rows = stacked(mine, half * rows)
        other_rows = stacked(other, opposite_rows(core, half))
        for begin, size in spans(count):
            near_ref[half, :, pl.ds(begin, size)] = weights_of(
                factors_ref,
                mine_rows,
                other_rows[begin : begin + size],
                core == 0 if begin == 0 else None,
            )
        begun_ref[half] = jnp.dot(
            near_ref[half, pl.ds(4 * rows, 4 * rows), :],
            other_rows[:count],
            preferred_element_type=jnp.float32,
        )


def far_weights_kernel(pieces, core_ref, factors_ref, *refs):
    mine, other = places_of(refs[: pieces[0]]), places_of(refs[pieces[0] : sum(pieces)])
    edge_ref, far_ref = refs[sum(pieces) :]
    edge = edge_ref.shape[2]
    first = 4 * rows - edge
    for half in range(2):
        mine_rows = stacked(mine, half * rows)
        other_rows = stacked(other, opposite_rows(core_ref[0], half))
        for begin, size in spans(edge + far_ref.shape[2]):
            start = first + begin
            weights = weights_of(
                factors_ref, mine_rows, other_rows[start : start + size]
            )
            if begin == 0:
                edge_ref[half] = weights[:, :edge]
                far_ref[half, :, pl.ds(0, size - edge)] = weights[:, edge:]
            else:
                far_ref[half, :, pl.ds(begin - edge, size)] = weights


def own_product(half, first, count, weights_refs, other_rows):
    weights = jnp.concatenate(
        [ref[half, pl.ds(first, count), :] for ref in weights_refs], axis=1
    )
    return jnp.dot(weights, other_rows, preferred_element_type=jnp.float32)


def own_kernel(pieces, core_ref, *refs):
    weights_refs, begun_ref, other = refs[:3], refs[3], places_of(refs[4 : 4 + pieces])
    near_ref, far_ref, joined_ref = refs[4 + pieces :]
    count = weights_refs[0].shape[2]
    edge = 4 * rows - weights_refs[1].shape[2]
    for half in range(2):
        other_rows = stacked(other, opposite_rows(core_ref[0], half))
        joined_ref[half, :, pl.ds(0, edge)] = weights_refs[0][half]
        joined_ref[half, :, pl.ds(edge, 4 * rows - edge)] = weights_refs[1][half]
        far_ref[half] = begun_ref[half] + own_product(
            half, 4 * rows, 4 * rows, weights_refs[1:], other_rows[count:]
        )
        near_ref[half] = own_product(half, rows, 3 * rows, weights_refs, other_rows)


def received(core, half, columns, other):
    its_half = jnp.where(core == 0, 1 - half, half)
    other_rows = stacked(other, pl.multiple_of(its_half * rows, rows))
    weights = jnp.concatenate(
        [ref[its_half, :, pl.ds(first, size)] for ref, first, size in columns], axis=1
    )
    return transposed_dot(weights, other_rows)


def far_kernel(pieces, core_ref, weights_ref, part_ref, *refs):
    other, sums = places_of(refs[:pieces]), places_of(refs[pieces:])
    for half in range(2):
        columns = [(weights_ref, 0, 4 * rows)]
        total = part_ref[half] + received(core_ref[0], half, columns, other)
        store_chips(sums, half * rows, 0, total)


def near_kernel(pieces, core_ref, weights_ref, part_ref, *refs):
    other, sums = places_of(refs[:pieces]), places_of(refs[pieces:])
    first = rows // 128 * 128
    columns = [(weights_ref, first, 4 * rows - first)]
    for half in range(2):
        total = received(core_ref[0], half, columns, other)
        total = total[rows - first :] + part_ref[half]
        store_chips(sums, half * rows, 0, total)


def self_kernel(pieces, core_ref, received_ref, *refs):
    weights_refs, other = refs[:3], places_of(refs[3 : 3 + pieces])
    sum_ref = refs[3 + pieces]
    core = core_ref[0]
    for half in range(2):
        other_rows = stacked(other, opposite_rows(core, half))
        total = own_product(half, 0, rows, weights_refs, other_rows)
        total = total + received(core, half, [(received_ref, 0, chunk)], other)[:rows]
        sum_ref[pl.ds(half * rows, rows), :] = total


def final_kernel(kept, core_ref, factors_ref, raw_ref, *refs):
    parts, grad_ref = refs[:-1], refs[-1]
    half = jnp.where(core_ref[0] == 0, 1 - kept, kept)
    place = pl.ds(pl.multiple_of(half * rows, rows), rows)
    unit, inverse = unit_rows(raw_ref[place, :].astype(jnp.float32))
    direction = parts[0][place, :].astype(jnp.float32)
    for part in parts[1:]:
        direction = direction + part[place, :].astype(jnp.float32)
    direction = direction * factors_ref[2:3, 0:1]
    along = jnp.sum(unit * direction, axis=1, keepdims=True)
    grad_ref[...] = (inverse * (direction - unit * along)).astype(jnp.bfloat16)


def call(kernel, out_shape, scalars, arrays, flops=0, after=(), kinds=None):
    kinds = kinds or [jnp.bfloat16] * len(out_shape)
    used = len(scalars) + len(arrays)

    def body(*refs):
        kernel(*refs[:used], *refs[used + len(after) :])

    return pl.pallas_call(
        body,
        in_specs=[pl.BlockSpec(memory_space=pltpu.SMEM)] * len(scalars)
        + [pl.BlockSpec(memory_space=pltpu.VMEM)] * len(arrays)
        + [pl.BlockSpec(memory_space=pl.ANY)] * len(after),
        out_specs=[pl.BlockSpec(memory_space=pltpu.VMEM)] * len(out_shape),
        out_shape=[
            jax.ShapeDtypeStruct(shape, kind_of)
            for shape, kind_of in zip(out_shape, kinds)
        ],
        compiler_params=pltpu.CompilerParams(vmem_limit_bytes=8 * 2**20),
        cost_estimate=pl.CostEstimate(
            flops=flops, bytes_accessed=2**20, transcendentals=0
        ),
    )(*scalars, *arrays, *after)


def add_kernel(groups, *refs):
    count = len(groups)
    inputs, sums = refs[: -count], refs[-count:]
    for sum_ref, group in zip(sums, groups):
        total = None
        for index, first in group:
            part = inputs[index][pl.ds(first, chip_rows), :].astype(jnp.float32)
            total = part if total is None else total + part
        sum_ref[...] = total.astype(sum_ref.dtype)


def add(groups, after=(), kind=jnp.bfloat16):
    arrays = []
    places = []
    for group in groups:
        place = []
        for part in group:
            array, first = part if isinstance(part, tuple) else (part, 0)
            if not any(array is known for known in arrays):
                arrays.append(array)
            index = [array is known for known in arrays].index(True)
            place.append((index, first))
        places.append(place)
    return call(
        functools.partial(add_kernel, places),
        [(chip_rows, arrays[0].shape[1])] * len(groups),
        (),
        arrays,
        after=after,
        kinds=[kind] * len(groups),
    )


def on_device(image_embeds, text_embeds, log_scale, logit_bias):
    width = image_embeds.shape[1]
    core = lax.axis_index("core")
    first_core = core == 0
    cores = core.astype(jnp.int32).reshape(1)
    give = jnp.where(first_core, text_embeds, image_embeds)
    keep = jnp.where(first_core, image_embeds, text_embeds)
    got = swap(give)
    unit, low, high, raw, factors = call(
        pack_kernel,
        [(chip_rows, width)] + [(rows, width)] * 2 + [(chip_rows, width), (8, 128)],
        (log_scale, logit_bias, cores),
        (keep, got),
        kinds=(jnp.bfloat16,) * 4 + (jnp.float32,),
    )
    across = pair(unit)
    left_low, right_high = ring(low, 1), ring(high, -1)
    late_high, late_low, _ = lax.optimization_barrier((high, low, left_low[:8]))
    left_high, right_low = ring(late_high, 1), ring(late_low, -1)
    distant_low, distant_high = ring(left_low, 1), ring(right_high, -1)
    far_left, far_right = ring(across, 1), ring(across, -1)
    low_far, high_far = pair(distant_low), pair(distant_high)
    left = jnp.concatenate([left_low, left_high], axis=0)
    right = jnp.concatenate([right_low, right_high], axis=0)
    distant = jnp.concatenate([distant_low, distant_high], axis=0)
    far_distant = jnp.concatenate([low_far, high_far], axis=0)
    near = [unit, left, right, across]
    far = [distant, far_left, far_right, far_distant]
    mine = near + far
    other = [
        swap(jnp.concatenate(near, axis=0)),
        swap(jnp.concatenate(far, axis=0)),
    ]
    near_rows, all_rows = 4 * rows, 8 * rows
    edge = near_rows % chunk
    block = (chip_rows, width)
    share = all_rows * all_rows * width // 5
    near_weights, far_begun = call(
        functools.partial(near_weights_kernel, (len(mine), 1)),
        [(2, all_rows, near_rows - edge), (2, near_rows, width)],
        (cores,),
        (factors, *mine, other[0]),
        12 * share,
        kinds=(jnp.bfloat16, jnp.float32),
    )
    edge_weights, far_weights = call(
        functools.partial(far_weights_kernel, (len(mine), len(other))),
        [(2, all_rows, edge), (2, all_rows, near_rows)],
        (cores,),
        (factors, *mine, *other),
        12 * share,
        (near_weights,),
    )
    far_received = swap(far_weights)
    weights = (near_weights, edge_weights, far_weights)
    near_part, far_part, near_joined = call(
        functools.partial(own_kernel, len(other)),
        [(2, 3 * rows, width), (2, 4 * rows, width), (2, all_rows, near_rows)],
        (cores,),
        (*weights, far_begun, *other),
        14 * share,
        kinds=(jnp.float32, jnp.float32, jnp.bfloat16),
    )
    near_received = swap(near_joined)
    far_sums = call(
        functools.partial(far_kernel, len(other)),
        [block] * 4,
        (cores,),
        (far_received, far_part, *other),
        10 * share,
    )
    arrived = [ring(far_sums[1], -1), ring(far_sums[2], 1), pair(far_sums[3])]
    near_sums = call(
        functools.partial(near_kernel, len(other)),
        [block] * 3,
        (cores,),
        (near_received, near_part, *other),
        8 * share,
    )
    (across_total,) = add([(near_sums[2], arrived[0], arrived[1])], (near_sums[0],))
    (distant_total,) = add([(far_sums[0], arrived[2])], (across_total,))
    (own_sum,) = call(
        functools.partial(self_kernel, len(other)),
        [block],
        (cores,),
        (near_received, *weights, *other),
        5 * share,
        (distant_total,),
        (jnp.float32,),
    )
    parts = [
        own_sum,
        ring(distant_total, 2),
        ring(near_sums[0], -1),
        ring(near_sums[1], 1),
        pair(across_total),
    ]
    (give,) = call(
        functools.partial(final_kernel, 0),
        [(rows, width)],
        (cores,),
        (factors, raw, *parts),
    )
    given = swap(give)
    (keep,) = call(
        functools.partial(final_kernel, 1),
        [(rows, width)],
        (cores,),
        (factors, raw, *parts),
        after=(give,),
    )
    image_grad = jnp.where(first_core, keep, given)
    text_grad = jnp.where(first_core, given, keep)
    return (image_grad, text_grad)


def solution(mesh):
    fine = Mesh(mesh.devices.reshape(extents), axes)
    split = P(axes, None)
    return jax.shard_map(
        on_device,
        mesh=fine,
        in_specs=(split, split, P(), P()),
        out_specs=(split, split),
        check_vma=False,
    )
```

```python
import functools

import jax
import jax.numpy as jnp
from jax import lax
from jax.experimental import pallas as pl
from jax.experimental.pallas import tpu as pltpu
from jax.sharding import Mesh, PartitionSpec as P

norm_eps = 1e-06
log2_e = 1.4426950408889634
axes = ("yh", "z", "x", "yl", "core")
extents = (2, 4, 4, 2, 2)
rows = 160
chip_rows = 2 * rows
chunk = 256


def pairs_of(move):
    pairs = []
    for yh in range(2):
        for z in range(4):
            for x in range(4):
                for yl in range(2):
                    for core in range(2):
                        place = (yh, z, x, yl, core)
                        pairs.append((linear(place), linear(move(*place))))
    return pairs


def linear(place):
    index = 0
    for value, extent in zip(place, extents):
        index = index * extent + value
    return index


def ring_move(steps):
    def move(yh, z, x, yl, core):
        if core == 0:
            return (yh, z, (x + steps) % 4, yl, core)
        return (yh, (z + steps) % 4, x, yl, core)

    return pairs_of(move)


def ring(value, steps):
    return lax.ppermute(value, axes, ring_move(steps))


def pair(value):
    def move(yh, z, x, yl, core):
        if core == 0:
            return (yh, z, x, 1 - yl, core)
        return (1 - yh, z, x, 1 - yl, core)

    return lax.ppermute(value, axes, pairs_of(move))


def swap(value):
    return lax.ppermute(value, "core", [(0, 1), (1, 0)])


def unit_rows(values):
    inverse = lax.rsqrt(jnp.sum(values * values, axis=1, keepdims=True) + norm_eps)
    return values * inverse, inverse


def pack_kernel(scale_ref, bias_ref, core_ref, keep_ref, got_ref, *refs):
    unit_ref, low_ref, high_ref, raw_ref, factors_ref = refs
    first_core = core_ref[0] == 0
    scale = jnp.exp(jnp.full((1, 128), scale_ref[0], jnp.float32))
    factors_ref[0:1, :] = -log2_e * scale
    factors_ref[1:2, :] = jnp.full((1, 128), -log2_e * bias_ref[0], jnp.float32)
    factors_ref[2:3, :] = scale
    keep = keep_ref[...].astype(jnp.float32)
    got = got_ref[...].astype(jnp.float32)
    low = jnp.where(first_core, keep, got)
    high = jnp.where(first_core, got, keep)
    for half, values in enumerate((low, high)):
        place = pl.ds(half * rows, rows)
        unit = unit_rows(values)[0].astype(jnp.bfloat16)
        unit_ref[place, :] = unit
        (low_ref, high_ref)[half][...] = unit
        raw_ref[place, :] = values.astype(jnp.bfloat16)


def stacked(places, begin):
    return jnp.concatenate(
        [ref[pl.ds(first + begin, rows), :] for ref, first in places], axis=0
    )


def places_of(refs):
    return [
        (ref, first) for ref in refs for first in range(0, ref.shape[0], chip_rows)
    ]


def opposite_rows(core, half):
    return pl.multiple_of(jnp.where(core == 0, half, 1 - half) * rows, rows)


def spans(count):
    return [(begin, min(chunk, count - begin)) for begin in range(0, count, chunk)]


def weights_of(factors_ref, mine_rows, other_rows, matched=None):
    blocks = []
    for begin in range(0, mine_rows.shape[0], 2 * rows):
        dots = lax.dot_general(
            mine_rows[begin : begin + 2 * rows],
            other_rows,
            (((1,), (1,)), ((), ())),
            preferred_element_type=jnp.float32,
        )
        power = jnp.exp2(dots * factors_ref[0:1, 0:1] + factors_ref[1:2, 0:1])
        share = pl.reciprocal(1.0 + power, approx=True)
        if matched is not None and begin == 0:
            row = lax.broadcasted_iota(jnp.int32, dots.shape, 0)
            column = lax.broadcasted_iota(jnp.int32, dots.shape, 1)
            own = (row == column) & (row < rows) & matched
            share = jnp.where(own, -power * share, share)
        blocks.append(share.astype(jnp.bfloat16))
    return jnp.concatenate(blocks, axis=0)


def transposed_dot(weights, values):
    return lax.dot_general(
        weights, values, (((0,), (0,)), ((), ())), preferred_element_type=jnp.float32
    )


def store_chips(refs, first, begin, total):
    done = 0
    while done < total.shape[0]:
        chip, offset = divmod(begin + done, rows)
        size = min(rows - offset, total.shape[0] - done)
        ref, base = refs[chip]
        ref[pl.ds(base + first + offset, size), :] = total[done : done + size].astype(
            ref.dtype
        )
        done += size


def near_weights_kernel(pieces, core_ref, factors_ref, *refs):
    mine, other = places_of(refs[: pieces[0]]), places_of(refs[pieces[0] : sum(pieces)])
    near_ref, begun_ref = refs[sum(pieces) :]
    core = core_ref[0]
    count = near_ref.shape[2]
    for half in range(2):
        mine_rows = stacked(mine, half * rows)
        other_rows = stacked(other, opposite_rows(core, half))
        for begin, size in spans(count):
            near_ref[half, :, pl.ds(begin, size)] = weights_of(
                factors_ref,
                mine_rows,
                other_rows[begin : begin + size],
                core == 0 if begin == 0 else None,
            )
        begun_ref[half] = jnp.dot(
            near_ref[half, pl.ds(4 * rows, 4 * rows), :],
            other_rows[:count],
            preferred_element_type=jnp.float32,
        )


def far_weights_kernel(pieces, core_ref, factors_ref, *refs):
    mine, other = places_of(refs[: pieces[0]]), places_of(refs[pieces[0] : sum(pieces)])
    edge_ref, far_ref = refs[sum(pieces) :]
    edge = edge_ref.shape[2]
    first = 8 * rows - edge - far_ref.shape[2]
    for half in range(2):
        mine_rows = stacked(mine, half * rows)
        other_rows = stacked(other, opposite_rows(core_ref[0], half))
        for begin, size in spans(edge + far_ref.shape[2]):
            start = first + begin
            weights = weights_of(
                factors_ref, mine_rows, other_rows[start : start + size]
            )
            if begin < edge:
                edge_ref[half, :, pl.ds(begin, size)] = weights
            else:
                far_ref[half, :, pl.ds(begin - edge, size)] = weights


def own_product(half, first, count, weights_refs, other_rows):
    weights = jnp.concatenate(
        [ref[half, pl.ds(first, count), :] for ref in weights_refs], axis=1
    )
    return jnp.dot(weights, other_rows, preferred_element_type=jnp.float32)


def own_kernel(pieces, core_ref, *refs):
    weights_refs, begun_ref, other = refs[:3], refs[3], places_of(refs[4 : 4 + pieces])
    near_ref, far_ref, low_ref, high_ref = refs[4 + pieces :]
    count = weights_refs[0].shape[2]
    low_ref[...] = weights_refs[0][...]
    high_ref[...] = weights_refs[1][...]
    for half in range(2):
        other_rows = stacked(other, opposite_rows(core_ref[0], half))
        far_ref[half] = begun_ref[half, pl.ds(rows, 3 * rows), :] + own_product(
            half, 5 * rows, 3 * rows, weights_refs[1:], other_rows[count:]
        )
        near_ref[half] = own_product(half, rows, 3 * rows, weights_refs, other_rows)


def received(core, half, columns, other):
    its_half = jnp.where(core == 0, 1 - half, half)
    other_rows = stacked(other, pl.multiple_of(its_half * rows, rows))
    weights = jnp.concatenate(
        [ref[its_half, :, pl.ds(first, size)] for ref, first, size in columns], axis=1
    )
    return transposed_dot(weights, other_rows)


def far_kernel(pieces, core_ref, weights_ref, part_ref, *refs):
    other, sums = places_of(refs[:pieces]), places_of(refs[pieces:-1])
    tail_ref = refs[-1]
    tail = tail_ref.shape[1]
    for half in range(2):
        columns = [(weights_ref, 0, weights_ref.shape[2])]
        total = received(core_ref[0], half, columns, other)
        tail_ref[half] = total[:tail]
        store_chips(sums, half * rows, 0, total[tail:] + part_ref[half])


def near_kernel(pieces, core_ref, low_ref, high_ref, part_ref, *refs):
    other, sums = places_of(refs[:pieces]), places_of(refs[pieces:])
    first = rows // 128 * 128
    count = low_ref.shape[2]
    columns = [(low_ref, first, count - first), (high_ref, 0, 4 * rows - count)]
    for half in range(2):
        total = received(core_ref[0], half, columns, other)[rows - first :]
        store_chips(sums, half * rows, 0, total + part_ref[half])


def distant_kernel(pieces, core_ref, high_ref, tail_ref, begun_ref, *refs):
    weights_refs, other = refs[:2], places_of(refs[2 : 2 + pieces])
    sums = places_of(refs[2 + pieces :])
    size = rows - tail_ref.shape[1]
    columns = [(high_ref, high_ref.shape[2] - size, size)]
    count = sum(ref.shape[2] for ref in weights_refs)
    for half in range(2):
        total = received(core_ref[0], half, columns, other)
        total = jnp.concatenate([total, tail_ref[half]], axis=0)
        other_rows = stacked(other, opposite_rows(core_ref[0], half))
        own = begun_ref[half, pl.ds(0, rows), :] + own_product(
            half, 4 * rows, rows, weights_refs, other_rows[8 * rows - count :]
        )
        store_chips(sums, half * rows, 0, total + own)


def self_kernel(pieces, core_ref, received_ref, *refs):
    weights_refs, other = refs[:3], places_of(refs[3 : 3 + pieces])
    sum_ref = refs[3 + pieces]
    core = core_ref[0]
    for half in range(2):
        other_rows = stacked(other, opposite_rows(core, half))
        total = own_product(half, 0, rows, weights_refs, other_rows)
        total = total + received(core, half, [(received_ref, 0, chunk)], other)[:rows]
        sum_ref[pl.ds(half * rows, rows), :] = total


def final_kernel(kept, core_ref, factors_ref, raw_ref, *refs):
    parts, grad_ref = refs[:-1], refs[-1]
    half = jnp.where(core_ref[0] == 0, 1 - kept, kept)
    place = pl.ds(pl.multiple_of(half * rows, rows), rows)
    unit, inverse = unit_rows(raw_ref[place, :].astype(jnp.float32))
    direction = parts[0][place, :].astype(jnp.float32)
    for part in parts[1:]:
        direction = direction + part[place, :].astype(jnp.float32)
    direction = direction * factors_ref[2:3, 0:1]
    along = jnp.sum(unit * direction, axis=1, keepdims=True)
    grad_ref[...] = (inverse * (direction - unit * along)).astype(jnp.bfloat16)


def call(kernel, out_shape, scalars, arrays, flops=0, after=(), kinds=None):
    kinds = kinds or [jnp.bfloat16] * len(out_shape)
    used = len(scalars) + len(arrays)

    def body(*refs):
        kernel(*refs[:used], *refs[used + len(after) :])

    return pl.pallas_call(
        body,
        in_specs=[pl.BlockSpec(memory_space=pltpu.SMEM)] * len(scalars)
        + [pl.BlockSpec(memory_space=pltpu.VMEM)] * len(arrays)
        + [pl.BlockSpec(memory_space=pl.ANY)] * len(after),
        out_specs=[pl.BlockSpec(memory_space=pltpu.VMEM)] * len(out_shape),
        out_shape=[
            jax.ShapeDtypeStruct(shape, kind_of)
            for shape, kind_of in zip(out_shape, kinds)
        ],
        compiler_params=pltpu.CompilerParams(vmem_limit_bytes=8 * 2**20),
        cost_estimate=pl.CostEstimate(
            flops=flops, bytes_accessed=2**20, transcendentals=0
        ),
    )(*scalars, *arrays, *after)


def add_kernel(groups, *refs):
    count = len(groups)
    inputs, sums = refs[: -count], refs[-count:]
    for sum_ref, group in zip(sums, groups):
        total = None
        for index, first in group:
            part = inputs[index][pl.ds(first, chip_rows), :].astype(jnp.float32)
            total = part if total is None else total + part
        sum_ref[...] = total.astype(sum_ref.dtype)


def add(groups, after=(), kind=jnp.bfloat16):
    arrays = []
    places = []
    for group in groups:
        place = []
        for part in group:
            array, first = part if isinstance(part, tuple) else (part, 0)
            if not any(array is known for known in arrays):
                arrays.append(array)
            index = [array is known for known in arrays].index(True)
            place.append((index, first))
        places.append(place)
    return call(
        functools.partial(add_kernel, places),
        [(chip_rows, arrays[0].shape[1])] * len(groups),
        (),
        arrays,
        after=after,
        kinds=[kind] * len(groups),
    )


def on_device(image_embeds, text_embeds, log_scale, logit_bias):
    width = image_embeds.shape[1]
    core = lax.axis_index("core")
    first_core = core == 0
    cores = core.astype(jnp.int32).reshape(1)
    give = jnp.where(first_core, text_embeds, image_embeds)
    keep = jnp.where(first_core, image_embeds, text_embeds)
    got = swap(give)
    unit, low, high, raw, factors = call(
        pack_kernel,
        [(chip_rows, width)] + [(rows, width)] * 2 + [(chip_rows, width), (8, 128)],
        (log_scale, logit_bias, cores),
        (keep, got),
        kinds=(jnp.bfloat16,) * 4 + (jnp.float32,),
    )
    across = pair(unit)
    left_low, right_high = ring(low, 1), ring(high, -1)
    late_high, late_low, _ = lax.optimization_barrier((high, low, left_low[:8]))
    left_high, right_low = ring(late_high, 1), ring(late_low, -1)
    distant_low, distant_high = ring(left_low, 1), ring(right_high, -1)
    far_left, far_right = ring(across, 1), ring(across, -1)
    low_far, high_far = pair(distant_low), pair(distant_high)
    left = jnp.concatenate([left_low, left_high], axis=0)
    right = jnp.concatenate([right_low, right_high], axis=0)
    distant = jnp.concatenate([distant_low, distant_high], axis=0)
    far_distant = jnp.concatenate([low_far, high_far], axis=0)
    near = [unit, left, right, across]
    far = [distant, far_left, far_right, far_distant]
    mine = near + far
    other = [
        swap(jnp.concatenate(near, axis=0)),
        swap(jnp.concatenate(far, axis=0)),
    ]
    near_rows, all_rows = 4 * rows, 8 * rows
    edge = near_rows % chunk
    block = (chip_rows, width)
    share = all_rows * all_rows * width // 5
    near_weights, far_begun = call(
        functools.partial(near_weights_kernel, (len(mine), 1)),
        [(2, all_rows, near_rows - edge), (2, near_rows, width)],
        (cores,),
        (factors, *mine, other[0]),
        12 * share,
        kinds=(jnp.bfloat16, jnp.float32),
    )
    edge_weights, far_weights = call(
        functools.partial(far_weights_kernel, (len(mine), len(other))),
        [(2, all_rows, chunk), (2, all_rows, 2 * chunk)],
        (cores,),
        (factors, *mine, *other),
        12 * share,
        (near_weights,),
    )
    far_received = swap(far_weights)
    weights = (near_weights, edge_weights, far_weights)
    near_part, far_part, near_copy, edge_copy = call(
        functools.partial(own_kernel, len(other)),
        [(2, 3 * rows, width)] * 2
        + [(2, all_rows, 2 * chunk), (2, all_rows, chunk)],
        (cores,),
        (*weights, far_begun, *other),
        14 * share,
        kinds=(jnp.float32,) * 2 + (jnp.bfloat16,) * 2,
    )
    near_received, edge_received = swap(near_copy), swap(edge_copy)
    *far_sums, tail = call(
        functools.partial(far_kernel, len(other)),
        [block] * 3 + [(2, 5 * rows - 3 * chunk, width)],
        (cores,),
        (far_received, far_part, *other),
        10 * share,
        kinds=[jnp.bfloat16] * 3 + [jnp.float32],
    )
    arrived = [ring(far_sums[0], -1), ring(far_sums[1], 1), pair(far_sums[2])]
    near_sums = call(
        functools.partial(near_kernel, len(other)),
        [block] * 3,
        (cores,),
        (near_received, edge_received, near_part, *other),
        8 * share,
    )
    (across_total,) = add([(near_sums[2], arrived[0], arrived[1])], (near_sums[0],))
    (distant_sum,) = call(
        functools.partial(distant_kernel, len(other)),
        [block],
        (cores,),
        (edge_received, tail, far_begun, edge_weights, far_weights, *other),
        4 * share,
        (across_total,),
    )
    (distant_total,) = add([(distant_sum, arrived[2])])
    (own_sum,) = call(
        functools.partial(self_kernel, len(other)),
        [block],
        (cores,),
        (near_received, *weights, *other),
        5 * share,
        (distant_total,),
        (jnp.float32,),
    )
    parts = [
        own_sum,
        ring(distant_total, 2),
        ring(near_sums[0], -1),
        ring(near_sums[1], 1),
        pair(across_total),
    ]
    (give,) = call(
        functools.partial(final_kernel, 0),
        [(rows, width)],
        (cores,),
        (factors, raw, *parts),
    )
    given = swap(give)
    (keep,) = call(
        functools.partial(final_kernel, 1),
        [(rows, width)],
        (cores,),
        (factors, raw, *parts),
        after=(give,),
    )
    image_grad = jnp.where(first_core, keep, given)
    text_grad = jnp.where(first_core, given, keep)
    return (image_grad, text_grad)


def solution(mesh):
    fine = Mesh(mesh.devices.reshape(extents), axes)
    split = P(axes, None)
    return jax.shard_map(
        on_device,
        mesh=fine,
        in_specs=(split, split, P(), P()),
        out_specs=(split, split),
        check_vma=False,
    )
```

```python
import functools

import jax
import jax.numpy as jnp
from jax import lax
from jax.experimental import pallas as pl
from jax.experimental.pallas import tpu as pltpu
from jax.sharding import Mesh, PartitionSpec as P

norm_eps = 1e-06
log2_e = 1.4426950408889634
axes = ("yh", "z", "x", "yl", "core")
extents = (2, 4, 4, 2, 2)
rows = 160
chip_rows = 2 * rows
chunk = 256


def pairs_of(move):
    pairs = []
    for yh in range(2):
        for z in range(4):
            for x in range(4):
                for yl in range(2):
                    for core in range(2):
                        place = (yh, z, x, yl, core)
                        pairs.append((linear(place), linear(move(*place))))
    return pairs


def linear(place):
    index = 0
    for value, extent in zip(place, extents):
        index = index * extent + value
    return index


def ring_move(steps):
    def move(yh, z, x, yl, core):
        if core == 0:
            return (yh, z, (x + steps) % 4, yl, core)
        return (yh, (z + steps) % 4, x, yl, core)

    return pairs_of(move)


def ring(value, steps):
    return lax.ppermute(value, axes, ring_move(steps))


def pair(value):
    def move(yh, z, x, yl, core):
        if core == 0:
            return (yh, z, x, 1 - yl, core)
        return (1 - yh, z, x, 1 - yl, core)

    return lax.ppermute(value, axes, pairs_of(move))


def swap(value):
    return lax.ppermute(value, "core", [(0, 1), (1, 0)])


def unit_rows(values):
    inverse = lax.rsqrt(jnp.sum(values * values, axis=1, keepdims=True) + norm_eps)
    return values * inverse, inverse


def pack_kernel(scale_ref, bias_ref, core_ref, keep_ref, got_ref, *refs):
    unit_ref, low_ref, high_ref, raw_ref, factors_ref = refs
    first_core = core_ref[0] == 0
    scale = jnp.exp(jnp.full((1, 128), scale_ref[0], jnp.float32))
    factors_ref[0:1, :] = -log2_e * scale
    factors_ref[1:2, :] = jnp.full((1, 128), -log2_e * bias_ref[0], jnp.float32)
    factors_ref[2:3, :] = scale
    keep = keep_ref[...].astype(jnp.float32)
    got = got_ref[...].astype(jnp.float32)
    low = jnp.where(first_core, keep, got)
    high = jnp.where(first_core, got, keep)
    for half, values in enumerate((low, high)):
        place = pl.ds(half * rows, rows)
        unit = unit_rows(values)[0].astype(jnp.bfloat16)
        unit_ref[place, :] = unit
        (low_ref, high_ref)[half][...] = unit
        raw_ref[place, :] = values.astype(jnp.bfloat16)


def stacked(places, begin):
    return jnp.concatenate(
        [ref[pl.ds(first + begin, rows), :] for ref, first in places], axis=0
    )


def places_of(refs):
    return [
        (ref, first) for ref in refs for first in range(0, ref.shape[0], chip_rows)
    ]


def opposite_rows(core, half):
    return pl.multiple_of(jnp.where(core == 0, half, 1 - half) * rows, rows)


def spans(count):
    return [(begin, min(chunk, count - begin)) for begin in range(0, count, chunk)]


def weights_of(factors_ref, mine_rows, other_rows, matched=None):
    blocks = []
    for begin in range(0, mine_rows.shape[0], 2 * rows):
        dots = lax.dot_general(
            mine_rows[begin : begin + 2 * rows],
            other_rows,
            (((1,), (1,)), ((), ())),
            preferred_element_type=jnp.float32,
        )
        power = jnp.exp2(dots * factors_ref[0:1, 0:1] + factors_ref[1:2, 0:1])
        share = pl.reciprocal(1.0 + power, approx=True)
        if matched is not None and begin == 0:
            row = lax.broadcasted_iota(jnp.int32, dots.shape, 0)
            column = lax.broadcasted_iota(jnp.int32, dots.shape, 1)
            own = (row == column) & (row < rows) & matched
            share = jnp.where(own, -power * share, share)
        blocks.append(share.astype(jnp.bfloat16))
    return jnp.concatenate(blocks, axis=0)


def transposed_dot(weights, values):
    return lax.dot_general(
        weights, values, (((0,), (0,)), ((), ())), preferred_element_type=jnp.float32
    )


def store_chips(refs, first, begin, total):
    done = 0
    while done < total.shape[0]:
        chip, offset = divmod(begin + done, rows)
        size = min(rows - offset, total.shape[0] - done)
        ref, base = refs[chip]
        ref[pl.ds(base + first + offset, size), :] = total[done : done + size].astype(
            ref.dtype
        )
        done += size


def near_weights_kernel(pieces, core_ref, factors_ref, *refs):
    mine, other = places_of(refs[: pieces[0]]), places_of(refs[pieces[0] : sum(pieces)])
    near_ref, begun_ref = refs[sum(pieces) :]
    core = core_ref[0]
    count = near_ref.shape[2]
    for half in range(2):
        mine_rows = stacked(mine, half * rows)
        other_rows = stacked(other, opposite_rows(core, half))
        for begin, size in spans(count):
            near_ref[half, :, pl.ds(begin, size)] = weights_of(
                factors_ref,
                mine_rows,
                other_rows[begin : begin + size],
                core == 0 if begin == 0 else None,
            )
        begun_ref[half] = jnp.dot(
            near_ref[half, pl.ds(4 * rows, 4 * rows), :],
            other_rows[:count],
            preferred_element_type=jnp.float32,
        )


def far_weights_kernel(pieces, core_ref, factors_ref, *refs):
    mine, other = places_of(refs[: pieces[0]]), places_of(refs[pieces[0] : sum(pieces)])
    (far_ref,) = refs[sum(pieces) :]
    first = 8 * rows - far_ref.shape[2]
    for half in range(2):
        mine_rows = stacked(mine, half * rows)
        other_rows = stacked(other, opposite_rows(core_ref[0], half))
        for begin, size in spans(far_ref.shape[2]):
            start = first + begin
            far_ref[half, :, pl.ds(begin, size)] = weights_of(
                factors_ref, mine_rows, other_rows[start : start + size]
            )


def own_product(half, first, count, weights_refs, other_rows):
    weights = jnp.concatenate(
        [ref[half, pl.ds(first, count), :] for ref in weights_refs], axis=1
    )
    return jnp.dot(weights, other_rows, preferred_element_type=jnp.float32)


def own_kernel(pieces, core_ref, factors_ref, *refs):
    mine, other = places_of(refs[: pieces[0]]), places_of(refs[pieces[0] : sum(pieces)])
    first_ref, last_ref, begun_ref, near_ref, far_ref, copy_ref, edge_ref = refs[
        sum(pieces) :
    ]
    count, edge = first_ref.shape[2], edge_ref.shape[2]
    copy_ref[...] = first_ref[...]
    for half in range(2):
        mine_rows = stacked(mine, half * rows)
        other_rows = stacked(other, opposite_rows(core_ref[0], half))
        edge_ref[half] = weights_of(
            factors_ref, mine_rows, other_rows[count : count + edge]
        )
        weights_refs = (first_ref, edge_ref, last_ref)
        far_ref[half] = begun_ref[half, pl.ds(rows, 3 * rows), :] + own_product(
            half, 5 * rows, 3 * rows, weights_refs[1:], other_rows[count:]
        )
        near_ref[half] = own_product(half, rows, 2 * rows, weights_refs, other_rows)


def received(core, half, columns, other):
    its_half = jnp.where(core == 0, 1 - half, half)
    other_rows = stacked(other, pl.multiple_of(its_half * rows, rows))
    weights = jnp.concatenate(
        [ref[its_half, :, pl.ds(first, size)] for ref, first, size in columns], axis=1
    )
    return transposed_dot(weights, other_rows)


def far_kernel(pieces, core_ref, weights_ref, part_ref, *refs):
    other, sums = places_of(refs[:pieces]), places_of(refs[pieces:-1])
    tail_ref = refs[-1]
    tail = tail_ref.shape[1]
    for half in range(2):
        columns = [(weights_ref, 0, weights_ref.shape[2])]
        total = received(core_ref[0], half, columns, other)
        tail_ref[half] = total[:tail]
        store_chips(sums, half * rows, 0, total[tail:] + part_ref[half])


def near_kernel(pieces, core_ref, low_ref, high_ref, part_ref, *refs):
    weights_refs, other = refs[:3], places_of(refs[3 : 3 + pieces])
    sums = places_of(refs[3 + pieces :])
    first = rows // 128 * 128
    count = low_ref.shape[2]
    columns = [(low_ref, first, count - first), (high_ref, 0, 4 * rows - count)]
    for half in range(2):
        total = received(core_ref[0], half, columns, other)[rows - first :]
        other_rows = stacked(other, opposite_rows(core_ref[0], half))
        own = own_product(half, 3 * rows, rows, weights_refs, other_rows)
        store_chips(sums[:2], half * rows, 0, total[: 2 * rows] + part_ref[half])
        store_chips(sums[2:], half * rows, 0, total[2 * rows :] + own)


def distant_kernel(pieces, core_ref, high_ref, tail_ref, begun_ref, *refs):
    weights_refs, other = refs[:2], places_of(refs[2 : 2 + pieces])
    sums = places_of(refs[2 + pieces :])
    size = rows - tail_ref.shape[1]
    columns = [(high_ref, high_ref.shape[2] - size, size)]
    count = sum(ref.shape[2] for ref in weights_refs)
    for half in range(2):
        total = received(core_ref[0], half, columns, other)
        total = jnp.concatenate([total, tail_ref[half]], axis=0)
        other_rows = stacked(other, opposite_rows(core_ref[0], half))
        own = begun_ref[half, pl.ds(0, rows), :] + own_product(
            half, 4 * rows, rows, weights_refs, other_rows[8 * rows - count :]
        )
        store_chips(sums, half * rows, 0, total + own)


def self_kernel(pieces, core_ref, received_ref, *refs):
    weights_refs, other = refs[:3], places_of(refs[3 : 3 + pieces])
    sum_ref = refs[3 + pieces]
    core = core_ref[0]
    for half in range(2):
        other_rows = stacked(other, opposite_rows(core, half))
        total = own_product(half, 0, rows, weights_refs, other_rows)
        total = total + received(core, half, [(received_ref, 0, chunk)], other)[:rows]
        sum_ref[pl.ds(half * rows, rows), :] = total


def final_kernel(kept, core_ref, factors_ref, raw_ref, *refs):
    parts, grad_ref = refs[:-1], refs[-1]
    half = jnp.where(core_ref[0] == 0, 1 - kept, kept)
    place = pl.ds(pl.multiple_of(half * rows, rows), rows)
    unit, inverse = unit_rows(raw_ref[place, :].astype(jnp.float32))
    direction = parts[0][place, :].astype(jnp.float32)
    for part in parts[1:]:
        direction = direction + part[place, :].astype(jnp.float32)
    direction = direction * factors_ref[2:3, 0:1]
    along = jnp.sum(unit * direction, axis=1, keepdims=True)
    grad_ref[...] = (inverse * (direction - unit * along)).astype(jnp.bfloat16)


def call(kernel, out_shape, scalars, arrays, flops=0, after=(), kinds=None):
    kinds = kinds or [jnp.bfloat16] * len(out_shape)
    used = len(scalars) + len(arrays)

    def body(*refs):
        kernel(*refs[:used], *refs[used + len(after) :])

    return pl.pallas_call(
        body,
        in_specs=[pl.BlockSpec(memory_space=pltpu.SMEM)] * len(scalars)
        + [pl.BlockSpec(memory_space=pltpu.VMEM)] * len(arrays)
        + [pl.BlockSpec(memory_space=pl.ANY)] * len(after),
        out_specs=[pl.BlockSpec(memory_space=pltpu.VMEM)] * len(out_shape),
        out_shape=[
            jax.ShapeDtypeStruct(shape, kind_of)
            for shape, kind_of in zip(out_shape, kinds)
        ],
        compiler_params=pltpu.CompilerParams(vmem_limit_bytes=8 * 2**20),
        cost_estimate=pl.CostEstimate(
            flops=flops, bytes_accessed=2**20, transcendentals=0
        ),
    )(*scalars, *arrays, *after)


def add_kernel(groups, *refs):
    count = len(groups)
    inputs, sums = refs[: -count], refs[-count:]
    for sum_ref, group in zip(sums, groups):
        total = None
        for index, first in group:
            part = inputs[index][pl.ds(first, chip_rows), :].astype(jnp.float32)
            total = part if total is None else total + part
        sum_ref[...] = total.astype(sum_ref.dtype)


def add(groups, after=(), kind=jnp.bfloat16):
    arrays = []
    places = []
    for group in groups:
        place = []
        for part in group:
            array, first = part if isinstance(part, tuple) else (part, 0)
            if not any(array is known for known in arrays):
                arrays.append(array)
            index = [array is known for known in arrays].index(True)
            place.append((index, first))
        places.append(place)
    return call(
        functools.partial(add_kernel, places),
        [(chip_rows, arrays[0].shape[1])] * len(groups),
        (),
        arrays,
        after=after,
        kinds=[kind] * len(groups),
    )


def on_device(image_embeds, text_embeds, log_scale, logit_bias):
    width = image_embeds.shape[1]
    core = lax.axis_index("core")
    first_core = core == 0
    cores = core.astype(jnp.int32).reshape(1)
    give = jnp.where(first_core, text_embeds, image_embeds)
    keep = jnp.where(first_core, image_embeds, text_embeds)
    got = swap(give)
    unit, low, high, raw, factors = call(
        pack_kernel,
        [(chip_rows, width)] + [(rows, width)] * 2 + [(chip_rows, width), (8, 128)],
        (log_scale, logit_bias, cores),
        (keep, got),
        kinds=(jnp.bfloat16,) * 4 + (jnp.float32,),
    )
    across = pair(unit)
    left_low, right_high = ring(low, 1), ring(high, -1)
    late_high, late_low, _ = lax.optimization_barrier((high, low, left_low[:8]))
    left_high, right_low = ring(late_high, 1), ring(late_low, -1)
    distant_low, distant_high = ring(left_low, 1), ring(right_high, -1)
    far_left, far_right = ring(across, 1), ring(across, -1)
    low_far, high_far = pair(distant_low), pair(distant_high)
    left = jnp.concatenate([left_low, left_high], axis=0)
    right = jnp.concatenate([right_low, right_high], axis=0)
    distant = jnp.concatenate([distant_low, distant_high], axis=0)
    far_distant = jnp.concatenate([low_far, high_far], axis=0)
    near = [unit, left, right, across]
    far = [distant, far_left, far_right, far_distant]
    mine = near + far
    other = [
        swap(jnp.concatenate(near, axis=0)),
        swap(jnp.concatenate(far, axis=0)),
    ]
    near_rows, all_rows = 4 * rows, 8 * rows
    edge = near_rows % chunk
    block = (chip_rows, width)
    share = all_rows * all_rows * width // 5
    near_weights, far_begun = call(
        functools.partial(near_weights_kernel, (len(mine), 1)),
        [(2, all_rows, near_rows - edge), (2, near_rows, width)],
        (cores,),
        (factors, *mine, other[0]),
        12 * share,
        kinds=(jnp.bfloat16, jnp.float32),
    )
    (far_weights,) = call(
        functools.partial(far_weights_kernel, (len(mine), len(other))),
        [(2, all_rows, 2 * chunk)],
        (cores,),
        (factors, *mine, *other),
        8 * share,
        (near_weights,),
    )
    far_received = swap(far_weights)
    near_part, far_part, near_copy, edge_weights = call(
        functools.partial(own_kernel, (len(mine), len(other))),
        [(2, 2 * rows, width), (2, 3 * rows, width)]
        + [(2, all_rows, 2 * chunk), (2, all_rows, chunk)],
        (cores,),
        (factors, *mine, *other, near_weights, far_weights, far_begun),
        16 * share,
        kinds=(jnp.float32,) * 2 + (jnp.bfloat16,) * 2,
    )
    weights = (near_weights, edge_weights, far_weights)
    near_received, edge_received = swap(near_copy), swap(edge_weights)
    *far_sums, tail = call(
        functools.partial(far_kernel, len(other)),
        [block] * 3 + [(2, 5 * rows - 3 * chunk, width)],
        (cores,),
        (far_received, far_part, *other),
        10 * share,
        kinds=[jnp.bfloat16] * 3 + [jnp.float32],
    )
    arrived = [ring(far_sums[0], -1), ring(far_sums[1], 1), pair(far_sums[2])]
    near_sums = call(
        functools.partial(near_kernel, len(other)),
        [block] * 3,
        (cores,),
        (near_received, edge_received, near_part, *weights, *other),
        8 * share,
    )
    (across_total,) = add([(near_sums[2], arrived[0], arrived[1])], (near_sums[0],))
    (distant_sum,) = call(
        functools.partial(distant_kernel, len(other)),
        [block],
        (cores,),
        (edge_received, tail, far_begun, edge_weights, far_weights, *other),
        4 * share,
        (across_total,),
    )
    (distant_total,) = add([(distant_sum, arrived[2])])
    (own_sum,) = call(
        functools.partial(self_kernel, len(other)),
        [block],
        (cores,),
        (near_received, *weights, *other),
        5 * share,
        (distant_total,),
        (jnp.float32,),
    )
    parts = [
        own_sum,
        ring(distant_total, 2),
        ring(near_sums[0], -1),
        ring(near_sums[1], 1),
        pair(across_total),
    ]
    (give,) = call(
        functools.partial(final_kernel, 0),
        [(rows, width)],
        (cores,),
        (factors, raw, *parts),
    )
    given = swap(give)
    (keep,) = call(
        functools.partial(final_kernel, 1),
        [(rows, width)],
        (cores,),
        (factors, raw, *parts),
        after=(give,),
    )
    image_grad = jnp.where(first_core, keep, given)
    text_grad = jnp.where(first_core, given, keep)
    return (image_grad, text_grad)


def solution(mesh):
    fine = Mesh(mesh.devices.reshape(extents), axes)
    split = P(axes, None)
    return jax.shard_map(
        on_device,
        mesh=fine,
        in_specs=(split, split, P(), P()),
        out_specs=(split, split),
        check_vma=False,
    )
```

```python
import functools

import jax
import jax.numpy as jnp
from jax import lax
from jax.experimental import pallas as pl
from jax.experimental.pallas import tpu as pltpu
from jax.sharding import Mesh, PartitionSpec as P

norm_eps = 1e-06
log2_e = 1.4426950408889634
axes = ("yh", "z", "x", "yl", "core")
extents = (2, 4, 4, 2, 2)
rows = 160
chip_rows = 2 * rows
chunk = 256


def pairs_of(move):
    pairs = []
    for yh in range(2):
        for z in range(4):
            for x in range(4):
                for yl in range(2):
                    for core in range(2):
                        place = (yh, z, x, yl, core)
                        pairs.append((linear(place), linear(move(*place))))
    return pairs


def linear(place):
    index = 0
    for value, extent in zip(place, extents):
        index = index * extent + value
    return index


def ring_move(steps):
    def move(yh, z, x, yl, core):
        if core == 0:
            return (yh, z, (x + steps) % 4, yl, core)
        return (yh, (z + steps) % 4, x, yl, core)

    return pairs_of(move)


def ring(value, steps):
    return lax.ppermute(value, axes, ring_move(steps))


def pair(value):
    def move(yh, z, x, yl, core):
        if core == 0:
            return (yh, z, x, 1 - yl, core)
        return (1 - yh, z, x, 1 - yl, core)

    return lax.ppermute(value, axes, pairs_of(move))


def swap(value):
    return lax.ppermute(value, "core", [(0, 1), (1, 0)])


def unit_rows(values):
    inverse = lax.rsqrt(jnp.sum(values * values, axis=1, keepdims=True) + norm_eps)
    return values * inverse, inverse


def pack_kernel(scale_ref, bias_ref, core_ref, keep_ref, got_ref, *refs):
    unit_ref, low_ref, high_ref, raw_ref, factors_ref = refs
    first_core = core_ref[0] == 0
    scale = jnp.exp(jnp.full((1, 128), scale_ref[0], jnp.float32))
    factors_ref[0:1, :] = -log2_e * scale
    factors_ref[1:2, :] = jnp.full((1, 128), -log2_e * bias_ref[0], jnp.float32)
    factors_ref[2:3, :] = scale
    keep = keep_ref[...].astype(jnp.float32)
    got = got_ref[...].astype(jnp.float32)
    low = jnp.where(first_core, keep, got)
    high = jnp.where(first_core, got, keep)
    for half, values in enumerate((low, high)):
        place = pl.ds(half * rows, rows)
        unit = unit_rows(values)[0].astype(jnp.bfloat16)
        unit_ref[place, :] = unit
        (low_ref, high_ref)[half][...] = unit
        raw_ref[place, :] = values.astype(jnp.bfloat16)


def stacked(places, begin):
    return jnp.concatenate(
        [ref[pl.ds(first + begin, rows), :] for ref, first in places], axis=0
    )


def places_of(refs):
    return [
        (ref, first) for ref in refs for first in range(0, ref.shape[0], chip_rows)
    ]


def opposite_rows(core, half):
    return pl.multiple_of(jnp.where(core == 0, half, 1 - half) * rows, rows)


def spans(count):
    return [(begin, min(chunk, count - begin)) for begin in range(0, count, chunk)]


def weights_of(factors_ref, mine_rows, other_rows, matched=None):
    blocks = []
    for begin in range(0, mine_rows.shape[0], 2 * rows):
        dots = lax.dot_general(
            mine_rows[begin : begin + 2 * rows],
            other_rows,
            (((1,), (1,)), ((), ())),
            preferred_element_type=jnp.float32,
        )
        power = jnp.exp2(dots * factors_ref[0:1, 0:1] + factors_ref[1:2, 0:1])
        share = pl.reciprocal(1.0 + power, approx=True)
        if matched is not None and begin == 0:
            row = lax.broadcasted_iota(jnp.int32, dots.shape, 0)
            column = lax.broadcasted_iota(jnp.int32, dots.shape, 1)
            own = (row == column) & (row < rows) & matched
            share = jnp.where(own, -power * share, share)
        blocks.append(share.astype(jnp.bfloat16))
    return jnp.concatenate(blocks, axis=0)


def transposed_dot(weights, values):
    return lax.dot_general(
        weights, values, (((0,), (0,)), ((), ())), preferred_element_type=jnp.float32
    )


def store_chips(refs, first, begin, total):
    done = 0
    while done < total.shape[0]:
        chip, offset = divmod(begin + done, rows)
        size = min(rows - offset, total.shape[0] - done)
        ref, base = refs[chip]
        ref[pl.ds(base + first + offset, size), :] = total[done : done + size].astype(
            ref.dtype
        )
        done += size


def near_weights_kernel(pieces, core_ref, factors_ref, *refs):
    mine, other = places_of(refs[: pieces[0]]), places_of(refs[pieces[0] : sum(pieces)])
    near_ref, begun_ref = refs[sum(pieces) :]
    core = core_ref[0]
    count = near_ref.shape[2]
    for half in range(2):
        mine_rows = stacked(mine, half * rows)
        other_rows = stacked(other, opposite_rows(core, half))
        for begin, size in spans(count):
            near_ref[half, :, pl.ds(begin, size)] = weights_of(
                factors_ref,
                mine_rows,
                other_rows[begin : begin + size],
                core == 0 if begin == 0 else None,
            )
        begun_ref[half] = jnp.dot(
            near_ref[half, pl.ds(4 * rows, 4 * rows), :],
            other_rows[:count],
            preferred_element_type=jnp.float32,
        )


def far_weights_kernel(pieces, core_ref, factors_ref, *refs):
    mine, other = places_of(refs[: pieces[0]]), places_of(refs[pieces[0] : sum(pieces)])
    (far_ref,) = refs[sum(pieces) :]
    first = 8 * rows - far_ref.shape[2]
    for half in range(2):
        mine_rows = stacked(mine, half * rows)
        other_rows = stacked(other, opposite_rows(core_ref[0], half))
        for begin, size in spans(far_ref.shape[2]):
            start = first + begin
            far_ref[half, :, pl.ds(begin, size)] = weights_of(
                factors_ref, mine_rows, other_rows[start : start + size]
            )


def own_product(half, first, count, weights_refs, other_rows):
    weights = jnp.concatenate(
        [ref[half, pl.ds(first, count), :] for ref in weights_refs], axis=1
    )
    return jnp.dot(weights, other_rows, preferred_element_type=jnp.float32)


def own_kernel(pieces, core_ref, factors_ref, *refs):
    mine, other = places_of(refs[: pieces[0]]), places_of(refs[pieces[0] : sum(pieces)])
    first_ref, last_ref, begun_ref, near_ref, far_ref, copy_ref, edge_ref = refs[
        sum(pieces) :
    ]
    count, edge = first_ref.shape[2], edge_ref.shape[2]
    copy_ref[...] = first_ref[...]
    for half in range(2):
        mine_rows = stacked(mine, half * rows)
        other_rows = stacked(other, opposite_rows(core_ref[0], half))
        edge_ref[half] = weights_of(
            factors_ref, mine_rows, other_rows[count : count + edge]
        )
        weights_refs = (first_ref, edge_ref, last_ref)
        far_ref[half] = begun_ref[half, pl.ds(rows, 3 * rows), :] + own_product(
            half, 5 * rows, 3 * rows, weights_refs[1:], other_rows[count:]
        )
        near_ref[half] = own_product(half, rows, 2 * rows, weights_refs, other_rows)


def received(core, half, columns, other):
    its_half = jnp.where(core == 0, 1 - half, half)
    other_rows = stacked(other, pl.multiple_of(its_half * rows, rows))
    weights = jnp.concatenate(
        [ref[its_half, :, pl.ds(first, size)] for ref, first, size in columns], axis=1
    )
    return transposed_dot(weights, other_rows)


def far_kernel(pieces, core_ref, weights_ref, part_ref, *refs):
    other, sums = places_of(refs[:pieces]), places_of(refs[pieces:-1])
    tail_ref = refs[-1]
    tail = tail_ref.shape[1]
    for half in range(2):
        columns = [(weights_ref, 0, weights_ref.shape[2])]
        total = received(core_ref[0], half, columns, other)
        tail_ref[half] = total[:tail]
        store_chips(sums, half * rows, 0, total[tail:] + part_ref[half])


def near_kernel(pieces, core_ref, low_ref, high_ref, part_ref, *refs):
    other, sums = places_of(refs[:pieces]), places_of(refs[pieces:])
    first = rows // 128 * 128
    count = low_ref.shape[2]
    columns = [(low_ref, first, count - first), (high_ref, 0, 4 * rows - count)]
    for half in range(2):
        total = received(core_ref[0], half, columns, other)[rows - first :]
        store_chips(sums[:2], half * rows, 0, total[: 2 * rows] + part_ref[half])
        store_chips(sums[2:], half * rows, 0, total[2 * rows :])


def across_kernel(pieces, core_ref, *refs):
    weights_refs, parts = refs[:3], refs[3:6]
    other, sums = places_of(refs[6 : 6 + pieces]), places_of(refs[6 + pieces :])
    for half in range(2):
        other_rows = stacked(other, opposite_rows(core_ref[0], half))
        total = own_product(half, 3 * rows, rows, weights_refs, other_rows)
        for part in parts:
            total = total + part[pl.ds(half * rows, rows), :].astype(jnp.float32)
        store_chips(sums, half * rows, 0, total)


def distant_kernel(pieces, core_ref, high_ref, tail_ref, begun_ref, *refs):
    weights_refs, other = refs[:2], places_of(refs[2 : 2 + pieces])
    sums = places_of(refs[2 + pieces :])
    size = rows - tail_ref.shape[1]
    columns = [(high_ref, high_ref.shape[2] - size, size)]
    count = sum(ref.shape[2] for ref in weights_refs)
    for half in range(2):
        total = received(core_ref[0], half, columns, other)
        total = jnp.concatenate([total, tail_ref[half]], axis=0)
        other_rows = stacked(other, opposite_rows(core_ref[0], half))
        own = begun_ref[half, pl.ds(0, rows), :] + own_product(
            half, 4 * rows, rows, weights_refs, other_rows[8 * rows - count :]
        )
        store_chips(sums, half * rows, 0, total + own)


def self_kernel(pieces, core_ref, received_ref, *refs):
    weights_refs, other = refs[:3], places_of(refs[3 : 3 + pieces])
    sum_ref = refs[3 + pieces]
    core = core_ref[0]
    for half in range(2):
        other_rows = stacked(other, opposite_rows(core, half))
        total = own_product(half, 0, rows, weights_refs, other_rows)
        total = total + received(core, half, [(received_ref, 0, chunk)], other)[:rows]
        sum_ref[pl.ds(half * rows, rows), :] = total


def final_kernel(kept, core_ref, factors_ref, raw_ref, *refs):
    parts, grad_ref = refs[:-1], refs[-1]
    half = jnp.where(core_ref[0] == 0, 1 - kept, kept)
    place = pl.ds(pl.multiple_of(half * rows, rows), rows)
    unit, inverse = unit_rows(raw_ref[place, :].astype(jnp.float32))
    direction = parts[0][place, :].astype(jnp.float32)
    for part in parts[1:]:
        direction = direction + part[place, :].astype(jnp.float32)
    direction = direction * factors_ref[2:3, 0:1]
    along = jnp.sum(unit * direction, axis=1, keepdims=True)
    grad_ref[...] = (inverse * (direction - unit * along)).astype(jnp.bfloat16)


def call(kernel, out_shape, scalars, arrays, flops=0, after=(), kinds=None):
    kinds = kinds or [jnp.bfloat16] * len(out_shape)
    used = len(scalars) + len(arrays)

    def body(*refs):
        kernel(*refs[:used], *refs[used + len(after) :])

    return pl.pallas_call(
        body,
        in_specs=[pl.BlockSpec(memory_space=pltpu.SMEM)] * len(scalars)
        + [pl.BlockSpec(memory_space=pltpu.VMEM)] * len(arrays)
        + [pl.BlockSpec(memory_space=pl.ANY)] * len(after),
        out_specs=[pl.BlockSpec(memory_space=pltpu.VMEM)] * len(out_shape),
        out_shape=[
            jax.ShapeDtypeStruct(shape, kind_of)
            for shape, kind_of in zip(out_shape, kinds)
        ],
        compiler_params=pltpu.CompilerParams(vmem_limit_bytes=8 * 2**20),
        cost_estimate=pl.CostEstimate(
            flops=flops, bytes_accessed=2**20, transcendentals=0
        ),
    )(*scalars, *arrays, *after)


def add_kernel(groups, *refs):
    count = len(groups)
    inputs, sums = refs[: -count], refs[-count:]
    for sum_ref, group in zip(sums, groups):
        total = None
        for index, first in group:
            part = inputs[index][pl.ds(first, chip_rows), :].astype(jnp.float32)
            total = part if total is None else total + part
        sum_ref[...] = total.astype(sum_ref.dtype)


def add(groups, after=(), kind=jnp.bfloat16):
    arrays = []
    places = []
    for group in groups:
        place = []
        for part in group:
            array, first = part if isinstance(part, tuple) else (part, 0)
            if not any(array is known for known in arrays):
                arrays.append(array)
            index = [array is known for known in arrays].index(True)
            place.append((index, first))
        places.append(place)
    return call(
        functools.partial(add_kernel, places),
        [(chip_rows, arrays[0].shape[1])] * len(groups),
        (),
        arrays,
        after=after,
        kinds=[kind] * len(groups),
    )


def on_device(image_embeds, text_embeds, log_scale, logit_bias):
    width = image_embeds.shape[1]
    core = lax.axis_index("core")
    first_core = core == 0
    cores = core.astype(jnp.int32).reshape(1)
    give = jnp.where(first_core, text_embeds, image_embeds)
    keep = jnp.where(first_core, image_embeds, text_embeds)
    got = swap(give)
    unit, low, high, raw, factors = call(
        pack_kernel,
        [(chip_rows, width)] + [(rows, width)] * 2 + [(chip_rows, width), (8, 128)],
        (log_scale, logit_bias, cores),
        (keep, got),
        kinds=(jnp.bfloat16,) * 4 + (jnp.float32,),
    )
    across = pair(unit)
    left_low, right_high = ring(low, 1), ring(high, -1)
    late_high, late_low, _ = lax.optimization_barrier((high, low, left_low[:8]))
    left_high, right_low = ring(late_high, 1), ring(late_low, -1)
    distant_low, distant_high = ring(left_low, 1), ring(right_high, -1)
    far_left, far_right = ring(across, 1), ring(across, -1)
    low_far, high_far = pair(distant_low), pair(distant_high)
    left = jnp.concatenate([left_low, left_high], axis=0)
    right = jnp.concatenate([right_low, right_high], axis=0)
    distant = jnp.concatenate([distant_low, distant_high], axis=0)
    far_distant = jnp.concatenate([low_far, high_far], axis=0)
    near = [unit, left, right, across]
    far = [distant, far_left, far_right, far_distant]
    mine = near + far
    other = [
        swap(jnp.concatenate(near, axis=0)),
        swap(jnp.concatenate(far, axis=0)),
    ]
    near_rows, all_rows = 4 * rows, 8 * rows
    edge = near_rows % chunk
    block = (chip_rows, width)
    share = all_rows * all_rows * width // 5
    near_weights, far_begun = call(
        functools.partial(near_weights_kernel, (len(mine), 1)),
        [(2, all_rows, near_rows - edge), (2, near_rows, width)],
        (cores,),
        (factors, *mine, other[0]),
        12 * share,
        kinds=(jnp.bfloat16, jnp.float32),
    )
    (far_weights,) = call(
        functools.partial(far_weights_kernel, (len(mine), len(other))),
        [(2, all_rows, 2 * chunk)],
        (cores,),
        (factors, *mine, *other),
        8 * share,
        (near_weights,),
    )
    far_received = swap(far_weights)
    near_part, far_part, near_copy, edge_weights = call(
        functools.partial(own_kernel, (len(mine), len(other))),
        [(2, 2 * rows, width), (2, 3 * rows, width)]
        + [(2, all_rows, 2 * chunk), (2, all_rows, chunk)],
        (cores,),
        (factors, *mine, *other, near_weights, far_weights, far_begun),
        16 * share,
        kinds=(jnp.float32,) * 2 + (jnp.bfloat16,) * 2,
    )
    weights = (near_weights, edge_weights, far_weights)
    near_received, edge_received = swap(near_copy), swap(edge_weights)
    *far_sums, tail = call(
        functools.partial(far_kernel, len(other)),
        [block] * 3 + [(2, 5 * rows - 3 * chunk, width)],
        (cores,),
        (far_received, far_part, *other),
        10 * share,
        kinds=[jnp.bfloat16] * 3 + [jnp.float32],
    )
    arrived = [ring(far_sums[0], -1), ring(far_sums[1], 1), pair(far_sums[2])]
    near_sums = call(
        functools.partial(near_kernel, len(other)),
        [block] * 3,
        (cores,),
        (near_received, edge_received, near_part, *other),
        8 * share,
    )
    (across_total,) = call(
        functools.partial(across_kernel, len(other)),
        [block],
        (cores,),
        (*weights, near_sums[2], arrived[0], arrived[1], *other),
        2 * share,
        (near_sums[0],),
    )
    (distant_sum,) = call(
        functools.partial(distant_kernel, len(other)),
        [block],
        (cores,),
        (edge_received, tail, far_begun, edge_weights, far_weights, *other),
        4 * share,
        (across_total,),
    )
    (distant_total,) = add([(distant_sum, arrived[2])])
    (own_sum,) = call(
        functools.partial(self_kernel, len(other)),
        [block],
        (cores,),
        (near_received, *weights, *other),
        5 * share,
        (distant_total,),
        (jnp.float32,),
    )
    parts = [
        own_sum,
        ring(distant_total, 2),
        ring(near_sums[0], -1),
        ring(near_sums[1], 1),
        pair(across_total),
    ]
    (give,) = call(
        functools.partial(final_kernel, 0),
        [(rows, width)],
        (cores,),
        (factors, raw, *parts),
    )
    given = swap(give)
    (keep,) = call(
        functools.partial(final_kernel, 1),
        [(rows, width)],
        (cores,),
        (factors, raw, *parts),
        after=(give,),
    )
    image_grad = jnp.where(first_core, keep, given)
    text_grad = jnp.where(first_core, given, keep)
    return (image_grad, text_grad)


def solution(mesh):
    fine = Mesh(mesh.devices.reshape(extents), axes)
    split = P(axes, None)
    return jax.shard_map(
        on_device,
        mesh=fine,
        in_specs=(split, split, P(), P()),
        out_specs=(split, split),
        check_vma=False,
    )
```
